512 devices in a mesh: tm: 16 (over y, core), space: 32 (over x, z).
Axes of the slice: x: 4, y: 8, z: 8, core: 2. Of those that a mesh axis runs over, the one named last changes fastest.
Arguments:
- basis: float32 [4, 16, 64, 64, 8, 128], P(None, None, 'tm', 'space'), may hold values from -60 to 60
- step_numerator: int32 [64], P('tm'), may hold values from 3 to 5
- step_denominator: int32 [64], P('tm'), may hold values from 3 to 4
Outputs:
- hessenberg: float32 [4, 16, 16], replicated
- triangle: float32 [16, 16], replicated
- next_block: float32 [16, 64, 64, 8, 128], P(None, 'tm', 'space')
The draws below stay inside these ranges and needn't reach their ends.
All inputs are finite; a program needn't handle non-finite values.
Results may differ from the reference program's by a relative error of at most 0.0003.
Values sent between devices are 32-bit elements; how exact they have to be, the bound alone decides.
No kernel may reach another device: no remote copies, remote signals or barrier semaphores. Data moves between devices by JAX's collectives and lax.ppermute only.
A program may use at most 64 MiB of HBM per device.

```python
import math
import jax
import jax.numpy as jnp
from jax import lax

RHS = 16
NB = 4
NY = 8
NX = 128
NT = 64
NZ = 64


def draw_basis(key, part):
    key = jax.random.fold_in(key, 5)
    sub_keys = jax.random.split(key, 8)
    full_shape = (RHS, NT, NZ, NY, NX)
    source = jax.random.truncated_normal(sub_keys[0], -4.0, 4.0, full_shape, jnp.float32)
    steepness = 2.0
    cell_scale = jnp.exp(jax.random.uniform(sub_keys[1], (1, NT, NZ, NY, NX), jnp.float32, math.log(0.2), math.log(2.0)))
    column_scale = jnp.exp(jax.random.uniform(sub_keys[2], (RHS, 1, 1, 1, 1), jnp.float32, math.log(0.25), math.log(2.5)))
    time_ramp = (1.0 + steepness * jnp.arange(NT, dtype=jnp.float32) / (NT - 1)) / (1.0 + 0.5 * steepness)
    plane_ramp = (1.0 + steepness * jnp.arange(NZ, dtype=jnp.float32) / (NZ - 1)) / (1.0 + 0.5 * steepness)
    entry_scale = cell_scale * column_scale * time_ramp[None, :, None, None, None] * plane_ramp[None, None, :, None, None]
    current = source * entry_scale

    def fresh_noise(which_key):
        return jax.random.truncated_normal(sub_keys[which_key], -4.0, 4.0, full_shape, jnp.float32) * cell_scale * column_scale
    block_zero = 0.8 * jnp.roll(current, 1, axis=2) + 0.6 * fresh_noise(3)
    block_one = 0.8 * jnp.roll(current, 2, axis=1) + 0.6 * fresh_noise(4)
    block_two = 0.8 * jnp.roll(current, 1, axis=1) + 0.6 * fresh_noise(5)
    return jnp.stack([block_zero, block_one, block_two, current])


def set_ends(drawn, stream_key, low, top_value):
    index_at = [jax.random.randint(jax.random.fold_in(stream_key, axis), (), 0, length) for axis, length in enumerate(drawn.shape)]
    main_axis = drawn.shape.index(max(drawn.shape))
    neighbour = index_at[:main_axis] + [(index_at[main_axis] + 1) % drawn.shape[main_axis]] + index_at[main_axis + 1:]
    return drawn.at[tuple(index_at)].set(low).at[tuple(neighbour)].set(top_value)


def setup_inputs(seed: int = 0) -> dict:
    keys = jax.random.split(jax.random.key(seed), 4)
    basis = draw_basis(jax.random.fold_in(keys[3], 71), 0)
    step_numerator = set_ends(jax.random.randint(keys[1], (NT,), 3, 6), jax.random.fold_in(keys[1], 1), 3, 5).astype(jnp.int32)
    step_denominator = set_ends(jax.random.randint(keys[2], (NT,), 3, 5), jax.random.fold_in(keys[2], 1), 3, 4).astype(jnp.int32)
    return dict(basis=basis, step_numerator=step_numerator, step_denominator=step_denominator)


def step_weights(size_now, size_prev, first_row):
    step_ratio = size_now / size_prev
    ones_like = jnp.ones_like(step_ratio)
    weight_now = jnp.where(first_row, ones_like, (1.0 + 2.0 * step_ratio) / (1.0 + step_ratio))
    weight_one = jnp.where(first_row, ones_like, 1.0 + step_ratio)
    weight_two = jnp.where(first_row, jnp.zeros_like(step_ratio), step_ratio * step_ratio / (1.0 + step_ratio))
    return (weight_now, weight_one, weight_two, 0.5 * size_now)

def apply_column(column_field, weight_now, weight_one, weight_two, kappa_step):
    zero_plane = jnp.zeros_like(column_field[:1])
    back_one = jnp.concatenate([zero_plane, column_field[:-1]], axis=0)
    back_two = jnp.concatenate([zero_plane, zero_plane, column_field[:-2]], axis=0)
    padded = jnp.pad(column_field, ((0, 0), (1, 1), (1, 1), (1, 1)))
    beside = padded[:, 2:, 1:-1, 1:-1] + padded[:, :-2, 1:-1, 1:-1]
    beside = beside + padded[:, 1:-1, 2:, 1:-1] + padded[:, 1:-1, :-2, 1:-1]
    beside = beside + padded[:, 1:-1, 1:-1, 2:] + padded[:, 1:-1, 1:-1, :-2]

    def spread(values):
        return values[:, None, None, None]
    return spread(weight_now) * column_field - spread(weight_one) * back_one + spread(weight_two) * back_two + spread(kappa_step) * (6.0 * column_field - beside)

def reference(basis, step_numerator, step_denominator):
    highest = lax.Precision.HIGHEST
    size_now = step_numerator.astype(jnp.float32) / step_denominator.astype(jnp.float32)
    size_prev = jnp.concatenate([size_now[:1], size_now[:-1]])
    first_row = jnp.arange(NT, dtype=jnp.int32) == 0
    weight_now, weight_one, weight_two, kappa_step = step_weights(size_now, size_prev, first_row)
    image = lax.map(lambda column_field: apply_column(column_field, weight_now, weight_one, weight_two, kappa_step), basis[NB - 1])
    cell_count = NT * NZ * NY * NX
    flat_basis = basis.reshape(NB * RHS, cell_count)
    wide_image = image.reshape(RHS, cell_count)
    projection = jnp.dot(flat_basis.astype(jnp.float32), wide_image.T.astype(jnp.float32), precision=highest, preferred_element_type=jnp.float32) / cell_count
    projected = wide_image - jnp.dot(projection.T.astype(jnp.float32), flat_basis.astype(jnp.float32), precision=highest, preferred_element_type=jnp.float32)
    gram_matrix = jnp.dot(projected.astype(jnp.float32), projected.T.astype(jnp.float32), precision=highest, preferred_element_type=jnp.float32) / cell_count
    lower_factor = jnp.linalg.cholesky(gram_matrix)
    solved = lax.linalg.triangular_solve(lower_factor, projected, left_side=True, lower=True)
    return (projection.reshape(NB, RHS, RHS), lower_factor.T, solved.reshape(RHS, NT, NZ, NY, NX))
```

```python
import jax
import jax.numpy as jnp
from jax import lax
from jax.sharding import Mesh, PartitionSpec as P

TM = ("y", "core")
SPACE = ("x", "z")


def size_of(axes):
    count = 1
    for axis in axes:
        count *= lax.axis_size(axis)
    return count


def group_sum(block, axes):
    count = size_of(axes)
    copies = jnp.broadcast_to(block, (count,) + block.shape)
    return lax.all_to_all(copies, axes, 0, 0).sum(0)


def step_weights(size_now, size_prev, first_row):
    step_ratio = size_now / size_prev
    ones_like = jnp.ones_like(step_ratio)
    weight_now = jnp.where(first_row, ones_like, (1.0 + 2.0 * step_ratio) / (1.0 + step_ratio))
    weight_one = jnp.where(first_row, ones_like, 1.0 + step_ratio)
    weight_two = jnp.where(
        first_row, jnp.zeros_like(step_ratio), step_ratio * step_ratio / (1.0 + step_ratio)
    )
    return (weight_now, weight_one, weight_two, 0.5 * size_now)


def spread(values):
    return values[None, :, None, None, None]


def per_device(basis, step_numerator, step_denominator):
    highest = lax.Precision.HIGHEST
    blocks, columns, step_count, planes, grid_y, grid_x = basis.shape
    current = basis[blocks - 1]
    size_now = step_numerator.astype(jnp.float32) / step_denominator.astype(jnp.float32)
    slabs = size_of(SPACE)
    groups = size_of(TM)
    up = [(i, i + 1) for i in range(slabs - 1)]
    down = [(i + 1, i) for i in range(slabs - 1)]
    later = [(i, i + 1) for i in range(groups - 1)]
    low = lax.ppermute(current[:, :, planes - 1 :], SPACE, up)
    high = lax.ppermute(current[:, :, :1], SPACE, down)
    earlier = lax.ppermute(current[:, step_count - 2 :], TM, later)
    size_before = lax.ppermute(size_now[step_count - 1 :], TM, later)
    global_step = lax.axis_index(TM) * step_count + jnp.arange(step_count, dtype=jnp.int32)
    first_row = global_step == 0
    size_prev = jnp.concatenate([size_before, size_now[:-1]])
    size_prev = jnp.where(first_row, size_now, size_prev)
    weight_now, weight_one, weight_two, kappa_step = step_weights(size_now, size_prev, first_row)
    extended = jnp.concatenate([earlier, current], axis=1)
    back_one = extended[:, 1 : step_count + 1]
    back_two = extended[:, 0:step_count]
    padded = jnp.concatenate([low, current, high], axis=2)
    beside = padded[:, :, 2:] + padded[:, :, :-2]
    pad_y = jnp.pad(current, ((0, 0), (0, 0), (0, 0), (1, 1), (0, 0)))
    beside = beside + pad_y[:, :, :, 2:] + pad_y[:, :, :, :-2]
    pad_x = jnp.pad(current, ((0, 0), (0, 0), (0, 0), (0, 0), (1, 1)))
    beside = beside + pad_x[..., 2:] + pad_x[..., :-2]
    image = (
        spread(weight_now) * current
        - spread(weight_one) * back_one
        + spread(weight_two) * back_two
        + spread(kappa_step) * (6.0 * current - beside)
    )
    cell_count = step_count * planes * grid_y * grid_x
    total_cells = cell_count * groups * slabs
    rows = blocks * columns
    flat_basis = basis.reshape(rows, cell_count)
    wide_image = image.reshape(columns, cell_count)
    both = jnp.concatenate([flat_basis, wide_image], axis=0)
    partial = jnp.dot(both, both.T, precision=highest, preferred_element_type=jnp.float32)
    products = group_sum(group_sum(partial, TM), SPACE) / total_cells
    projection = products[:rows, rows:]
    image_gram = products[rows:, rows:]
    basis_gram = products[:rows, :rows]
    twice = jnp.dot(projection.T, projection, precision=highest)
    quad = jnp.dot(projection.T, jnp.dot(basis_gram, projection, precision=highest), precision=highest)
    gram_matrix = image_gram - twice - twice + quad
    projected = wide_image - jnp.dot(
        projection.T, flat_basis, precision=highest, preferred_element_type=jnp.float32
    )
    lower_factor = jnp.linalg.cholesky(gram_matrix)
    solved = lax.linalg.triangular_solve(lower_factor, projected, left_side=True, lower=True)
    return (
        projection.reshape(blocks, columns, columns),
        lower_factor.T,
        solved.reshape(columns, step_count, planes, grid_y, grid_x),
    )


def solution(mesh):
    fine = Mesh(mesh.devices.reshape(8, 2, 4, 8), ("y", "core", "x", "z"))
    placed = (P(None, None, TM, SPACE, None, None), P(TM), P(TM))
    return jax.shard_map(
        per_device,
        mesh=fine,
        in_specs=placed,
        out_specs=(P(), P(), P(None, TM, SPACE, None, None)),
        check_vma=False,
    )
```

```python
import jax
import jax.numpy as jnp
from jax import lax
from jax.experimental import pallas as pl
from jax.experimental.pallas import tpu as pltpu
from jax.sharding import Mesh, PartitionSpec as P

TM = ("y", "core")
SPACE = ("x", "z")
COLS = 16
BLOCKS = 4
ROWS = BLOCKS * COLS
STEPS = 4
PLANES = 2
TILES = STEPS * PLANES
LINES = TILES * 8
CELLS = LINES * 128
TOTAL = 64 * 64 * 8 * 128
PARTS = 3
FULL = ROWS + COLS
HIGHEST = lax.Precision.HIGHEST
F32 = jnp.float32
BF16 = jnp.bfloat16
NT = (((1,), (1,)), ((), ()))
NN = (((1,), (0,)), ((), ()))


def params(megabytes):
    return pltpu.CompilerParams(vmem_limit_bytes=megabytes * 1024 * 1024)


def size_of(axes):
    count = 1
    for axis in axes:
        count *= lax.axis_size(axis)
    return count


def split(value):
    first = value.astype(BF16)
    rest = value - first.astype(F32)
    second = rest.astype(BF16)
    third = (rest - second.astype(F32)).astype(BF16)
    return first, second, third


def step_sizes(num_ref, den_ref):
    sizes = []
    for step in range(STEPS):
        top = jnp.full((8, 128), num_ref[step]).astype(F32)
        bottom = jnp.full((8, 128), den_ref[step]).astype(F32)
        sizes.append(top / bottom)
    return sizes


def edges_kernel(num_ref, den_ref, basis_ref, up_ref, down_ref, late_ref, size_ref, sems):
    last = BLOCKS - 1
    copies = [
        pltpu.make_async_copy(basis_ref.at[last, :, :, PLANES - 1], up_ref, sems.at[0]),
        pltpu.make_async_copy(basis_ref.at[last, :, :, 0], down_ref, sems.at[1]),
        pltpu.make_async_copy(
            basis_ref.at[last, :, pl.ds(STEPS - 2, 2)], late_ref.at[pl.ds(0, COLS)], sems.at[2]
        ),
    ]
    for copy in copies:
        copy.start()
    final_size = step_sizes(num_ref, den_ref)[STEPS - 1]
    for step in range(2):
        for plane in range(PLANES):
            size_ref[step, plane] = final_size
    tail = pltpu.make_async_copy(size_ref, late_ref.at[COLS], sems.at[3])
    tail.start()
    for copy in copies:
        copy.wait()
    tail.wait()


def edges(basis, num, den):
    smem = pl.BlockSpec(memory_space=pltpu.SMEM)
    anywhere = pl.BlockSpec(memory_space=pl.ANY)
    return pl.pallas_call(
        edges_kernel,
        out_shape=(
            jax.ShapeDtypeStruct((COLS, STEPS, 8, 128), F32),
            jax.ShapeDtypeStruct((COLS, STEPS, 8, 128), F32),
            jax.ShapeDtypeStruct((COLS + 1, 2, PLANES, 8, 128), F32),
        ),
        in_specs=[smem, smem, anywhere],
        out_specs=(anywhere, anywhere, anywhere),
        scratch_shapes=[pltpu.VMEM((2, PLANES, 8, 128), F32), pltpu.SemaphoreType.DMA((4,))],
        compiler_params=params(4),
        name="edges",
    )(num, den, basis)


def gathered_rows(field_ref, parts_ref, count):
    @pl.loop(0, TILES)
    def _(tile):
        for line in range(8):
            place = tile * 8 + line
            value = field_ref[pl.ds(place, count, stride=LINES), :]
            lanes = pl.ds(pl.multiple_of(place * 128, 128), 128)
            for part, piece in enumerate(split(value)):
                parts_ref[pl.ds(part * count, count), lanes] = piece


def part_products(products, count, offset, width):
    total = None
    for b in range(PARTS):
        group = None
        for a in range(PARTS - b):
            piece = products[a * count : (a + 1) * count, offset + b * width : offset + (b + 1) * width]
            group = piece if group is None else group + piece
        total = group if total is None else total + group
    return total


def basis_kernel(field_ref, parts_ref, packed_ref):
    gathered_rows(field_ref, parts_ref, ROWS)
    whole = parts_ref[...]
    products = lax.dot_general(whole, whole, NT, preferred_element_type=F32)
    gram = part_products(products, ROWS, 0, ROWS)
    pieces = [jnp.zeros((COLS, FULL), F32)]
    for block in range(BLOCKS):
        pieces.append(gram[block * COLS : (block + 1) * COLS, block * COLS :])
    used = FULL + sum(ROWS - block * COLS for block in range(BLOCKS))
    pieces.append(jnp.zeros((COLS, 256 - used), F32))
    packed_ref[...] = jnp.concatenate(pieces, axis=1)


def basis_products(flat):
    vmem = pl.BlockSpec(memory_space=pltpu.VMEM)
    return pl.pallas_call(
        basis_kernel,
        out_shape=(
            jax.ShapeDtypeStruct((PARTS * ROWS, CELLS), BF16),
            jax.ShapeDtypeStruct((COLS, 256), F32),
        ),
        in_specs=[vmem],
        out_specs=(vmem, vmem),
        compiler_params=params(20),
        name="basis_products",
    )(flat)


def image_kernel(
    num_ref, den_ref, field_ref, low_ref, high_ref, late_ref, basis_ref, packed_ref,
    parts_ref, copies_ref, image_ref,
):
    sizes = step_sizes(num_ref, den_ref)
    first = (lax.axis_index("y") == 0) & (lax.axis_index("core") == 0)
    start = jnp.full((8, 128), first.astype(jnp.int32)) == 1
    weights = []
    for step in range(STEPS):
        if step == 0:
            before = jnp.where(start, sizes[0], late_ref[COLS, 0, 0])
        else:
            before = sizes[step - 1]
        ratio = sizes[step] / before
        now = (1.0 + 2.0 * ratio) / (1.0 + ratio)
        one = 1.0 + ratio
        two = ratio * ratio / (1.0 + ratio)
        if step == 0:
            now = jnp.where(start, 1.0, now)
            one = jnp.where(start, 1.0, one)
            two = jnp.where(start, 0.0, two)
        weights.append((now, one, two, 0.5 * sizes[step]))
    line = lax.broadcasted_iota(jnp.int32, (8, 128), 0)
    lane = lax.broadcasted_iota(jnp.int32, (8, 128), 1)

    @pl.loop(0, COLS)
    def _(col):
        def own(step, plane):
            place = pl.multiple_of(col * LINES + (step * PLANES + plane) * 8, 8)
            return field_ref[pl.ds(place, 8), :]

        here = [[own(step, plane) for plane in range(PLANES)] for step in range(STEPS)]
        past = [[late_ref[col, step, plane] for plane in range(PLANES)] for step in range(2)]
        line_up = past + here
        for step in range(STEPS):
            now, one, two, kappa = weights[step]
            for plane in range(PLANES):
                value = here[step][plane]
                below = low_ref[col, step] if plane == 0 else here[step][plane - 1]
                above = high_ref[col, step] if plane == PLANES - 1 else here[step][plane + 1]
                beside = above + below
                beside += jnp.where(line < 7, pltpu.roll(value, 7, 0), 0.0)
                beside += jnp.where(line > 0, pltpu.roll(value, 1, 0), 0.0)
                beside += jnp.where(lane < 127, pltpu.roll(value, 127, 1), 0.0)
                beside += jnp.where(lane > 0, pltpu.roll(value, 1, 1), 0.0)
                result = (
                    now * value
                    - one * line_up[step + 1][plane]
                    + two * line_up[step][plane]
                    + kappa * (6.0 * value - beside)
                )
                place = pl.multiple_of(col * LINES + (step * PLANES + plane) * 8, 8)
                image_ref[pl.ds(place, 8), :] = result

    gathered_rows(image_ref, parts_ref, COLS)
    own_parts = parts_ref[...]
    with_basis = lax.dot_general(own_parts, basis_ref[...], NT, preferred_element_type=F32)
    with_self = lax.dot_general(own_parts, own_parts, NT, preferred_element_type=F32)
    main = jnp.concatenate(
        [
            part_products(with_basis, COLS, 0, ROWS),
            part_products(with_self, COLS, 0, COLS),
            jnp.zeros((COLS, 256 - FULL), F32),
        ],
        axis=1,
    )
    payload = main + packed_ref[...]
    for copy in range(copies_ref.shape[0]):
        copies_ref[copy, 0] = payload[:, :128]
        copies_ref[copy, 1] = payload[:, 128:]


def image_products(num, den, flat, low, high, late, basis_parts, packed, count):
    smem = pl.BlockSpec(memory_space=pltpu.SMEM)
    vmem = pl.BlockSpec(memory_space=pltpu.VMEM)
    per_block = COLS * LINES
    return pl.pallas_call(
        image_kernel,
        grid=(1,),
        out_shape=(
            jax.ShapeDtypeStruct((PARTS * COLS, CELLS), BF16),
            jax.ShapeDtypeStruct((count, 2, COLS, 128), F32),
        ),
        in_specs=[
            smem,
            smem,
            pl.BlockSpec((per_block, 128), lambda i: (BLOCKS - 1, 0)),
            vmem,
            vmem,
            vmem,
            vmem,
            vmem,
        ],
        out_specs=(vmem, vmem),
        scratch_shapes=[pltpu.VMEM((per_block, 128), F32)],
        compiler_params=params(20),
        name="image_products",
    )(num, den, flat, low, high, late, basis_parts, packed)


def finish_kernel(sums_ref, parts_ref, hess_ref, triangle_ref, next_ref):
    sums = sums_ref[0]
    for piece in range(1, sums_ref.shape[0]):
        sums = sums + sums_ref[piece]
    sums = sums * (1.0 / TOTAL)
    left, right = sums[0], sums[1]
    packed = jnp.concatenate([left, right], axis=1)
    proj = packed[:, :ROWS]
    image_gram = packed[:, ROWS:FULL]
    row = lax.broadcasted_iota(jnp.int32, (COLS, COLS), 0)
    col = lax.broadcasted_iota(jnp.int32, (COLS, COLS), 1)
    upper = []
    offset = FULL
    for block in range(BLOCKS):
        width = ROWS - block * COLS
        rows = packed[:, offset : offset + width]
        pieces = [0.5 * rows[:, :COLS]]
        if block:
            pieces.insert(0, jnp.zeros((COLS, block * COLS), F32))
        if width > COLS:
            pieces.append(rows[:, COLS:])
        upper.append(jnp.concatenate(pieces, axis=1))
        offset += width
    half = jnp.concatenate(upper, axis=0)
    carried = lax.dot_general(proj, half, NN, precision=HIGHEST, preferred_element_type=F32) - proj
    cross = lax.dot_general(carried, proj, NT, precision=HIGHEST, preferred_element_type=F32)
    cross_t = lax.dot_general(proj, carried, NT, precision=HIGHEST, preferred_element_type=F32)
    gram = image_gram + (cross + cross_t)
    eye = jnp.where(row == col, 1.0, 0.0).astype(F32)
    work = jnp.concatenate(
        [gram, -proj, eye, jnp.zeros((COLS, 128 - FULL - COLS), F32)], axis=1
    )
    wide_row = lax.broadcasted_iota(jnp.int32, (COLS, 128), 0)
    scale = jnp.zeros((COLS, 128), F32)
    for step in range(COLS):
        column = jnp.broadcast_to(work[:, step : step + 1], (COLS, 128))
        pivot = jnp.broadcast_to(column[step : step + 1], (COLS, 128))
        pivot_row = jnp.broadcast_to(work[step : step + 1], (COLS, 128))
        work = work - jnp.where(wide_row > step, column / pivot, 0.0) * pivot_row
        scale = jnp.where(wide_row == step, lax.rsqrt(pivot), scale)
    work = work * scale
    hess_ref[...] = proj.T
    triangle_ref[...] = jnp.where(row <= col, work[:, :COLS], 0.0)
    factors = split(work[:, COLS : COLS + FULL])
    stacked = []
    for part in range(PARTS):
        on_basis = factors[part][:, :ROWS]
        on_image = factors[part][:, ROWS:]
        pieces = []
        for piece in (on_basis, on_image):
            for other in range(PARTS):
                pieces.append(piece if other < PARTS - part else jnp.zeros_like(piece))
        stacked.append(jnp.concatenate(pieces, axis=1))
    factor = jnp.concatenate(stacked, axis=0)
    for tile in range(TILES):
        lanes = pl.ds(tile * 1024, 1024)
        product = lax.dot_general(factor, parts_ref[:, lanes], NN, preferred_element_type=F32)
        value = product[:COLS] + (product[COLS : 2 * COLS] + product[2 * COLS :])
        for line in range(8):
            next_ref[pl.ds(tile * 8 + line, COLS, stride=LINES), :] = value[
                :, line * 128 : (line + 1) * 128
            ]


def finish(sums, parts):
    vmem = pl.BlockSpec(memory_space=pltpu.VMEM)
    return pl.pallas_call(
        finish_kernel,
        out_shape=(
            jax.ShapeDtypeStruct((ROWS, COLS), F32),
            jax.ShapeDtypeStruct((COLS, COLS), F32),
            jax.ShapeDtypeStruct((COLS * LINES, 128), F32),
        ),
        in_specs=[vmem, vmem],
        out_specs=(vmem, vmem, vmem),
        compiler_params=params(20),
        name="finish",
    )(sums, parts)


def exchanged(copies, axes):
    return lax.all_to_all(copies, axes, 0, 0)


def per_device(basis, num, den):
    slabs = size_of(SPACE)
    groups = size_of(TM)
    above = [(i, i + 1) for i in range(slabs - 1)]
    below = [(i + 1, i) for i in range(slabs - 1)]
    later = [(i, i + 1) for i in range(groups - 1)]
    flat = basis.reshape(ROWS * LINES, 128)
    up, down, late = edges(basis, num, den)
    low = lax.ppermute(up, SPACE, above)
    high = lax.ppermute(down, SPACE, below)
    earlier = lax.ppermute(late, TM, later)
    basis_parts, packed = basis_products(flat)
    image_parts, copies = image_products(
        num, den, flat, low, high, earlier, basis_parts, packed, groups
    )
    sums = exchanged(copies, TM).sum(0)
    sums = exchanged(jnp.broadcast_to(sums, (slabs,) + sums.shape), SPACE)
    parts = jnp.concatenate([basis_parts, image_parts], axis=0)
    hess, triangle, following = finish(sums, parts)
    return (
        hess.reshape(BLOCKS, COLS, COLS),
        triangle,
        following.reshape(COLS, STEPS, PLANES, 8, 128),
    )


def solution(mesh):
    fine = Mesh(mesh.devices.reshape(8, 2, 4, 8), ("y", "core", "x", "z"))
    placed = (P(None, None, TM, SPACE, None, None), P(TM), P(TM))
    return jax.shard_map(
        per_device,
        mesh=fine,
        in_specs=placed,
        out_specs=(P(), P(), P(None, TM, SPACE, None, None)),
        check_vma=False,
    )
```

```python
import jax
import jax.numpy as jnp
from jax import lax
from jax.experimental import pallas as pl
from jax.experimental.pallas import tpu as pltpu
from jax.sharding import Mesh, PartitionSpec as P

TM = ("y", "core")
SPACE = ("x", "z")
COLS = 16
BLOCKS = 4
ROWS = BLOCKS * COLS
STEPS = 4
PLANES = 2
TILES = STEPS * PLANES
LINES = TILES * 8
CELLS = LINES * 128
TOTAL = 64 * 64 * 8 * 128
PARTS = 3
GROUPS = 16
SLABS = 32
FULL = ROWS + COLS
HIGHEST = lax.Precision.HIGHEST
F32 = jnp.float32
BF16 = jnp.bfloat16
NT = (((1,), (1,)), ((), ()))
NN = (((1,), (0,)), ((), ()))


def params(megabytes):
    return pltpu.CompilerParams(vmem_limit_bytes=megabytes * 1024 * 1024)


def in_hbm(array):
    return pltpu.with_memory_space_constraint(array, pltpu.HBM)


def size_of(axes):
    count = 1
    for axis in axes:
        count *= lax.axis_size(axis)
    return count


def split(value):
    first = value.astype(BF16)
    rest = value - first.astype(F32)
    second = rest.astype(BF16)
    third = (rest - second.astype(F32)).astype(BF16)
    return first, second, third


def edges_kernel(
    num_hbm, den_hbm, basis_hbm, up_ref, down_ref, late_ref, sizes_ref, num_ref, den_ref, tail_ref, sems
):
    last = BLOCKS - 1
    counts = [
        pltpu.make_async_copy(num_hbm, num_ref, sems.at[4]),
        pltpu.make_async_copy(den_hbm, den_ref, sems.at[5]),
    ]
    copies = [
        pltpu.make_async_copy(basis_hbm.at[last, :, :, PLANES - 1], up_ref, sems.at[0]),
        pltpu.make_async_copy(basis_hbm.at[last, :, :, 0], down_ref, sems.at[1]),
        pltpu.make_async_copy(
            basis_hbm.at[last, :, pl.ds(STEPS - 2, 2)], late_ref.at[pl.ds(0, COLS)], sems.at[2]
        ),
    ]
    for copy in counts + copies:
        copy.start()
    for copy in counts:
        copy.wait()
    for step in range(STEPS):
        top = jnp.full((8, 128), num_ref[step]).astype(F32)
        bottom = jnp.full((8, 128), den_ref[step]).astype(F32)
        sizes_ref[step] = top / bottom
    for step in range(2):
        for plane in range(PLANES):
            tail_ref[step, plane] = sizes_ref[STEPS - 1]
    tail = pltpu.make_async_copy(tail_ref, late_ref.at[COLS], sems.at[3])
    tail.start()
    for copy in copies:
        copy.wait()
    tail.wait()


def edges(basis, num, den):
    hbm = pl.BlockSpec(memory_space=pltpu.HBM)
    vmem = pl.BlockSpec(memory_space=pltpu.VMEM)
    anywhere = pl.BlockSpec(memory_space=pl.ANY)
    return pl.pallas_call(
        edges_kernel,
        out_shape=(
            jax.ShapeDtypeStruct((COLS, STEPS, 8, 128), F32),
            jax.ShapeDtypeStruct((COLS, STEPS, 8, 128), F32),
            jax.ShapeDtypeStruct((COLS + 1, 2, PLANES, 8, 128), F32),
            jax.ShapeDtypeStruct((STEPS, 8, 128), F32),
        ),
        in_specs=[hbm, hbm, hbm],
        out_specs=(anywhere, anywhere, anywhere, vmem),
        scratch_shapes=[
            pltpu.SMEM((STEPS,), jnp.int32),
            pltpu.SMEM((STEPS,), jnp.int32),
            pltpu.VMEM((2, PLANES, 8, 128), F32),
            pltpu.SemaphoreType.DMA((6,)),
        ],
        compiler_params=params(4),
        name="edges",
    )(in_hbm(num), in_hbm(den), in_hbm(basis))


def gather_block(field_ref, parts_ref, row, stride):
    @pl.loop(0, TILES)
    def _(tile):
        for line in range(8):
            place = tile * 8 + line
            value = field_ref[pl.ds(place, COLS, stride=LINES), :]
            lanes = pl.ds(pl.multiple_of(place * 128, 128), 128)
            for part, piece in enumerate(split(value)):
                parts_ref[pl.ds(row + part * stride, COLS), lanes] = piece


def part_products(products, count, offset, width):
    total = None
    for b in range(PARTS):
        group = None
        for a in range(PARTS - b):
            piece = products[a * count : (a + 1) * count, offset + b * width : offset + (b + 1) * width]
            group = piece if group is None else group + piece
        total = group if total is None else total + group
    return total


def basis_kernel(flat_hbm, parts_ref, gram_ref, last_ref, field_ref, sems):
    per_block = COLS * LINES
    copies = []
    for block in range(BLOCKS):
        rows = pl.ds(block * per_block, per_block)
        target = last_ref if block == BLOCKS - 1 else field_ref.at[block]
        copies.append(pltpu.make_async_copy(flat_hbm.at[rows], target, sems.at[block]))
        copies[-1].start()
    for block in range(BLOCKS):
        copies[block].wait()
        source = last_ref if block == BLOCKS - 1 else field_ref.at[block]
        gather_block(source, parts_ref, block * COLS, ROWS)
    whole = parts_ref[: PARTS * ROWS]
    products = lax.dot_general(whole, whole, NT, preferred_element_type=F32)
    gram = part_products(products, ROWS, 0, ROWS)
    packed = jnp.concatenate([gram[: ROWS // 2], gram[ROWS // 2 :]], axis=1)
    for piece in range(GROUPS):
        gram_ref[piece] = packed[piece * 2 : piece * 2 + 2]


def basis_products(flat):
    vmem = pl.BlockSpec(memory_space=pltpu.VMEM)
    per_block = COLS * LINES
    return pl.pallas_call(
        basis_kernel,
        out_shape=(
            jax.ShapeDtypeStruct((PARTS * FULL, CELLS), BF16),
            jax.ShapeDtypeStruct((GROUPS, 2, 128), F32),
            jax.ShapeDtypeStruct((per_block, 128), F32),
        ),
        in_specs=[pl.BlockSpec(memory_space=pltpu.HBM)],
        out_specs=(vmem, vmem, vmem),
        scratch_shapes=[
            pltpu.VMEM((BLOCKS - 1, per_block, 128), F32),
            pltpu.SemaphoreType.DMA((BLOCKS,)),
        ],
        compiler_params=params(20),
        name="basis_products",
    )(in_hbm(flat))


def image_kernel(
    sizes_ref, field_ref, low_ref, high_ref, late_ref, parts_in_ref, parts_ref, main_ref, image_ref
):
    sizes = [sizes_ref[step] for step in range(STEPS)]
    first = (lax.axis_index("y") == 0) & (lax.axis_index("core") == 0)
    start = jnp.full((8, 128), first.astype(jnp.int32)) == 1
    weights = []
    for step in range(STEPS):
        if step == 0:
            before = jnp.where(start, sizes[0], late_ref[COLS, 0, 0])
        else:
            before = sizes[step - 1]
        ratio = sizes[step] / before
        now = (1.0 + 2.0 * ratio) / (1.0 + ratio)
        one = 1.0 + ratio
        two = ratio * ratio / (1.0 + ratio)
        if step == 0:
            now = jnp.where(start, 1.0, now)
            one = jnp.where(start, 1.0, one)
            two = jnp.where(start, 0.0, two)
        weights.append((now, one, two, 0.5 * sizes[step]))
    line = lax.broadcasted_iota(jnp.int32, (8, 128), 0)
    lane = lax.broadcasted_iota(jnp.int32, (8, 128), 1)

    @pl.loop(0, COLS)
    def _(col):
        def own(step, plane):
            place = pl.multiple_of(col * LINES + (step * PLANES + plane) * 8, 8)
            return field_ref[pl.ds(place, 8), :]

        here = [[own(step, plane) for plane in range(PLANES)] for step in range(STEPS)]
        past = [[late_ref[col, step, plane] for plane in range(PLANES)] for step in range(2)]
        line_up = past + here
        for step in range(STEPS):
            now, one, two, kappa = weights[step]
            for plane in range(PLANES):
                value = here[step][plane]
                below = low_ref[col, step] if plane == 0 else here[step][plane - 1]
                above = high_ref[col, step] if plane == PLANES - 1 else here[step][plane + 1]
                beside = above + below
                beside += jnp.where(line < 7, pltpu.roll(value, 7, 0), 0.0)
                beside += jnp.where(line > 0, pltpu.roll(value, 1, 0), 0.0)
                beside += jnp.where(lane < 127, pltpu.roll(value, 127, 1), 0.0)
                beside += jnp.where(lane > 0, pltpu.roll(value, 1, 1), 0.0)
                result = (
                    now * value
                    - one * line_up[step + 1][plane]
                    + two * line_up[step][plane]
                    + kappa * (6.0 * value - beside)
                )
                place = pl.multiple_of(col * LINES + (step * PLANES + plane) * 8, 8)
                image_ref[pl.ds(place, 8), :] = result

    base = PARTS * ROWS
    gather_block(image_ref, parts_ref, base, COLS)
    own_parts = parts_ref[base:]
    products = lax.dot_general(own_parts, parts_ref[...], NT, preferred_element_type=F32)
    proj = part_products(products, COLS, 0, ROWS)
    gram = part_products(products, COLS, base, COLS)
    packed = jnp.concatenate([proj[:8], proj[8:]], axis=1)
    main_ref[0] = packed[:4]
    main_ref[1] = packed[4:]
    for half in range(2):
        pieces = [gram[half * 8 + row : half * 8 + row + 1] for row in range(8)]
        main_ref[2, half : half + 1] = jnp.concatenate(pieces, axis=1)
    main_ref[2, 2:4] = jnp.zeros((2, 128), F32)


def image_products(sizes, field, low, high, late, parts):
    vmem = pl.BlockSpec(memory_space=pltpu.VMEM)
    return pl.pallas_call(
        image_kernel,
        out_shape=(
            jax.ShapeDtypeStruct((PARTS * FULL, CELLS), BF16),
            jax.ShapeDtypeStruct((3, 4, 128), F32),
        ),
        in_specs=[vmem] * 6,
        out_specs=(vmem, vmem),
        scratch_shapes=[pltpu.VMEM((COLS * LINES, 128), F32)],
        input_output_aliases={5: 0},
        compiler_params=params(20),
        name="image_products",
    )(sizes, field, low, high, late, parts)


def join_kernel(main_ref, gram_ref, copies_ref):
    gram = gram_ref[0]
    for piece in range(1, GROUPS):
        gram = gram + gram_ref[piece]
    for copy in range(SLABS):
        copies_ref[copy, 0] = main_ref[0]
        copies_ref[copy, 1] = main_ref[1]
        copies_ref[copy, 2, 0:2] = main_ref[2, 0:2]
        copies_ref[copy, 2, 2:4] = gram


def join(main, gram):
    vmem = pl.BlockSpec(memory_space=pltpu.VMEM)
    return pl.pallas_call(
        join_kernel,
        out_shape=jax.ShapeDtypeStruct((SLABS, 3, 4, 128), F32),
        in_specs=[vmem, vmem],
        out_specs=vmem,
        compiler_params=params(4),
        name="join",
    )(main, gram)


def finish_kernel(sums_ref, parts_ref, hess_ref, triangle_ref, next_ref, gram_ref):
    sums = sums_ref[0]
    for piece in range(1, GROUPS):
        sums = sums + sums_ref[piece]
    for piece in range(GROUPS):
        gram_ref[piece * 2 : piece * 2 + 2] = sums_ref[piece, 2, 2:4]
    sums = sums * (1.0 / TOTAL)
    proj = jnp.concatenate(
        [sums[0, :, :ROWS], sums[1, :, :ROWS], sums[0, :, ROWS:], sums[1, :, ROWS:]], axis=0
    )
    image_gram = jnp.concatenate(
        [
            sums[2, half : half + 1, line * COLS : (line + 1) * COLS]
            for half in range(2)
            for line in range(8)
        ],
        axis=0,
    )
    row = lax.broadcasted_iota(jnp.int32, (COLS, COLS), 0)
    col = lax.broadcasted_iota(jnp.int32, (COLS, COLS), 1)
    packed = gram_ref[...] * (1.0 / TOTAL)
    basis_gram = jnp.concatenate([packed[:, :ROWS], packed[:, ROWS:]], axis=0)
    carried = lax.dot_general(
        proj, basis_gram, NN, precision=HIGHEST, preferred_element_type=F32
    ) - 2.0 * proj
    gram = image_gram + lax.dot_general(
        carried, proj, NT, precision=HIGHEST, preferred_element_type=F32
    )
    eye = jnp.where(row == col, 1.0, 0.0).astype(F32)
    work = jnp.concatenate(
        [gram, -proj, eye, jnp.zeros((COLS, 128 - FULL - COLS), F32)], axis=1
    )
    wide_row = lax.broadcasted_iota(jnp.int32, (COLS, 128), 0)
    scale = jnp.zeros((COLS, 128), F32)
    for step in range(COLS):
        column = jnp.broadcast_to(work[:, step : step + 1], (COLS, 128))
        pivot = jnp.broadcast_to(column[step : step + 1], (COLS, 128))
        pivot_row = jnp.broadcast_to(work[step : step + 1], (COLS, 128))
        work = work - jnp.where(wide_row > step, column / pivot, 0.0) * pivot_row
        scale = jnp.where(wide_row == step, lax.rsqrt(pivot), scale)
    work = work * scale
    hess_ref[...] = proj.T
    triangle_ref[...] = jnp.where(row <= col, work[:, :COLS], 0.0)
    factors = split(work[:, COLS : COLS + FULL])
    stacked = []
    for part in range(PARTS):
        on_basis = factors[part][:, :ROWS]
        on_image = factors[part][:, ROWS:]
        pieces = []
        for piece in (on_basis, on_image):
            for other in range(PARTS):
                pieces.append(piece if other < PARTS - part else jnp.zeros_like(piece))
        stacked.append(jnp.concatenate(pieces, axis=1))
    factor = jnp.concatenate(stacked, axis=0)
    for tile in range(TILES):
        lanes = pl.ds(tile * 1024, 1024)
        product = lax.dot_general(factor, parts_ref[:, lanes], NN, preferred_element_type=F32)
        value = product[:COLS] + (product[COLS : 2 * COLS] + product[2 * COLS :])
        for line in range(8):
            next_ref[pl.ds(tile * 8 + line, COLS, stride=LINES), :] = value[
                :, line * 128 : (line + 1) * 128
            ]


def finish(sums, parts):
    vmem = pl.BlockSpec(memory_space=pltpu.VMEM)
    return pl.pallas_call(
        finish_kernel,
        out_shape=(
            jax.ShapeDtypeStruct((ROWS, COLS), F32),
            jax.ShapeDtypeStruct((COLS, COLS), F32),
            jax.ShapeDtypeStruct((COLS * LINES, 128), F32),
        ),
        in_specs=[vmem, vmem],
        out_specs=(vmem, vmem, vmem),
        scratch_shapes=[pltpu.VMEM((ROWS // 2, 128), F32)],
        compiler_params=params(20),
        name="finish",
    )(sums, parts)


def exchanged(copies, axes):
    return lax.all_to_all(copies, axes, 0, 0)


def per_device(basis, num, den):
    slabs = size_of(SPACE)
    groups = size_of(TM)
    above = [(i, i + 1) for i in range(slabs - 1)]
    below = [(i + 1, i) for i in range(slabs - 1)]
    later = [(i, i + 1) for i in range(groups - 1)]
    flat = basis.reshape(ROWS * LINES, 128)
    up, down, late, sizes = edges(basis, num, den)
    low = lax.ppermute(up, SPACE, above)
    high = lax.ppermute(down, SPACE, below)
    earlier = lax.ppermute(late, TM, later)
    parts, basis_gram, field = basis_products(flat)
    basis_gram = exchanged(basis_gram, TM)
    parts, main = image_products(sizes, field, low, high, earlier, parts)
    sums = exchanged(join(main, basis_gram), SPACE).sum(0)
    sums = exchanged(jnp.broadcast_to(sums, (groups,) + sums.shape), TM)
    hess, triangle, following = finish(sums, parts)
    return (
        hess.reshape(BLOCKS, COLS, COLS),
        triangle,
        following.reshape(COLS, STEPS, PLANES, 8, 128),
    )


def solution(mesh):
    fine = Mesh(mesh.devices.reshape(8, 2, 4, 8), ("y", "core", "x", "z"))
    placed = (P(None, None, TM, SPACE, None, None), P(TM), P(TM))
    return jax.shard_map(
        per_device,
        mesh=fine,
        in_specs=placed,
        out_specs=(P(), P(), P(None, TM, SPACE, None, None)),
        check_vma=False,
    )
```

```python
import jax
import jax.numpy as jnp
from jax import lax
from jax.experimental import pallas as pl
from jax.experimental.pallas import tpu as pltpu
from jax.sharding import Mesh, PartitionSpec as P

TM = ("y", "core")
SPACE = ("x", "z")
GROUPS = 16
SLABS = 32
COLS = 16
BLOCKS = 4
ROWS = BLOCKS * COLS
FULL = ROWS + COLS
STEPS = 4
PLANES = 2
LINES = 8
PLACES = STEPS * PLANES * LINES
CELLS = PLACES * 128
TOTAL = 64 * 64 * 8 * 128
PARTS = 3
CHUNKS = 4
HIGHEST = lax.Precision.HIGHEST
F32 = jnp.float32
BF16 = jnp.bfloat16
NT = (((1,), (1,)), ((), ()))
NN = (((1,), (0,)), ((), ()))
VMEM = pl.BlockSpec(memory_space=pltpu.VMEM)
HBM = pl.BlockSpec(memory_space=pltpu.HBM)


def params(megabytes):
    return pltpu.CompilerParams(vmem_limit_bytes=megabytes * 1024 * 1024)


def in_hbm(array):
    return pltpu.with_memory_space_constraint(array, pltpu.HBM)


def size_of(axes):
    count = 1
    for axis in axes:
        count *= lax.axis_size(axis)
    return count


def place_of(step, plane, line):
    return (step * PLANES + plane) * LINES + line


def split(value):
    first = value.astype(BF16)
    rest = value - first.astype(F32)
    second = rest.astype(BF16)
    third = (rest - second.astype(F32)).astype(BF16)
    return first, second, third


def faces_kernel(basis_hbm, up_ref, down_ref, sems):
    copies = []
    columns = pl.ds(ROWS - COLS, COLS)
    for step in range(STEPS):
        for line in range(LINES):
            for plane, target in ((PLANES - 1, up_ref), (0, down_ref)):
                source = basis_hbm.at[columns, place_of(step, plane, line), 0]
                copies.append(
                    pltpu.make_async_copy(
                        source, target.at[step * LINES + line], sems.at[len(copies)]
                    )
                )
    for copy in copies:
        copy.start()
    for copy in copies:
        copy.wait()


def faces(basis):
    face = jax.ShapeDtypeStruct((STEPS * LINES, COLS, 128), F32)
    return pl.pallas_call(
        faces_kernel,
        out_shape=(face, face),
        in_specs=[HBM],
        out_specs=(VMEM, VMEM),
        scratch_shapes=[pltpu.SemaphoreType.DMA((2 * STEPS * LINES,))],
        compiler_params=params(4),
        name="faces",
    )(in_hbm(basis))


def ending_kernel(
    num_hbm, den_hbm, basis_hbm, after_ref, late_ref, sizes_ref, num_ref, den_ref, sems
):
    counts = [
        pltpu.make_async_copy(num_hbm, num_ref, sems.at[0]),
        pltpu.make_async_copy(den_hbm, den_ref, sems.at[1]),
    ]
    copies = []
    columns = pl.ds(ROWS - COLS, COLS)
    first = place_of(STEPS - 2, 0, 0)
    for place in range(first, PLACES):
        copies.append(
            pltpu.make_async_copy(
                basis_hbm.at[columns, place, 0], late_ref.at[place - first], sems.at[2 + len(copies)]
            )
        )
    for copy in counts + copies:
        copy.start()
    for copy in counts:
        copy.wait()
    for step in range(STEPS):
        top = jnp.full((COLS, 128), num_ref[step]).astype(F32)
        bottom = jnp.full((COLS, 128), den_ref[step]).astype(F32)
        sizes_ref[step] = top / bottom
    late_ref[PLACES - first] = sizes_ref[STEPS - 1]
    for copy in copies:
        copy.wait()


def ending(num, den, basis, after):
    kept = 2 * PLANES * LINES
    return pl.pallas_call(
        ending_kernel,
        out_shape=(
            jax.ShapeDtypeStruct((kept + 1, COLS, 128), F32),
            jax.ShapeDtypeStruct((STEPS, COLS, 128), F32),
        ),
        in_specs=[HBM, HBM, HBM, pl.BlockSpec(memory_space=pl.ANY)],
        out_specs=(VMEM, VMEM),
        scratch_shapes=[
            pltpu.SMEM((STEPS,), jnp.int32),
            pltpu.SMEM((STEPS,), jnp.int32),
            pltpu.SemaphoreType.DMA((2 + kept,)),
        ],
        compiler_params=params(4),
        name="ending",
    )(in_hbm(num), in_hbm(den), in_hbm(basis), after)


def part_products(products, count, offset, width):
    total = None
    for b in range(PARTS):
        group = None
        for a in range(PARTS - b):
            piece = products[a * count : (a + 1) * count, offset + b * width : offset + (b + 1) * width]
            group = piece if group is None else group + piece
        total = group if total is None else total + group
    return total


def basis_kernel(basis_hbm, parts_ref, last_ref, keep_ref, give_ref, field_ref, sems):
    copies = [
        pltpu.make_async_copy(basis_hbm.at[:, place, 0], field_ref.at[place], sems.at[place])
        for place in range(PLACES)
    ]
    for copy in copies:
        copy.start()
    products = None
    per_chunk = PLACES // CHUNKS
    for chunk in range(CHUNKS):
        for place in range(chunk * per_chunk, (chunk + 1) * per_chunk):
            copies[place].wait()
            value = field_ref[place]
            last_ref[place] = value[ROWS - COLS :]
            for part, piece in enumerate(split(value)):
                parts_ref[part * ROWS : (part + 1) * ROWS, place * 128 : (place + 1) * 128] = piece
        lanes = slice(chunk * per_chunk * 128, (chunk + 1) * per_chunk * 128)
        piece = parts_ref[: PARTS * ROWS, lanes]
        product = lax.dot_general(piece, piece, NT, preferred_element_type=F32)
        products = product if products is None else products + product
    gram = part_products(products, ROWS, 0, ROWS)
    rows = [gram[block * COLS : (block + 1) * COLS, block * COLS :] for block in range(BLOCKS)]
    packed = jnp.concatenate([rows[0], rows[1], rows[3]], axis=1)
    halves = []
    for half in range(2):
        rest = rows[2][half * 8 : half * 8 + 8]
        rest = jnp.concatenate([rest[2 * i : 2 * i + 2] for i in range(4)], axis=1)
        halves.append((packed[half * 8 : half * 8 + 8], rest))
    own = lax.axis_index("core")
    first = jnp.full((8, 128), own) == 0
    for target, flip in ((keep_ref, False), (give_ref, True)):
        one, two = (halves[1], halves[0]) if flip else (halves[0], halves[1])
        target[0:8] = jnp.where(first, one[0], two[0])
        target[8:10] = jnp.where(first[:2], one[1], two[1])
        target[10:16] = jnp.zeros((6, 128), F32)


def basis_products(basis):
    return pl.pallas_call(
        basis_kernel,
        out_shape=(
            jax.ShapeDtypeStruct((PARTS * FULL, CELLS), BF16),
            jax.ShapeDtypeStruct((PLACES, COLS, 128), F32),
            jax.ShapeDtypeStruct((16, 128), F32),
            jax.ShapeDtypeStruct((16, 128), F32),
        ),
        in_specs=[HBM],
        out_specs=(VMEM, VMEM, VMEM, VMEM),
        scratch_shapes=[
            pltpu.VMEM((PLACES, ROWS, 128), F32),
            pltpu.SemaphoreType.DMA((PLACES,)),
        ],
        compiler_params=params(20),
        name="basis_products",
    )(in_hbm(basis))


def image_kernel(
    sizes_ref, field_ref, low_ref, high_ref, late_ref, keep_ref, got_ref, parts_in_ref,
    parts_ref, copies_ref,
):
    sizes = [sizes_ref[step] for step in range(STEPS)]
    first = (lax.axis_index("y") == 0) & (lax.axis_index("core") == 0)
    start = jnp.full((COLS, 128), first.astype(jnp.int32)) == 1
    weights = []
    for step in range(STEPS):
        if step == 0:
            before = jnp.where(start, sizes[0], late_ref[2 * PLANES * LINES])
        else:
            before = sizes[step - 1]
        ratio = sizes[step] / before
        now = (1.0 + 2.0 * ratio) / (1.0 + ratio)
        one = 1.0 + ratio
        two = ratio * ratio / (1.0 + ratio)
        if step == 0:
            now = jnp.where(start, 1.0, now)
            one = jnp.where(start, 1.0, one)
            two = jnp.where(start, 0.0, two)
        weights.append((now, one, two, 0.5 * sizes[step]))
    lane = lax.broadcasted_iota(jnp.int32, (COLS, 128), 1)
    base = PARTS * ROWS

    def at(step, plane, line):
        if step < 0:
            return late_ref[place_of(step + 2, plane, line)]
        return field_ref[place_of(step, plane, line)]

    for step in range(STEPS):
        now, one, two, kappa = weights[step]
        for plane in range(PLANES):
            for line in range(LINES):
                value = at(step, plane, line)
                side = step * LINES + line
                beside = low_ref[side] if plane == 0 else at(step, plane - 1, line)
                beside += high_ref[side] if plane == PLANES - 1 else at(step, plane + 1, line)
                if line > 0:
                    beside += at(step, plane, line - 1)
                if line < LINES - 1:
                    beside += at(step, plane, line + 1)
                beside += jnp.where(lane < 127, pltpu.roll(value, 127, 1), 0.0)
                beside += jnp.where(lane > 0, pltpu.roll(value, 1, 1), 0.0)
                result = (
                    now * value
                    - one * at(step - 1, plane, line)
                    + two * at(step - 2, plane, line)
                    + kappa * (6.0 * value - beside)
                )
                place = place_of(step, plane, line)
                for part, piece in enumerate(split(result)):
                    parts_ref[
                        base + part * COLS : base + (part + 1) * COLS, place * 128 : (place + 1) * 128
                    ] = piece
    own_parts = parts_ref[base:]
    products = lax.dot_general(own_parts, parts_ref[...], NT, preferred_element_type=F32)
    proj = part_products(products, COLS, 0, ROWS)
    gram = part_products(products, COLS, base, COLS)
    packed = jnp.concatenate([proj[:8], proj[8:]], axis=1)
    pieces = []
    for half in range(2):
        lines = [gram[half * 8 + row : half * 8 + row + 1] for row in range(8)]
        pieces.append(jnp.concatenate(lines, axis=1))
    chip = keep_ref[...] + got_ref[...]
    last = jnp.concatenate(pieces + [chip[8:10]], axis=0)
    for copy in range(SLABS):
        copies_ref[copy, 0] = packed[:4]
        copies_ref[copy, 1] = packed[4:]
        copies_ref[copy, 2] = chip[0:4]
        copies_ref[copy, 3] = chip[4:8]
        copies_ref[copy, 4] = last


def image_products(sizes, field, low, high, late, keep, got, parts):
    return pl.pallas_call(
        image_kernel,
        out_shape=(
            jax.ShapeDtypeStruct((PARTS * FULL, CELLS), BF16),
            jax.ShapeDtypeStruct((SLABS, 5, 4, 128), F32),
        ),
        in_specs=[VMEM] * 8,
        out_specs=(VMEM, VMEM),
        input_output_aliases={7: 0},
        compiler_params=params(20),
        name="image_products",
    )(sizes, field, low, high, late, keep, got, parts)


def finish_kernel(sums_ref, parts_ref, hess_ref, triangle_ref, next_hbm, next_ref, sems):
    cores = []
    for core in range(2):
        total = sums_ref[core]
        for piece in range(core + 2, GROUPS, 2):
            total = total + sums_ref[piece]
        cores.append(total * (1.0 / TOTAL))
    sums = cores[0] + cores[1]
    proj = jnp.concatenate(
        [sums[0, :, :ROWS], sums[1, :, :ROWS], sums[0, :, ROWS:], sums[1, :, ROWS:]], axis=0
    )
    image_gram = jnp.concatenate(
        [
            sums[4, half : half + 1, line * COLS : (line + 1) * COLS]
            for half in range(2)
            for line in range(8)
        ],
        axis=0,
    )
    packed = jnp.concatenate([cores[0][2], cores[0][3], cores[1][2], cores[1][3]], axis=0)
    rest = jnp.concatenate(
        [cores[core][4, 2:4, 32 * i : 32 * i + 32] for core in range(2) for i in range(4)], axis=0
    )
    kept = [packed[:, :64], packed[:, 64:112], rest, packed[:, 112:]]
    upper = []
    for block in range(BLOCKS):
        pieces = [0.5 * kept[block][:, :COLS]]
        if block:
            pieces.insert(0, jnp.zeros((COLS, block * COLS), F32))
        if block < BLOCKS - 1:
            pieces.append(kept[block][:, COLS:])
        upper.append(jnp.concatenate(pieces, axis=1))
    half = jnp.concatenate(upper, axis=0)
    carried = lax.dot_general(proj, half, NN, precision=HIGHEST, preferred_element_type=F32) - proj
    cross = lax.dot_general(carried, proj, NT, precision=HIGHEST, preferred_element_type=F32)
    cross_t = lax.dot_general(proj, carried, NT, precision=HIGHEST, preferred_element_type=F32)
    gram = image_gram + (cross + cross_t)
    row = lax.broadcasted_iota(jnp.int32, (COLS, COLS), 0)
    col = lax.broadcasted_iota(jnp.int32, (COLS, COLS), 1)
    eye = jnp.where(row == col, 1.0, 0.0).astype(F32)
    work = jnp.concatenate(
        [gram, -proj, eye, jnp.zeros((COLS, 128 - FULL - COLS), F32)], axis=1
    )
    wide_row = lax.broadcasted_iota(jnp.int32, (COLS, 128), 0)
    scale = jnp.zeros((COLS, 128), F32)
    for step in range(COLS):
        column = jnp.broadcast_to(work[:, step : step + 1], (COLS, 128))
        pivot = jnp.broadcast_to(column[step : step + 1], (COLS, 128))
        pivot_row = jnp.broadcast_to(work[step : step + 1], (COLS, 128))
        work = work - jnp.where(wide_row > step, column / pivot, 0.0) * pivot_row
        scale = jnp.where(wide_row == step, lax.rsqrt(pivot), scale)
    work = work * scale
    hess_ref[...] = proj.T
    triangle_ref[...] = jnp.where(row <= col, work[:, :COLS], 0.0)
    factors = split(work[:, COLS : COLS + FULL])
    stacked = []
    for part in range(PARTS):
        pieces = []
        for piece in (factors[part][:, :ROWS], factors[part][:, ROWS:]):
            for other in range(PARTS):
                pieces.append(piece if other < PARTS - part else jnp.zeros_like(piece))
        stacked.append(jnp.concatenate(pieces, axis=1))
    factor = jnp.concatenate(stacked, axis=0)
    copies = []
    for tile in range(PLACES // 8):
        lanes = slice(tile * 1024, (tile + 1) * 1024)
        product = lax.dot_general(factor, parts_ref[:, lanes], NN, preferred_element_type=F32)
        value = product[:COLS] + (product[COLS : 2 * COLS] + product[2 * COLS :])
        for line in range(8):
            place = tile * 8 + line
            next_ref[place] = value[:, line * 128 : (line + 1) * 128]
            copies.append(
                pltpu.make_async_copy(next_ref.at[place], next_hbm.at[:, place, 0], sems.at[place])
            )
            copies[-1].start()
    for copy in copies:
        copy.wait()


def finish(sums, parts):
    return pl.pallas_call(
        finish_kernel,
        out_shape=(
            jax.ShapeDtypeStruct((ROWS, COLS), F32),
            jax.ShapeDtypeStruct((COLS, COLS), F32),
            jax.ShapeDtypeStruct((COLS, PLACES, 1, 128), F32),
        ),
        in_specs=[VMEM, VMEM],
        out_specs=(VMEM, VMEM, HBM),
        scratch_shapes=[
            pltpu.VMEM((PLACES, COLS, 128), F32),
            pltpu.SemaphoreType.DMA((PLACES,)),
        ],
        compiler_params=params(20),
        name="finish",
    )(sums, parts)


def exchanged(copies, axes):
    return lax.all_to_all(copies, axes, 0, 0)


def per_device(basis, num, den):
    slabs = size_of(SPACE)
    groups = size_of(TM)
    above = [(i, i + 1) for i in range(slabs - 1)]
    below = [(i + 1, i) for i in range(slabs - 1)]
    later = [(i, i + 1) for i in range(groups - 1)]
    flat = basis.reshape(ROWS, PLACES, 1, 128)
    up, down = faces(flat)
    low = lax.ppermute(up, SPACE, above)
    high = lax.ppermute(down, SPACE, below)
    late, sizes = ending(num, den, flat, up)
    late = lax.ppermute(late, TM, later)
    parts, field, keep, give = basis_products(flat)
    got = lax.ppermute(give, "core", [(0, 1), (1, 0)])
    parts, copies = image_products(sizes, field, low, high, late, keep, got, parts)
    sums = exchanged(copies, SPACE).sum(0)
    sums = exchanged(jnp.broadcast_to(sums, (groups,) + sums.shape), TM)
    hess, triangle, following = finish(sums, parts)
    return (
        hess.reshape(BLOCKS, COLS, COLS),
        triangle,
        following.reshape(COLS, STEPS, PLANES, LINES, 128),
    )


def solution(mesh):
    fine = Mesh(mesh.devices.reshape(8, 2, 4, 8), ("y", "core", "x", "z"))
    placed = (P(None, None, TM, SPACE, None, None), P(TM), P(TM))
    return jax.shard_map(
        per_device,
        mesh=fine,
        in_specs=placed,
        out_specs=(P(), P(), P(None, TM, SPACE, None, None)),
        check_vma=False,
    )
```

```python
import jax
import jax.numpy as jnp
from jax import lax
from jax.experimental import pallas as pl
from jax.experimental.pallas import tpu as pltpu
from jax.sharding import Mesh, PartitionSpec as P

TM = ("y", "core")
SPACE = ("x", "z")
GROUPS = 16
SLABS = 32
COLS = 16
BLOCKS = 4
ROWS = BLOCKS * COLS
FULL = ROWS + COLS
STEPS = 4
PLANES = 2
LINES = 8
PLACES = STEPS * PLANES * LINES
CELLS = PLACES * 128
TOTAL = 64 * 64 * 8 * 128
PARTS = 3
CHUNKS = 1
HIGHEST = lax.Precision.HIGHEST
F32 = jnp.float32
BF16 = jnp.bfloat16
NT = (((1,), (1,)), ((), ()))
NN = (((1,), (0,)), ((), ()))
VMEM = pl.BlockSpec(memory_space=pltpu.VMEM)
HBM = pl.BlockSpec(memory_space=pltpu.HBM)


def params(megabytes):
    return pltpu.CompilerParams(vmem_limit_bytes=megabytes * 1024 * 1024)


def in_hbm(array):
    return pltpu.with_memory_space_constraint(array, pltpu.HBM)


def size_of(axes):
    count = 1
    for axis in axes:
        count *= lax.axis_size(axis)
    return count


def place_of(step, plane, line):
    return (step * PLANES + plane) * LINES + line


def split(value):
    first = value.astype(BF16)
    rest = value - first.astype(F32)
    second = rest.astype(BF16)
    third = (rest - second.astype(F32)).astype(BF16)
    return first, second, third


def edges_kernel(
    num_hbm, den_hbm, basis_hbm, up_ref, down_ref, late_ref, sizes_ref, num_ref, den_ref, sems
):
    last = BLOCKS - 1
    counts = [
        pltpu.make_async_copy(num_hbm, num_ref, sems.at[3]),
        pltpu.make_async_copy(den_hbm, den_ref, sems.at[4]),
    ]
    copies = [
        pltpu.make_async_copy(basis_hbm.at[last, :, :, PLANES - 1], up_ref, sems.at[0]),
        pltpu.make_async_copy(basis_hbm.at[last, :, :, 0], down_ref, sems.at[1]),
        pltpu.make_async_copy(
            basis_hbm.at[last, :, pl.ds(STEPS - 2, 2)], late_ref.at[pl.ds(0, COLS)], sems.at[2]
        ),
    ]
    for copy in copies + counts:
        copy.start()
    for copy in counts:
        copy.wait()
    for step in range(STEPS):
        top = jnp.full((COLS, 128), num_ref[step]).astype(F32)
        bottom = jnp.full((COLS, 128), den_ref[step]).astype(F32)
        sizes_ref[step] = top / bottom
    for step in range(2):
        for plane in range(PLANES):
            late_ref[COLS, step, plane] = sizes_ref[STEPS - 1, :LINES]
    for copy in copies:
        copy.wait()


def edges(num, den, basis):
    face = jax.ShapeDtypeStruct((COLS, STEPS, LINES, 128), F32)
    return pl.pallas_call(
        edges_kernel,
        out_shape=(
            face,
            face,
            jax.ShapeDtypeStruct((COLS + 1, 2, PLANES, LINES, 128), F32),
            jax.ShapeDtypeStruct((STEPS, COLS, 128), F32),
        ),
        in_specs=[HBM, HBM, HBM],
        out_specs=(VMEM, VMEM, VMEM, VMEM),
        scratch_shapes=[
            pltpu.SMEM((STEPS,), jnp.int32),
            pltpu.SMEM((STEPS,), jnp.int32),
            pltpu.SemaphoreType.DMA((5,)),
        ],
        compiler_params=params(4),
        name="edges",
    )(in_hbm(num), in_hbm(den), in_hbm(basis))


def part_products(products, count, offset, width):
    total = None
    for b in range(PARTS):
        group = None
        for a in range(PARTS - b):
            piece = products[a * count : (a + 1) * count, offset + b * width : offset + (b + 1) * width]
            group = piece if group is None else group + piece
        total = group if total is None else total + group
    return total


def basis_kernel(basis_hbm, parts_ref, last_ref, keep_ref, give_ref, field_ref, sems):
    copies = [
        pltpu.make_async_copy(basis_hbm.at[:, place, 0], field_ref.at[place], sems.at[place])
        for place in range(PLACES)
    ]
    for copy in copies:
        copy.start()
    products = None
    per_chunk = PLACES // CHUNKS
    for chunk in range(CHUNKS):
        for place in range(chunk * per_chunk, (chunk + 1) * per_chunk):
            copies[place].wait()
            value = field_ref[place]
            last_ref[place] = value[ROWS - COLS :]
            for part, piece in enumerate(split(value)):
                parts_ref[part * ROWS : (part + 1) * ROWS, place * 128 : (place + 1) * 128] = piece
        lanes = slice(chunk * per_chunk * 128, (chunk + 1) * per_chunk * 128)
        piece = parts_ref[: PARTS * ROWS, lanes]
        product = lax.dot_general(piece, piece, NT, preferred_element_type=F32)
        products = product if products is None else products + product
    gram = part_products(products, ROWS, 0, ROWS)
    rows = [gram[block * COLS : (block + 1) * COLS, block * COLS :] for block in range(BLOCKS)]
    packed = jnp.concatenate([rows[0], rows[1], rows[3]], axis=1)
    halves = []
    for half in range(2):
        rest = rows[2][half * 8 : half * 8 + 8]
        rest = jnp.concatenate([rest[2 * i : 2 * i + 2] for i in range(4)], axis=1)
        halves.append((packed[half * 8 : half * 8 + 8], rest))
    own = lax.axis_index("core")
    first = jnp.full((8, 128), own) == 0
    for target, flip in ((keep_ref, False), (give_ref, True)):
        one, two = (halves[1], halves[0]) if flip else (halves[0], halves[1])
        target[0:8] = jnp.where(first, one[0], two[0])
        target[8:10] = jnp.where(first[:2], one[1], two[1])
        target[10:16] = jnp.zeros((6, 128), F32)


def basis_products(basis):
    return pl.pallas_call(
        basis_kernel,
        out_shape=(
            jax.ShapeDtypeStruct((PARTS * FULL, CELLS), BF16),
            jax.ShapeDtypeStruct((PLACES, COLS, 128), F32),
            jax.ShapeDtypeStruct((16, 128), F32),
            jax.ShapeDtypeStruct((16, 128), F32),
        ),
        in_specs=[HBM],
        out_specs=(VMEM, VMEM, VMEM, VMEM),
        scratch_shapes=[
            pltpu.VMEM((PLACES, ROWS, 128), F32),
            pltpu.SemaphoreType.DMA((PLACES,)),
        ],
        compiler_params=params(20),
        name="basis_products",
    )(in_hbm(basis))


def image_kernel(
    sizes_ref, field_ref, low_ref, high_ref, late_ref, keep_ref, got_ref, parts_in_ref,
    parts_ref, copies_ref,
):
    side_rows = 2 * PLANES * LINES
    sizes = [sizes_ref[step] for step in range(STEPS)]
    first = (lax.axis_index("y") == 0) & (lax.axis_index("core") == 0)
    start = jnp.full((COLS, 128), first.astype(jnp.int32)) == 1
    weights = []
    for step in range(STEPS):
        if step == 0:
            before = late_ref[pl.ds(COLS * side_rows, LINES), :]
            before = jnp.where(start, sizes[0], jnp.concatenate([before, before], axis=0))
        else:
            before = sizes[step - 1]
        ratio = sizes[step] / before
        now = (1.0 + 2.0 * ratio) / (1.0 + ratio)
        one = 1.0 + ratio
        two = ratio * ratio / (1.0 + ratio)
        if step == 0:
            now = jnp.where(start, 1.0, now)
            one = jnp.where(start, 1.0, one)
            two = jnp.where(start, 0.0, two)
        weights.append((now, one, two, 0.5 * sizes[step]))
    lane = lax.broadcasted_iota(jnp.int32, (COLS, 128), 1)
    base = PARTS * ROWS

    def turned(ref, place):
        return ref[pl.ds(place, COLS, stride=side_rows), :]

    past = [turned(late_ref, place) for place in range(side_rows)]

    def at(step, plane, line):
        if step < 0:
            return past[place_of(step + 2, plane, line)]
        return field_ref[place_of(step, plane, line)]

    for step in range(STEPS):
        now, one, two, kappa = weights[step]
        for plane in range(PLANES):
            for line in range(LINES):
                value = at(step, plane, line)
                side = step * LINES + line
                beside = turned(low_ref, side) if plane == 0 else at(step, plane - 1, line)
                beside += turned(high_ref, side) if plane == PLANES - 1 else at(step, plane + 1, line)
                if line > 0:
                    beside += at(step, plane, line - 1)
                if line < LINES - 1:
                    beside += at(step, plane, line + 1)
                beside += jnp.where(lane < 127, pltpu.roll(value, 127, 1), 0.0)
                beside += jnp.where(lane > 0, pltpu.roll(value, 1, 1), 0.0)
                result = (
                    now * value
                    - one * at(step - 1, plane, line)
                    + two * at(step - 2, plane, line)
                    + kappa * (6.0 * value - beside)
                )
                place = place_of(step, plane, line)
                for part, piece in enumerate(split(result)):
                    parts_ref[
                        base + part * COLS : base + (part + 1) * COLS, place * 128 : (place + 1) * 128
                    ] = piece
    own_parts = parts_ref[base:]
    products = lax.dot_general(own_parts, parts_ref[...], NT, preferred_element_type=F32)
    proj = part_products(products, COLS, 0, ROWS)
    gram = part_products(products, COLS, base, COLS)
    packed = jnp.concatenate([proj[:8], proj[8:]], axis=1)
    pieces = []
    for half in range(2):
        lines = [gram[half * 8 + row : half * 8 + row + 1] for row in range(8)]
        pieces.append(jnp.concatenate(lines, axis=1))
    chip = keep_ref[...] + got_ref[...]
    last = jnp.concatenate(pieces + [chip[8:10]], axis=0)
    for copy in range(SLABS):
        copies_ref[copy, 0] = packed[:4]
        copies_ref[copy, 1] = packed[4:]
        copies_ref[copy, 2] = chip[0:4]
        copies_ref[copy, 3] = chip[4:8]
        copies_ref[copy, 4] = last


def image_products(sizes, field, low, high, late, keep, got, parts):
    return pl.pallas_call(
        image_kernel,
        out_shape=(
            jax.ShapeDtypeStruct((PARTS * FULL, CELLS), BF16),
            jax.ShapeDtypeStruct((SLABS, 5, 4, 128), F32),
        ),
        in_specs=[VMEM] * 8,
        out_specs=(VMEM, VMEM),
        input_output_aliases={7: 0},
        compiler_params=params(20),
        name="image_products",
    )(sizes, field, low, high, late, keep, got, parts)


def regroup_kernel(sums_ref, copies_ref):
    total = sums_ref[0]
    for piece in range(1, SLABS):
        total = total + sums_ref[piece]
    for copy in range(GROUPS):
        copies_ref[copy] = total


def regroup(sums):
    return pl.pallas_call(
        regroup_kernel,
        out_shape=jax.ShapeDtypeStruct((GROUPS, 5, 4, 128), F32),
        in_specs=[VMEM],
        out_specs=VMEM,
        compiler_params=params(4),
        name="regroup",
    )(sums)


def finish_kernel(sums_ref, parts_ref, hess_ref, triangle_ref, next_ref):
    cores = []
    for core in range(2):
        total = sums_ref[core]
        for piece in range(core + 2, GROUPS, 2):
            total = total + sums_ref[piece]
        cores.append(total * (1.0 / TOTAL))
    sums = cores[0] + cores[1]
    proj = jnp.concatenate(
        [sums[0, :, :ROWS], sums[1, :, :ROWS], sums[0, :, ROWS:], sums[1, :, ROWS:]], axis=0
    )
    image_gram = jnp.concatenate(
        [
            sums[4, half : half + 1, line * COLS : (line + 1) * COLS]
            for half in range(2)
            for line in range(8)
        ],
        axis=0,
    )
    packed = jnp.concatenate([cores[0][2], cores[0][3], cores[1][2], cores[1][3]], axis=0)
    rest = jnp.concatenate(
        [cores[core][4, 2:4, 32 * i : 32 * i + 32] for core in range(2) for i in range(4)], axis=0
    )
    kept = [packed[:, :64], packed[:, 64:112], rest, packed[:, 112:]]
    upper = []
    for block in range(BLOCKS):
        pieces = [0.5 * kept[block][:, :COLS]]
        if block:
            pieces.insert(0, jnp.zeros((COLS, block * COLS), F32))
        if block < BLOCKS - 1:
            pieces.append(kept[block][:, COLS:])
        upper.append(jnp.concatenate(pieces, axis=1))
    half = jnp.concatenate(upper, axis=0)
    carried = lax.dot_general(proj, half, NN, precision=HIGHEST, preferred_element_type=F32) - proj
    cross = lax.dot_general(carried, proj, NT, precision=HIGHEST, preferred_element_type=F32)
    cross_t = lax.dot_general(proj, carried, NT, precision=HIGHEST, preferred_element_type=F32)
    gram = image_gram + (cross + cross_t)
    row = lax.broadcasted_iota(jnp.int32, (COLS, COLS), 0)
    col = lax.broadcasted_iota(jnp.int32, (COLS, COLS), 1)
    eye = jnp.where(row == col, 1.0, 0.0).astype(F32)
    work = jnp.concatenate(
        [gram, -proj, eye, jnp.zeros((COLS, 128 - FULL - COLS), F32)], axis=1
    )
    wide_row = lax.broadcasted_iota(jnp.int32, (COLS, 128), 0)
    columns = [jnp.broadcast_to(gram[:, k : k + 1], (COLS, 128)) for k in range(COLS)]
    scale = jnp.zeros((COLS, 128), F32)
    for step in range(COLS):
        pivot = jnp.broadcast_to(columns[step][step : step + 1], (COLS, 128))
        factor = jnp.where(wide_row > step, columns[step] * (1.0 / pivot), 0.0)
        for k in range(step + 1, COLS):
            columns[k] = columns[k] - factor * columns[k][step : step + 1]
        work = work - factor * work[step : step + 1]
        scale = jnp.where(wide_row == step, lax.rsqrt(pivot), scale)
    work = work * scale
    hess_ref[...] = proj.T
    triangle_ref[...] = jnp.where(row <= col, work[:, :COLS], 0.0)
    factors = split(work[:, COLS : COLS + FULL])
    stacked = []
    for part in range(PARTS):
        pieces = []
        for piece in (factors[part][:, :ROWS], factors[part][:, ROWS:]):
            for other in range(PARTS):
                pieces.append(piece if other < PARTS - part else jnp.zeros_like(piece))
        stacked.append(jnp.concatenate(pieces, axis=1))
    factor = jnp.concatenate(stacked, axis=0)
    for tile in range(PLACES // 8):
        lanes = slice(tile * 1024, (tile + 1) * 1024)
        product = lax.dot_general(factor, parts_ref[:, lanes], NN, preferred_element_type=F32)
        value = product[:COLS] + (product[COLS : 2 * COLS] + product[2 * COLS :])
        for line in range(8):
            next_ref[pl.ds(tile * 8 + line, COLS, stride=PLACES), :] = value[
                :, line * 128 : (line + 1) * 128
            ]


def finish(sums, parts):
    return pl.pallas_call(
        finish_kernel,
        out_shape=(
            jax.ShapeDtypeStruct((ROWS, COLS), F32),
            jax.ShapeDtypeStruct((COLS, COLS), F32),
            jax.ShapeDtypeStruct((COLS * PLACES, 128), F32),
        ),
        in_specs=[VMEM, VMEM],
        out_specs=(VMEM, VMEM, VMEM),
        compiler_params=params(20),
        name="finish",
    )(sums, parts)


def exchanged(copies, axes):
    return lax.all_to_all(copies, axes, 0, 0)


def per_device(basis, num, den):
    slabs = size_of(SPACE)
    groups = size_of(TM)
    above = [(i, i + 1) for i in range(slabs - 1)]
    below = [(i + 1, i) for i in range(slabs - 1)]
    later = [(i, i + 1) for i in range(groups - 1)]
    flat = basis.reshape(ROWS, PLACES, 1, 128)
    up, down, late, sizes = edges(num, den, basis)
    low = lax.ppermute(up, SPACE, above).reshape(-1, 128)
    high = lax.ppermute(down, SPACE, below).reshape(-1, 128)
    late = lax.ppermute(late, TM, later).reshape(-1, 128)
    parts, field, keep, give = basis_products(flat)
    got = lax.ppermute(give, "core", [(0, 1), (1, 0)])
    parts, copies = image_products(sizes, field, low, high, late, keep, got, parts)
    sums = exchanged(regroup(exchanged(copies, SPACE)), TM)
    hess, triangle, following = finish(sums, parts)
    return (
        hess.reshape(BLOCKS, COLS, COLS),
        triangle,
        following.reshape(COLS, STEPS, PLANES, LINES, 128),
    )


def solution(mesh):
    fine = Mesh(mesh.devices.reshape(8, 2, 4, 8), ("y", "core", "x", "z"))
    placed = (P(None, None, TM, SPACE, None, None), P(TM), P(TM))
    return jax.shard_map(
        per_device,
        mesh=fine,
        in_specs=placed,
        out_specs=(P(), P(), P(None, TM, SPACE, None, None)),
        check_vma=False,
    )
```

```python
import jax
import jax.numpy as jnp
from jax import lax
from jax.experimental import pallas as pl
from jax.experimental.pallas import tpu as pltpu
from jax.sharding import Mesh, PartitionSpec as P

TM = ("y", "core")
SPACE = ("x", "z")
GROUPS = 16
SLABS = 32
COLS = 16
BLOCKS = 4
ROWS = BLOCKS * COLS
FULL = ROWS + COLS
STEPS = 4
PLANES = 2
LINES = 8
PLACES = STEPS * PLANES * LINES
CELLS = PLACES * 128
TOTAL = 64 * 64 * 8 * 128
PARTS = 3
HIGHEST = lax.Precision.HIGHEST
F32 = jnp.float32
BF16 = jnp.bfloat16
NT = (((1,), (1,)), ((), ()))
NN = (((1,), (0,)), ((), ()))
VMEM = pl.BlockSpec(memory_space=pltpu.VMEM)
HBM = pl.BlockSpec(memory_space=pltpu.HBM)


def params(megabytes):
    return pltpu.CompilerParams(vmem_limit_bytes=megabytes * 1024 * 1024)


def in_hbm(array):
    return pltpu.with_memory_space_constraint(array, pltpu.HBM)


def size_of(axes):
    count = 1
    for axis in axes:
        count *= lax.axis_size(axis)
    return count


def place_of(step, plane, line):
    return (step * PLANES + plane) * LINES + line


def split(value):
    first = value.astype(BF16)
    rest = value - first.astype(F32)
    second = rest.astype(BF16)
    third = (rest - second.astype(F32)).astype(BF16)
    return first, second, third


def edges_kernel(
    num_hbm, den_hbm, basis_hbm, up_ref, down_ref, one_ref, two_ref, sizes_ref, num_ref, den_ref, sems
):
    last = BLOCKS - 1
    counts = [
        pltpu.make_async_copy(num_hbm, num_ref, sems.at[4]),
        pltpu.make_async_copy(den_hbm, den_ref, sems.at[5]),
    ]
    copies = [
        pltpu.make_async_copy(basis_hbm.at[last, :, :, PLANES - 1], up_ref, sems.at[0]),
        pltpu.make_async_copy(basis_hbm.at[last, :, :, 0], down_ref, sems.at[1]),
        pltpu.make_async_copy(
            basis_hbm.at[last, :, STEPS - 1], one_ref.at[pl.ds(0, COLS)], sems.at[2]
        ),
        pltpu.make_async_copy(basis_hbm.at[last, :, STEPS - 2], two_ref, sems.at[3]),
    ]
    for copy in copies + counts:
        copy.start()
    for copy in counts:
        copy.wait()
    for step in range(STEPS):
        top = jnp.full((COLS, 128), num_ref[step]).astype(F32)
        bottom = jnp.full((COLS, 128), den_ref[step]).astype(F32)
        sizes_ref[step] = top / bottom
    for plane in range(PLANES):
        one_ref[COLS, plane] = sizes_ref[STEPS - 1, :LINES]
    for copy in copies:
        copy.wait()


def edges(num, den, basis):
    face = jax.ShapeDtypeStruct((COLS, STEPS, LINES, 128), F32)
    return pl.pallas_call(
        edges_kernel,
        out_shape=(
            face,
            face,
            jax.ShapeDtypeStruct((COLS + 1, PLANES, LINES, 128), F32),
            jax.ShapeDtypeStruct((COLS, PLANES, LINES, 128), F32),
            jax.ShapeDtypeStruct((STEPS, COLS, 128), F32),
        ),
        in_specs=[HBM, HBM, HBM],
        out_specs=(VMEM,) * 5,
        scratch_shapes=[
            pltpu.SMEM((STEPS,), jnp.int32),
            pltpu.SMEM((STEPS,), jnp.int32),
            pltpu.SemaphoreType.DMA((6,)),
        ],
        compiler_params=params(4),
        name="edges",
    )(in_hbm(num), in_hbm(den), in_hbm(basis))


def part_products(products, count, offset, width):
    total = None
    for b in range(PARTS):
        group = None
        for a in range(PARTS - b):
            piece = products[a * count : (a + 1) * count, offset + b * width : offset + (b + 1) * width]
            group = piece if group is None else group + piece
        total = group if total is None else total + group
    return total


def basis_kernel(basis_hbm, parts_ref, last_ref, keep_ref, give_ref, field_ref, sems):
    copies = [
        pltpu.make_async_copy(basis_hbm.at[:, place, 0], field_ref.at[place], sems.at[place])
        for place in range(PLACES)
    ]
    for copy in copies:
        copy.start()
    for place in range(PLACES):
        copies[place].wait()
        value = field_ref[place]
        last_ref[place] = value[ROWS - COLS :]
        for part, piece in enumerate(split(value)):
            parts_ref[part * ROWS : (part + 1) * ROWS, place * 128 : (place + 1) * 128] = piece
    products = lax.dot_general(
        parts_ref[: 2 * ROWS], parts_ref[: PARTS * ROWS], NT, preferred_element_type=F32
    )

    def pair(a, b):
        return products[a * ROWS : (a + 1) * ROWS, b * ROWS : (b + 1) * ROWS]

    gram = pair(0, 0) + ((pair(0, 1) + pair(1, 0)) + (pair(1, 1) + (pair(0, 2) + pair(0, 2).T)))
    rows = [gram[block * COLS : (block + 1) * COLS, block * COLS :] for block in range(BLOCKS)]
    packed = jnp.concatenate([rows[0], rows[1], rows[3]], axis=1)
    halves = []
    for half in range(2):
        rest = rows[2][half * 8 : half * 8 + 8]
        rest = jnp.concatenate([rest[2 * i : 2 * i + 2] for i in range(4)], axis=1)
        halves.append((packed[half * 8 : half * 8 + 8], rest))
    own = lax.axis_index("core")
    first = jnp.full((8, 128), own) == 0
    for target, flip in ((keep_ref, False), (give_ref, True)):
        one, two = (halves[1], halves[0]) if flip else (halves[0], halves[1])
        target[0:8] = jnp.where(first, one[0], two[0])
        target[8:10] = jnp.where(first[:2], one[1], two[1])
        target[10:16] = jnp.zeros((6, 128), F32)


def basis_products(basis):
    return pl.pallas_call(
        basis_kernel,
        out_shape=(
            jax.ShapeDtypeStruct((PARTS * FULL, CELLS), BF16),
            jax.ShapeDtypeStruct((PLACES, COLS, 128), F32),
            jax.ShapeDtypeStruct((16, 128), F32),
            jax.ShapeDtypeStruct((16, 128), F32),
        ),
        in_specs=[HBM],
        out_specs=(VMEM, VMEM, VMEM, VMEM),
        scratch_shapes=[
            pltpu.VMEM((PLACES, ROWS, 128), F32),
            pltpu.SemaphoreType.DMA((PLACES,)),
        ],
        compiler_params=params(20),
        name="basis_products",
    )(in_hbm(basis))


def image_kernel(
    sizes_ref, field_ref, low_ref, high_ref, one_ref, two_ref, keep_ref, got_ref, parts_in_ref,
    parts_ref, copies_ref,
):
    sizes = [sizes_ref[step] for step in range(STEPS)]
    first = (lax.axis_index("y") == 0) & (lax.axis_index("core") == 0)
    start = jnp.full((COLS, 128), first.astype(jnp.int32)) == 1
    weights = []
    for step in range(STEPS):
        if step == 0:
            before = one_ref[pl.ds(COLS * PLANES * LINES, LINES), :]
            before = jnp.where(start, sizes[0], jnp.concatenate([before, before], axis=0))
        else:
            before = sizes[step - 1]
        ratio = sizes[step] / before
        now = (1.0 + 2.0 * ratio) / (1.0 + ratio)
        one = 1.0 + ratio
        two = ratio * ratio / (1.0 + ratio)
        if step == 0:
            now = jnp.where(start, 1.0, now)
            one = jnp.where(start, 1.0, one)
            two = jnp.where(start, 0.0, two)
        weights.append((now, one, two, 0.5 * sizes[step]))
    lane = lax.broadcasted_iota(jnp.int32, (COLS, 128), 1)
    base = PARTS * ROWS

    def turned(ref, place):
        return ref[pl.ds(place, COLS, stride=ref.shape[0] // COLS), :]

    past = {}
    for plane in range(PLANES):
        for line in range(LINES):
            place = plane * LINES + line
            past[-1, plane, line] = one_ref[pl.ds(place, COLS, stride=PLANES * LINES), :]
            past[-2, plane, line] = turned(two_ref, place)

    def at(step, plane, line):
        if step < 0:
            return past[step, plane, line]
        return field_ref[place_of(step, plane, line)]

    for step in range(STEPS):
        now, one, two, kappa = weights[step]
        for plane in range(PLANES):
            for line in range(LINES):
                value = at(step, plane, line)
                side = step * LINES + line
                beside = turned(low_ref, side) if plane == 0 else at(step, plane - 1, line)
                beside += turned(high_ref, side) if plane == PLANES - 1 else at(step, plane + 1, line)
                if line > 0:
                    beside += at(step, plane, line - 1)
                if line < LINES - 1:
                    beside += at(step, plane, line + 1)
                beside += jnp.where(lane < 127, pltpu.roll(value, 127, 1), 0.0)
                beside += jnp.where(lane > 0, pltpu.roll(value, 1, 1), 0.0)
                result = (
                    now * value
                    - one * at(step - 1, plane, line)
                    + two * at(step - 2, plane, line)
                    + kappa * (6.0 * value - beside)
                )
                place = place_of(step, plane, line)
                for part, piece in enumerate(split(result)):
                    parts_ref[
                        base + part * COLS : base + (part + 1) * COLS, place * 128 : (place + 1) * 128
                    ] = piece
    own_parts = parts_ref[base:]
    products = lax.dot_general(own_parts, parts_ref[...], NT, preferred_element_type=F32)
    proj = part_products(products, COLS, 0, ROWS)
    gram = part_products(products, COLS, base, COLS)
    packed = jnp.concatenate([proj[:8], proj[8:]], axis=1)
    pieces = []
    for half in range(2):
        lines = [gram[half * 8 + row : half * 8 + row + 1] for row in range(8)]
        pieces.append(jnp.concatenate(lines, axis=1))
    chip = keep_ref[...] + got_ref[...]
    last = jnp.concatenate(pieces + [chip[8:10]], axis=0)
    for copy in range(SLABS):
        copies_ref[copy, 0] = packed[:4]
        copies_ref[copy, 1] = packed[4:]
        copies_ref[copy, 2] = chip[0:4]
        copies_ref[copy, 3] = chip[4:8]
        copies_ref[copy, 4] = last


def image_products(sizes, field, low, high, one, two, keep, got, parts):
    return pl.pallas_call(
        image_kernel,
        out_shape=(
            jax.ShapeDtypeStruct((PARTS * FULL, CELLS), BF16),
            jax.ShapeDtypeStruct((SLABS, 5, 4, 128), F32),
        ),
        in_specs=[VMEM] * 9,
        out_specs=(VMEM, VMEM),
        input_output_aliases={8: 0},
        compiler_params=params(20),
        name="image_products",
    )(sizes, field, low, high, one, two, keep, got, parts)


def regroup_kernel(sums_ref, copies_ref):
    total = sums_ref[0]
    for piece in range(1, SLABS):
        total = total + sums_ref[piece]
    for copy in range(GROUPS):
        copies_ref[copy] = total


def regroup(sums):
    return pl.pallas_call(
        regroup_kernel,
        out_shape=jax.ShapeDtypeStruct((GROUPS, 5, 4, 128), F32),
        in_specs=[VMEM],
        out_specs=VMEM,
        compiler_params=params(4),
        name="regroup",
    )(sums)


def finish_kernel(sums_ref, parts_ref, hess_ref, triangle_ref, next_ref):
    cores = []
    for core in range(2):
        total = sums_ref[core]
        for piece in range(core + 2, GROUPS, 2):
            total = total + sums_ref[piece]
        cores.append(total * (1.0 / TOTAL))
    sums = cores[0] + cores[1]
    proj = jnp.concatenate(
        [sums[0, :, :ROWS], sums[1, :, :ROWS], sums[0, :, ROWS:], sums[1, :, ROWS:]], axis=0
    )
    image_gram = jnp.concatenate(
        [
            sums[4, half : half + 1, line * COLS : (line + 1) * COLS]
            for half in range(2)
            for line in range(8)
        ],
        axis=0,
    )
    packed = jnp.concatenate([cores[0][2], cores[0][3], cores[1][2], cores[1][3]], axis=0)
    rest = jnp.concatenate(
        [cores[core][4, 2:4, 32 * i : 32 * i + 32] for core in range(2) for i in range(4)], axis=0
    )
    kept = [packed[:, :64], packed[:, 64:112], rest, packed[:, 112:]]
    upper = []
    for block in range(BLOCKS):
        pieces = [0.5 * kept[block][:, :COLS]]
        if block:
            pieces.insert(0, jnp.zeros((COLS, block * COLS), F32))
        if block < BLOCKS - 1:
            pieces.append(kept[block][:, COLS:])
        upper.append(jnp.concatenate(pieces, axis=1))
    half = jnp.concatenate(upper, axis=0)
    carried = lax.dot_general(proj, half, NN, precision=HIGHEST, preferred_element_type=F32) - proj
    cross = lax.dot_general(carried, proj, NT, precision=HIGHEST, preferred_element_type=F32)
    cross_t = lax.dot_general(proj, carried, NT, precision=HIGHEST, preferred_element_type=F32)
    gram = image_gram + (cross + cross_t)
    row = lax.broadcasted_iota(jnp.int32, (COLS, COLS), 0)
    col = lax.broadcasted_iota(jnp.int32, (COLS, COLS), 1)
    eye = jnp.where(row == col, 1.0, 0.0).astype(F32)
    work = jnp.concatenate(
        [gram, -proj, eye, jnp.zeros((COLS, 128 - FULL - COLS), F32)], axis=1
    )
    wide_row = lax.broadcasted_iota(jnp.int32, (COLS, 128), 0)
    columns = [jnp.broadcast_to(gram[:, k : k + 1], (COLS, 128)) for k in range(COLS)]
    scale = jnp.zeros((COLS, 128), F32)
    for step in range(COLS):
        pivot = jnp.broadcast_to(columns[step][step : step + 1], (COLS, 128))
        factor = jnp.where(wide_row > step, columns[step] * (1.0 / pivot), 0.0)
        for k in range(step + 1, COLS):
            columns[k] = columns[k] - factor * columns[k][step : step + 1]
        work = work - factor * work[step : step + 1]
        scale = jnp.where(wide_row == step, lax.rsqrt(pivot), scale)
    work = work * scale
    hess_ref[...] = proj.T
    triangle_ref[...] = jnp.where(row <= col, work[:, :COLS], 0.0)
    factors = split(work[:, COLS : COLS + FULL])
    stacked = []
    for part in range(PARTS):
        pieces = []
        for piece in (factors[part][:, :ROWS], factors[part][:, ROWS:]):
            for other in range(PARTS):
                pieces.append(piece if other < PARTS - part else jnp.zeros_like(piece))
        stacked.append(jnp.concatenate(pieces, axis=1))
    factor = jnp.concatenate(stacked, axis=0)
    for tile in range(PLACES // 8):
        lanes = slice(tile * 1024, (tile + 1) * 1024)
        product = lax.dot_general(factor, parts_ref[:, lanes], NN, preferred_element_type=F32)
        value = product[:COLS] + (product[COLS : 2 * COLS] + product[2 * COLS :])
        for line in range(8):
            next_ref[pl.ds(tile * 8 + line, COLS, stride=PLACES), :] = value[
                :, line * 128 : (line + 1) * 128
            ]


def finish(sums, parts):
    return pl.pallas_call(
        finish_kernel,
        out_shape=(
            jax.ShapeDtypeStruct((ROWS, COLS), F32),
            jax.ShapeDtypeStruct((COLS, COLS), F32),
            jax.ShapeDtypeStruct((COLS * PLACES, 128), F32),
        ),
        in_specs=[VMEM, VMEM],
        out_specs=(VMEM, VMEM, VMEM),
        compiler_params=params(20),
        name="finish",
    )(sums, parts)


def exchanged(copies, axes):
    return lax.all_to_all(copies, axes, 0, 0)


def per_device(basis, num, den):
    slabs = size_of(SPACE)
    groups = size_of(TM)
    above = [(i, i + 1) for i in range(slabs - 1)]
    below = [(i + 1, i) for i in range(slabs - 1)]
    later = [(i, i + 1) for i in range(groups - 1)]
    flat = basis.reshape(ROWS, PLACES, 1, 128)
    up, down, one, two, sizes = edges(num, den, basis)
    low = lax.ppermute(up, SPACE, above).reshape(-1, 128)
    high = lax.ppermute(down, SPACE, below).reshape(-1, 128)
    one = lax.ppermute(one, TM, later).reshape(-1, 128)
    two = lax.ppermute(two, TM, later).reshape(-1, 128)
    parts, field, keep, give = basis_products(flat)
    got = lax.ppermute(give, "core", [(0, 1), (1, 0)])
    parts, copies = image_products(sizes, field, low, high, one, two, keep, got, parts)
    sums = exchanged(regroup(exchanged(copies, SPACE)), TM)
    hess, triangle, following = finish(sums, parts)
    return (
        hess.reshape(BLOCKS, COLS, COLS),
        triangle,
        following.reshape(COLS, STEPS, PLANES, LINES, 128),
    )


def solution(mesh):
    fine = Mesh(mesh.devices.reshape(8, 2, 4, 8), ("y", "core", "x", "z"))
    placed = (P(None, None, TM, SPACE, None, None), P(TM), P(TM))
    return jax.shard_map(
        per_device,
        mesh=fine,
        in_specs=placed,
        out_specs=(P(), P(), P(None, TM, SPACE, None, None)),
        check_vma=False,
    )
```

```python
import jax
import jax.numpy as jnp
from jax import lax
from jax.experimental import pallas as pl
from jax.experimental.pallas import tpu as pltpu
from jax.sharding import Mesh, PartitionSpec as P

TM = ("y", "core")
SPACE = ("x", "z")
GROUPS = 16
SLABS = 32
COLS = 16
BLOCKS = 4
ROWS = BLOCKS * COLS
FULL = ROWS + COLS
STEPS = 4
PLANES = 2
LINES = 8
PLACES = STEPS * PLANES * LINES
CELLS = PLACES * 128
SIDE = 2 * PLANES * LINES
TOTAL = 64 * 64 * 8 * 128
PARTS = 3
HIGHEST = lax.Precision.HIGHEST
F32 = jnp.float32
BF16 = jnp.bfloat16
NT = (((1,), (1,)), ((), ()))
NN = (((1,), (0,)), ((), ()))
VMEM = pl.BlockSpec(memory_space=pltpu.VMEM)
HBM = pl.BlockSpec(memory_space=pltpu.HBM)


def params(megabytes):
    return pltpu.CompilerParams(vmem_limit_bytes=megabytes * 1024 * 1024)


def in_hbm(array):
    return pltpu.with_memory_space_constraint(array, pltpu.HBM)


def size_of(axes):
    count = 1
    for axis in axes:
        count *= lax.axis_size(axis)
    return count


def place_of(step, plane, line):
    return (step * PLANES + plane) * LINES + line


def split(value):
    first = value.astype(BF16)
    rest = value - first.astype(F32)
    second = rest.astype(BF16)
    third = (rest - second.astype(F32)).astype(BF16)
    return first, second, third


def edges_kernel(
    num_hbm, den_hbm, basis_hbm, near_ref, far_ref, late_ref, sizes_ref, num_ref, den_ref, sems
):
    last = BLOCKS - 1
    odd = lax.axis_index("z") % 2
    counts = [
        pltpu.make_async_copy(num_hbm, num_ref, sems.at[3]),
        pltpu.make_async_copy(den_hbm, den_ref, sems.at[4]),
    ]
    copies = [
        pltpu.make_async_copy(basis_hbm.at[last, :, :, 1 - odd], near_ref, sems.at[0]),
        pltpu.make_async_copy(basis_hbm.at[last, :, :, odd], far_ref, sems.at[1]),
        pltpu.make_async_copy(
            basis_hbm.at[last, :, pl.ds(STEPS - 2, 2)], late_ref.at[pl.ds(0, COLS)], sems.at[2]
        ),
    ]
    for copy in copies + counts:
        copy.start()
    for copy in counts:
        copy.wait()
    for step in range(STEPS):
        top = jnp.full((COLS, 128), num_ref[step]).astype(F32)
        bottom = jnp.full((COLS, 128), den_ref[step]).astype(F32)
        sizes_ref[step] = top / bottom
    for step in range(2):
        for plane in range(PLANES):
            late_ref[COLS, step, plane] = sizes_ref[STEPS - 1, :LINES]
    for copy in copies:
        copy.wait()


def edges(num, den, basis):
    face = jax.ShapeDtypeStruct((COLS, STEPS, LINES, 128), F32)
    return pl.pallas_call(
        edges_kernel,
        out_shape=(
            face,
            face,
            jax.ShapeDtypeStruct((COLS + 1, 2, PLANES, LINES, 128), F32),
            jax.ShapeDtypeStruct((STEPS, COLS, 128), F32),
        ),
        in_specs=[HBM, HBM, HBM],
        out_specs=(VMEM, VMEM, VMEM, VMEM),
        scratch_shapes=[
            pltpu.SMEM((STEPS,), jnp.int32),
            pltpu.SMEM((STEPS,), jnp.int32),
            pltpu.SemaphoreType.DMA((5,)),
        ],
        compiler_params=params(4),
        name="edges",
    )(in_hbm(num), in_hbm(den), in_hbm(basis))


def part_products(products, count, offset, width):
    total = None
    for b in range(PARTS):
        group = None
        for a in range(PARTS - b):
            piece = products[a * count : (a + 1) * count, offset + b * width : offset + (b + 1) * width]
            group = piece if group is None else group + piece
        total = group if total is None else total + group
    return total


def basis_kernel(basis_hbm, parts_ref, last_ref, keep_ref, give_ref, field_ref, sems):
    copies = [
        pltpu.make_async_copy(basis_hbm.at[:, place, 0], field_ref.at[place], sems.at[place])
        for place in range(PLACES)
    ]
    for copy in copies:
        copy.start()
    for place in range(PLACES):
        copies[place].wait()
        value = field_ref[place]
        last_ref[place] = value[ROWS - COLS :]
        for part, piece in enumerate(split(value)):
            parts_ref[part * ROWS : (part + 1) * ROWS, place * 128 : (place + 1) * 128] = piece
    whole = parts_ref[: PARTS * ROWS]
    products = lax.dot_general(whole, whole, NT, preferred_element_type=F32)
    gram = part_products(products, ROWS, 0, ROWS)
    rows = [gram[block * COLS : (block + 1) * COLS, block * COLS :] for block in range(BLOCKS)]
    packed = jnp.concatenate([rows[0], rows[1], rows[3]], axis=1)
    halves = []
    for half in range(2):
        rest = rows[2][half * 8 : half * 8 + 8]
        rest = jnp.concatenate([rest[2 * i : 2 * i + 2] for i in range(4)], axis=1)
        halves.append((packed[half * 8 : half * 8 + 8], rest))
    own = lax.axis_index("core")
    first = jnp.full((8, 128), own) == 0
    for target, flip in ((keep_ref, False), (give_ref, True)):
        one, two = (halves[1], halves[0]) if flip else (halves[0], halves[1])
        target[0:8] = jnp.where(first, one[0], two[0])
        target[8:10] = jnp.where(first[:2], one[1], two[1])
        target[10:16] = jnp.zeros((6, 128), F32)


def basis_products(basis):
    return pl.pallas_call(
        basis_kernel,
        out_shape=(
            jax.ShapeDtypeStruct((PARTS * FULL, CELLS), BF16),
            jax.ShapeDtypeStruct((PLACES, COLS, 128), F32),
            jax.ShapeDtypeStruct((16, 128), F32),
            jax.ShapeDtypeStruct((16, 128), F32),
        ),
        in_specs=[HBM],
        out_specs=(VMEM, VMEM, VMEM, VMEM),
        scratch_shapes=[
            pltpu.VMEM((PLACES, ROWS, 128), F32),
            pltpu.SemaphoreType.DMA((PLACES,)),
        ],
        compiler_params=params(20),
        name="basis_products",
    )(in_hbm(basis))


def inner_kernel(sizes_ref, field_ref, late_ref, inner_ref):
    sizes = [sizes_ref[step] for step in range(STEPS)]
    first = (lax.axis_index("y") == 0) & (lax.axis_index("core") == 0)
    start = jnp.full((COLS, 128), first.astype(jnp.int32)) == 1
    weights = []
    for step in range(STEPS):
        if step == 0:
            before = late_ref[pl.ds(COLS * SIDE, LINES), :]
            before = jnp.where(start, sizes[0], jnp.concatenate([before, before], axis=0))
        else:
            before = sizes[step - 1]
        ratio = sizes[step] / before
        now = (1.0 + 2.0 * ratio) / (1.0 + ratio)
        one = 1.0 + ratio
        two = ratio * ratio / (1.0 + ratio)
        if step == 0:
            now = jnp.where(start, 1.0, now)
            one = jnp.where(start, 1.0, one)
            two = jnp.where(start, 0.0, two)
        weights.append((now, one, two, 0.5 * sizes[step]))
    lane = lax.broadcasted_iota(jnp.int32, (COLS, 128), 1)

    past = [late_ref[pl.ds(place, COLS, stride=SIDE), :] for place in range(SIDE)]

    def at(step, plane, line):
        if step < 0:
            return past[place_of(step + 2, plane, line)]
        return field_ref[place_of(step, plane, line)]

    for step in range(STEPS):
        now, one, two, kappa = weights[step]
        for plane in range(PLANES):
            for line in range(LINES):
                value = at(step, plane, line)
                beside = at(step, PLANES - 1 - plane, line)
                if line > 0:
                    beside += at(step, plane, line - 1)
                if line < LINES - 1:
                    beside += at(step, plane, line + 1)
                beside += jnp.where(lane < 127, pltpu.roll(value, 127, 1), 0.0)
                beside += jnp.where(lane > 0, pltpu.roll(value, 1, 1), 0.0)
                result = (
                    now * value
                    - one * at(step - 1, plane, line)
                    + two * at(step - 2, plane, line)
                    + kappa * (6.0 * value - beside)
                )
                inner_ref[place_of(step, plane, line)] = result


def inner(sizes, field, late):
    return pl.pallas_call(
        inner_kernel,
        out_shape=jax.ShapeDtypeStruct((PLACES, COLS, 128), F32),
        in_specs=[VMEM] * 3,
        out_specs=VMEM,
        compiler_params=params(8),
        name="inner",
    )(sizes, field, late)


def image_kernel(
    sizes_ref, inner_ref, near_ref, far_ref, keep_ref, got_ref, parts_in_ref, parts_ref, copies_ref
):
    base = PARTS * ROWS
    odd = jnp.full((COLS, 128), lax.axis_index("z") % 2) == 1
    for step in range(STEPS):
        kappa = 0.5 * sizes_ref[step]
        for line in range(LINES):
            side = pl.ds(step * LINES + line, COLS, stride=STEPS * LINES)
            near = near_ref[side, :]
            far = far_ref[side, :]
            for plane, halo in ((0, jnp.where(odd, near, far)), (1, jnp.where(odd, far, near))):
                place = place_of(step, plane, line)
                for part, piece in enumerate(split(inner_ref[place] - kappa * halo)):
                    parts_ref[
                        base + part * COLS : base + (part + 1) * COLS, place * 128 : (place + 1) * 128
                    ] = piece
    own_parts = parts_ref[base:]
    products = lax.dot_general(own_parts, parts_ref[...], NT, preferred_element_type=F32)
    proj = part_products(products, COLS, 0, ROWS)
    gram = part_products(products, COLS, base, COLS)
    packed = jnp.concatenate([proj[:8], proj[8:]], axis=1)
    pieces = []
    for half in range(2):
        lines = [gram[half * 8 + row : half * 8 + row + 1] for row in range(8)]
        pieces.append(jnp.concatenate(lines, axis=1))
    chip = keep_ref[...] + got_ref[...]
    last = jnp.concatenate(pieces + [chip[8:10]], axis=0)
    for copy in range(SLABS):
        copies_ref[copy, 0] = packed[:4]
        copies_ref[copy, 1] = packed[4:]
        copies_ref[copy, 2] = chip[0:4]
        copies_ref[copy, 3] = chip[4:8]
        copies_ref[copy, 4] = last


def image_products(sizes, inside, near, far, keep, got, parts):
    return pl.pallas_call(
        image_kernel,
        out_shape=(
            jax.ShapeDtypeStruct((PARTS * FULL, CELLS), BF16),
            jax.ShapeDtypeStruct((SLABS, 5, 4, 128), F32),
        ),
        in_specs=[VMEM] * 7,
        out_specs=(VMEM, VMEM),
        input_output_aliases={6: 0},
        compiler_params=params(20),
        name="image_products",
    )(sizes, inside, near, far, keep, got, parts)


def regroup_kernel(sums_ref, copies_ref):
    total = sums_ref[0]
    for piece in range(1, SLABS):
        total = total + sums_ref[piece]
    for copy in range(GROUPS):
        copies_ref[copy] = total


def regroup(sums):
    return pl.pallas_call(
        regroup_kernel,
        out_shape=jax.ShapeDtypeStruct((GROUPS, 5, 4, 128), F32),
        in_specs=[VMEM],
        out_specs=VMEM,
        compiler_params=params(4),
        name="regroup",
    )(sums)


def finish_kernel(sums_ref, parts_ref, hess_ref, triangle_ref, next_ref):
    cores = []
    for core in range(2):
        total = sums_ref[core]
        for piece in range(core + 2, GROUPS, 2):
            total = total + sums_ref[piece]
        cores.append(total * (1.0 / TOTAL))
    sums = cores[0] + cores[1]
    proj = jnp.concatenate(
        [sums[0, :, :ROWS], sums[1, :, :ROWS], sums[0, :, ROWS:], sums[1, :, ROWS:]], axis=0
    )
    image_gram = jnp.concatenate(
        [
            sums[4, half : half + 1, line * COLS : (line + 1) * COLS]
            for half in range(2)
            for line in range(8)
        ],
        axis=0,
    )
    packed = jnp.concatenate([cores[0][2], cores[0][3], cores[1][2], cores[1][3]], axis=0)
    rest = jnp.concatenate(
        [cores[core][4, 2:4, 32 * i : 32 * i + 32] for core in range(2) for i in range(4)], axis=0
    )
    kept = [packed[:, :64], packed[:, 64:112], rest, packed[:, 112:]]
    upper = []
    for block in range(BLOCKS):
        pieces = [0.5 * kept[block][:, :COLS]]
        if block:
            pieces.insert(0, jnp.zeros((COLS, block * COLS), F32))
        if block < BLOCKS - 1:
            pieces.append(kept[block][:, COLS:])
        upper.append(jnp.concatenate(pieces, axis=1))
    half = jnp.concatenate(upper, axis=0)
    carried = lax.dot_general(proj, half, NN, precision=HIGHEST, preferred_element_type=F32) - proj
    cross = lax.dot_general(carried, proj, NT, precision=HIGHEST, preferred_element_type=F32)
    cross_t = lax.dot_general(proj, carried, NT, precision=HIGHEST, preferred_element_type=F32)
    gram = image_gram + (cross + cross_t)
    row = lax.broadcasted_iota(jnp.int32, (COLS, COLS), 0)
    col = lax.broadcasted_iota(jnp.int32, (COLS, COLS), 1)
    eye = jnp.where(row == col, 1.0, 0.0).astype(F32)
    work = jnp.concatenate(
        [gram, -proj, eye, jnp.zeros((COLS, 128 - FULL - COLS), F32)], axis=1
    )
    wide_row = lax.broadcasted_iota(jnp.int32, (COLS, 128), 0)
    columns = [jnp.broadcast_to(gram[:, k : k + 1], (COLS, 128)) for k in range(COLS)]
    scale = jnp.zeros((COLS, 128), F32)
    for step in range(COLS):
        pivot = jnp.broadcast_to(columns[step][step : step + 1], (COLS, 128))
        factor = jnp.where(wide_row > step, columns[step] * (1.0 / pivot), 0.0)
        for k in range(step + 1, COLS):
            columns[k] = columns[k] - factor * columns[k][step : step + 1]
        work = work - factor * work[step : step + 1]
        scale = jnp.where(wide_row == step, lax.rsqrt(pivot), scale)
    work = work * scale
    hess_ref[...] = proj.T
    triangle_ref[...] = jnp.where(row <= col, work[:, :COLS], 0.0)
    factors = split(work[:, COLS : COLS + FULL])
    stacked = []
    for part in range(PARTS):
        pieces = []
        for piece in (factors[part][:, :ROWS], factors[part][:, ROWS:]):
            for other in range(PARTS):
                pieces.append(piece if other < PARTS - part else jnp.zeros_like(piece))
        stacked.append(jnp.concatenate(pieces, axis=1))
    factor = jnp.concatenate(stacked, axis=0)
    for tile in range(PLACES // 8):
        lanes = slice(tile * 1024, (tile + 1) * 1024)
        product = lax.dot_general(factor, parts_ref[:, lanes], NN, preferred_element_type=F32)
        value = product[:COLS] + (product[COLS : 2 * COLS] + product[2 * COLS :])
        for line in range(8):
            next_ref[pl.ds(tile * 8 + line, COLS, stride=PLACES), :] = value[
                :, line * 128 : (line + 1) * 128
            ]


def finish(sums, parts):
    return pl.pallas_call(
        finish_kernel,
        out_shape=(
            jax.ShapeDtypeStruct((ROWS, COLS), F32),
            jax.ShapeDtypeStruct((COLS, COLS), F32),
            jax.ShapeDtypeStruct((COLS * PLACES, 128), F32),
        ),
        in_specs=[VMEM, VMEM],
        out_specs=(VMEM, VMEM, VMEM),
        compiler_params=params(20),
        name="finish",
    )(sums, parts)


def exchanged(copies, axes):
    return lax.all_to_all(copies, axes, 0, 0)


def per_device(basis, num, den):
    slabs = size_of(SPACE)
    groups = size_of(TM)
    pairs = [(i, i ^ 1) for i in range(slabs)]
    others = [(i, ((i + 1) ^ 1) - 1) for i in range(1, slabs - 1)]
    later = [(i, i + 1) for i in range(groups - 1)]
    flat = basis.reshape(ROWS, PLACES, 1, 128)
    near, far, late, sizes = edges(num, den, basis)
    near = lax.ppermute(near, SPACE, pairs).reshape(-1, 128)
    far = lax.ppermute(far, SPACE, others).reshape(-1, 128)
    late = lax.ppermute(late, TM, later).reshape(-1, 128)
    parts, field, keep, give = basis_products(flat)
    got = lax.ppermute(give, "core", [(0, 1), (1, 0)])
    inside = inner(sizes, field, late)
    parts, copies = image_products(sizes, inside, near, far, keep, got, parts)
    sums = exchanged(regroup(exchanged(copies, SPACE)), TM)
    hess, triangle, following = finish(sums, parts)
    return (
        hess.reshape(BLOCKS, COLS, COLS),
        triangle,
        following.reshape(COLS, STEPS, PLANES, LINES, 128),
    )


def solution(mesh):
    fine = Mesh(mesh.devices.reshape(8, 2, 4, 8), ("y", "core", "x", "z"))
    placed = (P(None, None, TM, SPACE, None, None), P(TM), P(TM))
    return jax.shard_map(
        per_device,
        mesh=fine,
        in_specs=placed,
        out_specs=(P(), P(), P(None, TM, SPACE, None, None)),
        check_vma=False,
    )
```

```python
import jax
import jax.numpy as jnp
from jax import lax
from jax.experimental import pallas as pl
from jax.experimental.pallas import tpu as pltpu
from jax.sharding import Mesh, PartitionSpec as P

TM = ("y", "core")
SPACE = ("x", "z")
GROUPS = 16
SLABS = 32
COLS = 16
BLOCKS = 4
ROWS = BLOCKS * COLS
FULL = ROWS + COLS
STEPS = 4
PLANES = 2
LINES = 8
PLACES = STEPS * PLANES * LINES
CELLS = PLACES * 128
SIDE = PLANES * LINES
TOTAL = 64 * 64 * 8 * 128
PARTS = 3
HIGHEST = lax.Precision.HIGHEST
F32 = jnp.float32
BF16 = jnp.bfloat16
NT = (((1,), (1,)), ((), ()))
NN = (((1,), (0,)), ((), ()))
VMEM = pl.BlockSpec(memory_space=pltpu.VMEM)
HBM = pl.BlockSpec(memory_space=pltpu.HBM)


def params(megabytes):
    return pltpu.CompilerParams(vmem_limit_bytes=megabytes * 1024 * 1024)


def in_hbm(array):
    return pltpu.with_memory_space_constraint(array, pltpu.HBM)


def size_of(axes):
    count = 1
    for axis in axes:
        count *= lax.axis_size(axis)
    return count


def place_of(step, plane, line):
    return (step * PLANES + plane) * LINES + line


def split(value):
    first = value.astype(BF16)
    rest = value - first.astype(F32)
    second = rest.astype(BF16)
    third = (rest - second.astype(F32)).astype(BF16)
    return first, second, third


def edges_kernel(
    num_hbm, den_hbm, basis_hbm, near_ref, far_ref, late_ref, sizes_ref, num_ref, den_ref, sems
):
    last = BLOCKS - 1
    odd = lax.axis_index("z") % 2
    counts = [
        pltpu.make_async_copy(num_hbm, num_ref, sems.at[3]),
        pltpu.make_async_copy(den_hbm, den_ref, sems.at[4]),
    ]
    copies = [
        pltpu.make_async_copy(basis_hbm.at[last, :, :, 1 - odd], near_ref, sems.at[0]),
        pltpu.make_async_copy(basis_hbm.at[last, :, :, odd], far_ref, sems.at[1]),
        pltpu.make_async_copy(
            basis_hbm.at[last, :, STEPS - 1], late_ref.at[pl.ds(0, COLS)], sems.at[2]
        ),
    ]
    for copy in copies + counts:
        copy.start()
    for copy in counts:
        copy.wait()
    for step in range(STEPS):
        top = jnp.full((COLS, 128), num_ref[step]).astype(F32)
        bottom = jnp.full((COLS, 128), den_ref[step]).astype(F32)
        sizes_ref[step] = top / bottom
    for plane in range(PLANES):
        late_ref[COLS, plane] = sizes_ref[STEPS - 1, :LINES]
    for copy in copies:
        copy.wait()


def edges(num, den, basis):
    face = jax.ShapeDtypeStruct((COLS, STEPS, LINES, 128), F32)
    return pl.pallas_call(
        edges_kernel,
        out_shape=(
            face,
            face,
            jax.ShapeDtypeStruct((COLS + 1, PLANES, LINES, 128), F32),
            jax.ShapeDtypeStruct((STEPS, COLS, 128), F32),
        ),
        in_specs=[HBM, HBM, HBM],
        out_specs=(VMEM, VMEM, VMEM, VMEM),
        scratch_shapes=[
            pltpu.SMEM((STEPS,), jnp.int32),
            pltpu.SMEM((STEPS,), jnp.int32),
            pltpu.SemaphoreType.DMA((5,)),
        ],
        compiler_params=params(4),
        name="edges",
    )(in_hbm(num), in_hbm(den), in_hbm(basis))


def part_products(products, count, offset, width):
    total = None
    for b in range(PARTS):
        group = None
        for a in range(PARTS - b):
            piece = products[a * count : (a + 1) * count, offset + b * width : offset + (b + 1) * width]
            group = piece if group is None else group + piece
        total = group if total is None else total + group
    return total


def basis_kernel(basis_hbm, parts_ref, last_ref, keep_ref, give_ref, field_ref, sems):
    copies = [
        pltpu.make_async_copy(basis_hbm.at[:, place, 0], field_ref.at[place], sems.at[place])
        for place in range(PLACES)
    ]
    for copy in copies:
        copy.start()
    for place in range(PLACES):
        copies[place].wait()
        value = field_ref[place]
        last_ref[place] = value[ROWS - COLS :]
        if place_of(STEPS - 2, 0, 0) <= place < place_of(STEPS - 1, 0, 0):
            give_ref[place - place_of(STEPS - 2, 0, 0)] = value[ROWS - COLS :]
        for part, piece in enumerate(split(value)):
            parts_ref[part * ROWS : (part + 1) * ROWS, place * 128 : (place + 1) * 128] = piece
    whole = parts_ref[: PARTS * ROWS]
    products = lax.dot_general(whole, whole, NT, preferred_element_type=F32)
    gram = part_products(products, ROWS, 0, ROWS)
    rows = [gram[block * COLS : (block + 1) * COLS, block * COLS :] for block in range(BLOCKS)]
    packed = jnp.concatenate([rows[0], rows[1], rows[3]], axis=1)
    halves = []
    for half in range(2):
        rest = rows[2][half * 8 : half * 8 + 8]
        rest = jnp.concatenate([rest[2 * i : 2 * i + 2] for i in range(4)], axis=1)
        halves.append((packed[half * 8 : half * 8 + 8], rest))
    own = lax.axis_index("core")
    first = jnp.full((8, 128), own) == 0
    for target, flip in ((keep_ref, False), (give_ref.at[SIDE], True)):
        one, two = (halves[1], halves[0]) if flip else (halves[0], halves[1])
        target[0:8] = jnp.where(first, one[0], two[0])
        target[8:10] = jnp.where(first[:2], one[1], two[1])
        target[10:COLS] = jnp.zeros((COLS - 10, 128), F32)


def basis_products(basis):
    return pl.pallas_call(
        basis_kernel,
        out_shape=(
            jax.ShapeDtypeStruct((PARTS * FULL, CELLS), BF16),
            jax.ShapeDtypeStruct((PLACES, COLS, 128), F32),
            jax.ShapeDtypeStruct((COLS, 128), F32),
            jax.ShapeDtypeStruct((SIDE + 1, COLS, 128), F32),
        ),
        in_specs=[HBM],
        out_specs=(VMEM, VMEM, VMEM, VMEM),
        scratch_shapes=[
            pltpu.VMEM((PLACES, ROWS, 128), F32),
            pltpu.SemaphoreType.DMA((PLACES,)),
        ],
        compiler_params=params(20),
        name="basis_products",
    )(in_hbm(basis))


def inner_kernel(sizes_ref, field_ref, late_ref, near_ref, far_ref, inner_ref, weight_ref):
    sizes = [sizes_ref[step] for step in range(STEPS)]
    odd = jnp.full((COLS, 128), lax.axis_index("z") % 2) == 1
    first = (lax.axis_index("y") == 0) & (lax.axis_index("core") == 0)
    start = jnp.full((COLS, 128), first.astype(jnp.int32)) == 1
    lane = lax.broadcasted_iota(jnp.int32, (COLS, 128), 1)

    def at(step, plane, line):
        if step < 0:
            return late_ref[pl.ds(plane * LINES + line, COLS, stride=SIDE), :]
        return field_ref[place_of(step, plane, line)]

    for step in range(STEPS):
        kappa = 0.5 * sizes[step]
        if step == 0:
            before = late_ref[pl.ds(COLS * SIDE, LINES), :]
            before = jnp.where(start, sizes[0], jnp.concatenate([before, before], axis=0))
        else:
            before = sizes[step - 1]
        ratio = sizes[step] / before
        now = (1.0 + 2.0 * ratio) / (1.0 + ratio)
        one = 1.0 + ratio
        two = ratio * ratio / (1.0 + ratio)
        if step == 0:
            now = jnp.where(start, 1.0, now)
            one = jnp.where(start, 1.0, one)
            weight_ref[...] = jnp.where(start, 0.0, two)
        for line in range(LINES):
            side = pl.ds(step * LINES + line, COLS, stride=STEPS * LINES)
            near = near_ref[side, :]
            far = far_ref[side, :]
            for plane, halo in ((0, jnp.where(odd, near, far)), (1, jnp.where(odd, far, near))):
                value = at(step, plane, line)
                beside = halo + at(step, PLANES - 1 - plane, line)
                if line > 0:
                    beside += at(step, plane, line - 1)
                if line < LINES - 1:
                    beside += at(step, plane, line + 1)
                beside += jnp.where(lane < 127, pltpu.roll(value, 127, 1), 0.0)
                beside += jnp.where(lane > 0, pltpu.roll(value, 1, 1), 0.0)
                result = now * value - one * at(step - 1, plane, line)
                if step > 0:
                    result += two * at(step - 2, plane, line)
                result += kappa * (6.0 * value - beside)
                inner_ref[place_of(step, plane, line)] = result


def inner(sizes, field, late, near, far):
    return pl.pallas_call(
        inner_kernel,
        out_shape=(
            jax.ShapeDtypeStruct((PLACES, COLS, 128), F32),
            jax.ShapeDtypeStruct((COLS, 128), F32),
        ),
        in_specs=[VMEM] * 5,
        out_specs=(VMEM, VMEM),
        compiler_params=params(8),
        name="inner",
    )(sizes, field, late, near, far)


def image_kernel(
    weight_ref, inner_ref, keep_ref, got_ref, parts_in_ref, parts_ref, copies_ref
):
    base = PARTS * ROWS
    weight = weight_ref[...]
    for place in range(PLACES):
        result = inner_ref[place]
        if place < SIDE:
            result += weight * got_ref[place]
        for part, piece in enumerate(split(result)):
            parts_ref[
                base + part * COLS : base + (part + 1) * COLS, place * 128 : (place + 1) * 128
            ] = piece
    own_parts = parts_ref[base:]
    products = lax.dot_general(own_parts, parts_ref[...], NT, preferred_element_type=F32)
    proj = part_products(products, COLS, 0, ROWS)
    gram = part_products(products, COLS, base, COLS)
    packed = jnp.concatenate([proj[:8], proj[8:]], axis=1)
    pieces = []
    for half in range(2):
        lines = [gram[half * 8 + row : half * 8 + row + 1] for row in range(8)]
        pieces.append(jnp.concatenate(lines, axis=1))
    chip = keep_ref[...] + got_ref[SIDE]
    last = jnp.concatenate(pieces + [chip[8:10]], axis=0)
    for copy in range(SLABS):
        copies_ref[copy, 0] = packed[:4]
        copies_ref[copy, 1] = packed[4:]
        copies_ref[copy, 2] = chip[0:4]
        copies_ref[copy, 3] = chip[4:8]
        copies_ref[copy, 4] = last


def image_products(weight, inside, keep, got, parts):
    return pl.pallas_call(
        image_kernel,
        out_shape=(
            jax.ShapeDtypeStruct((PARTS * FULL, CELLS), BF16),
            jax.ShapeDtypeStruct((SLABS, 5, 4, 128), F32),
        ),
        in_specs=[VMEM] * 5,
        out_specs=(VMEM, VMEM),
        input_output_aliases={4: 0},
        compiler_params=params(20),
        name="image_products",
    )(weight, inside, keep, got, parts)


def regroup_kernel(sums_ref, copies_ref):
    total = sums_ref[0]
    for piece in range(1, SLABS):
        total = total + sums_ref[piece]
    for copy in range(GROUPS):
        copies_ref[copy] = total


def regroup(sums):
    return pl.pallas_call(
        regroup_kernel,
        out_shape=jax.ShapeDtypeStruct((GROUPS, 5, 4, 128), F32),
        in_specs=[VMEM],
        out_specs=VMEM,
        compiler_params=params(4),
        name="regroup",
    )(sums)


def finish_kernel(sums_ref, parts_ref, hess_ref, triangle_ref, next_ref):
    cores = []
    for core in range(2):
        total = sums_ref[core]
        for piece in range(core + 2, GROUPS, 2):
            total = total + sums_ref[piece]
        cores.append(total * (1.0 / TOTAL))
    sums = cores[0] + cores[1]
    proj = jnp.concatenate(
        [sums[0, :, :ROWS], sums[1, :, :ROWS], sums[0, :, ROWS:], sums[1, :, ROWS:]], axis=0
    )
    image_gram = jnp.concatenate(
        [
            sums[4, half : half + 1, line * COLS : (line + 1) * COLS]
            for half in range(2)
            for line in range(8)
        ],
        axis=0,
    )
    packed = jnp.concatenate([cores[0][2], cores[0][3], cores[1][2], cores[1][3]], axis=0)
    rest = jnp.concatenate(
        [cores[core][4, 2:4, 32 * i : 32 * i + 32] for core in range(2) for i in range(4)], axis=0
    )
    kept = [packed[:, :64], packed[:, 64:112], rest, packed[:, 112:]]
    upper = []
    for block in range(BLOCKS):
        pieces = [0.5 * kept[block][:, :COLS]]
        if block:
            pieces.insert(0, jnp.zeros((COLS, block * COLS), F32))
        if block < BLOCKS - 1:
            pieces.append(kept[block][:, COLS:])
        upper.append(jnp.concatenate(pieces, axis=1))
    half = jnp.concatenate(upper, axis=0)
    carried = lax.dot_general(proj, half, NN, precision=HIGHEST, preferred_element_type=F32) - proj
    cross = lax.dot_general(carried, proj, NT, precision=HIGHEST, preferred_element_type=F32)
    cross_t = lax.dot_general(proj, carried, NT, precision=HIGHEST, preferred_element_type=F32)
    gram = image_gram + (cross + cross_t)
    row = lax.broadcasted_iota(jnp.int32, (COLS, COLS), 0)
    col = lax.broadcasted_iota(jnp.int32, (COLS, COLS), 1)
    eye = jnp.where(row == col, 1.0, 0.0).astype(F32)
    work = jnp.concatenate(
        [gram, -proj, eye, jnp.zeros((COLS, 128 - FULL - COLS), F32)], axis=1
    )
    wide_row = lax.broadcasted_iota(jnp.int32, (COLS, 128), 0)
    columns = [jnp.broadcast_to(gram[:, k : k + 1], (COLS, 128)) for k in range(COLS)]
    scale = jnp.zeros((COLS, 128), F32)
    for step in range(COLS):
        pivot = jnp.broadcast_to(columns[step][step : step + 1], (COLS, 128))
        factor = jnp.where(wide_row > step, columns[step] * (1.0 / pivot), 0.0)
        for k in range(step + 1, COLS):
            columns[k] = columns[k] - factor * columns[k][step : step + 1]
        work = work - factor * work[step : step + 1]
        scale = jnp.where(wide_row == step, lax.rsqrt(pivot), scale)
    work = work * scale
    hess_ref[...] = proj.T
    triangle_ref[...] = jnp.where(row <= col, work[:, :COLS], 0.0)
    factors = split(work[:, COLS : COLS + FULL])
    stacked = []
    for part in range(PARTS):
        pieces = []
        for piece in (factors[part][:, :ROWS], factors[part][:, ROWS:]):
            for other in range(PARTS):
                pieces.append(piece if other < PARTS - part else jnp.zeros_like(piece))
        stacked.append(jnp.concatenate(pieces, axis=1))
    factor = jnp.concatenate(stacked, axis=0)
    for tile in range(PLACES // 8):
        lanes = slice(tile * 1024, (tile + 1) * 1024)
        product = lax.dot_general(factor, parts_ref[:, lanes], NN, preferred_element_type=F32)
        value = product[:COLS] + (product[COLS : 2 * COLS] + product[2 * COLS :])
        for line in range(8):
            next_ref[pl.ds(tile * 8 + line, COLS, stride=PLACES), :] = value[
                :, line * 128 : (line + 1) * 128
            ]


def finish(sums, parts):
    return pl.pallas_call(
        finish_kernel,
        out_shape=(
            jax.ShapeDtypeStruct((ROWS, COLS), F32),
            jax.ShapeDtypeStruct((COLS, COLS), F32),
            jax.ShapeDtypeStruct((COLS * PLACES, 128), F32),
        ),
        in_specs=[VMEM, VMEM],
        out_specs=(VMEM, VMEM, VMEM),
        compiler_params=params(20),
        name="finish",
    )(sums, parts)


def exchanged(copies, axes):
    return lax.all_to_all(copies, axes, 0, 0)


def per_device(basis, num, den):
    slabs = size_of(SPACE)
    groups = size_of(TM)
    pairs = [(i, i ^ 1) for i in range(slabs)]
    others = [(i, ((i + 1) ^ 1) - 1) for i in range(1, slabs - 1)]
    later = [(i, i + 1) for i in range(groups - 1)]
    flat = basis.reshape(ROWS, PLACES, 1, 128)
    near, far, late, sizes = edges(num, den, basis)
    near = lax.ppermute(near, SPACE, pairs).reshape(-1, 128)
    far = lax.ppermute(far, SPACE, others).reshape(-1, 128)
    late = lax.ppermute(late, TM, later).reshape(-1, 128)
    parts, field, keep, give = basis_products(flat)
    got = lax.ppermute(give, TM, later + [(groups - 1, 0)])
    inside, weight = inner(sizes, field, late, near, far)
    parts, copies = image_products(weight, inside, keep, got, parts)
    sums = exchanged(regroup(exchanged(copies, SPACE)), TM)
    hess, triangle, following = finish(sums, parts)
    return (
        hess.reshape(BLOCKS, COLS, COLS),
        triangle,
        following.reshape(COLS, STEPS, PLANES, LINES, 128),
    )


def solution(mesh):
    fine = Mesh(mesh.devices.reshape(8, 2, 4, 8), ("y", "core", "x", "z"))
    placed = (P(None, None, TM, SPACE, None, None), P(TM), P(TM))
    return jax.shard_map(
        per_device,
        mesh=fine,
        in_specs=placed,
        out_specs=(P(), P(), P(None, TM, SPACE, None, None)),
        check_vma=False,
    )
```

```python
import jax
import jax.numpy as jnp
from jax import lax
from jax.experimental import pallas as pl
from jax.experimental.pallas import tpu as pltpu
from jax.sharding import Mesh, PartitionSpec as P

TM = ("y", "core")
SPACE = ("x", "z")
GROUPS = 16
SLABS = 32
COLS = 16
BLOCKS = 4
ROWS = BLOCKS * COLS
FULL = ROWS + COLS
STEPS = 4
PLANES = 2
LINES = 8
PLACES = STEPS * PLANES * LINES
CELLS = PLACES * 128
SIDE = 2 * PLANES * LINES
TOTAL = 64 * 64 * 8 * 128
PARTS = 3
HIGHEST = lax.Precision.HIGHEST
F32 = jnp.float32
BF16 = jnp.bfloat16
NT = (((1,), (1,)), ((), ()))
NN = (((1,), (0,)), ((), ()))
VMEM = pl.BlockSpec(memory_space=pltpu.VMEM)
HBM = pl.BlockSpec(memory_space=pltpu.HBM)


def params(megabytes):
    return pltpu.CompilerParams(vmem_limit_bytes=megabytes * 1024 * 1024)


def in_hbm(array):
    return pltpu.with_memory_space_constraint(array, pltpu.HBM)


def size_of(axes):
    count = 1
    for axis in axes:
        count *= lax.axis_size(axis)
    return count


def place_of(step, plane, line):
    return (step * PLANES + plane) * LINES + line


def split(value):
    first = value.astype(BF16)
    rest = value - first.astype(F32)
    second = rest.astype(BF16)
    third = (rest - second.astype(F32)).astype(BF16)
    return first, second, third


def edges_kernel(
    num_hbm, den_hbm, basis_hbm, first_ref, second_ref, late_ref, sizes_ref, num_ref, den_ref, sems
):
    last = BLOCKS - 1
    flip = (lax.axis_index("z") + lax.axis_index("core")) % 2
    counts = [
        pltpu.make_async_copy(num_hbm, num_ref, sems.at[3]),
        pltpu.make_async_copy(den_hbm, den_ref, sems.at[4]),
    ]
    copies = [
        pltpu.make_async_copy(basis_hbm.at[last, :, :, 1 - flip], first_ref, sems.at[0]),
        pltpu.make_async_copy(basis_hbm.at[last, :, :, flip], second_ref, sems.at[1]),
        pltpu.make_async_copy(
            basis_hbm.at[last, :, pl.ds(STEPS - 2, 2)], late_ref.at[pl.ds(0, COLS)], sems.at[2]
        ),
    ]
    for copy in copies + counts:
        copy.start()
    for copy in counts:
        copy.wait()
    for step in range(STEPS):
        top = jnp.full((COLS, 128), num_ref[step]).astype(F32)
        bottom = jnp.full((COLS, 128), den_ref[step]).astype(F32)
        sizes_ref[step] = top / bottom
    for step in range(2):
        for plane in range(PLANES):
            late_ref[COLS, step, plane] = sizes_ref[STEPS - 1, :LINES]
    for copy in copies:
        copy.wait()


def edges(num, den, basis):
    face = jax.ShapeDtypeStruct((COLS, STEPS, LINES, 128), F32)
    return pl.pallas_call(
        edges_kernel,
        out_shape=(
            face,
            face,
            jax.ShapeDtypeStruct((COLS + 1, 2, PLANES, LINES, 128), F32),
            jax.ShapeDtypeStruct((STEPS, COLS, 128), F32),
        ),
        in_specs=[HBM, HBM, HBM],
        out_specs=(VMEM, VMEM, VMEM, VMEM),
        scratch_shapes=[
            pltpu.SMEM((STEPS,), jnp.int32),
            pltpu.SMEM((STEPS,), jnp.int32),
            pltpu.SemaphoreType.DMA((5,)),
        ],
        compiler_params=params(4),
        name="edges",
    )(in_hbm(num), in_hbm(den), in_hbm(basis))


def part_products(products, count, offset, width):
    total = None
    for b in range(PARTS):
        group = None
        for a in range(PARTS - b):
            piece = products[a * count : (a + 1) * count, offset + b * width : offset + (b + 1) * width]
            group = piece if group is None else group + piece
        total = group if total is None else total + group
    return total


def basis_kernel(basis_hbm, parts_ref, last_ref, keep_ref, give_ref, field_ref, sems):
    copies = [
        pltpu.make_async_copy(basis_hbm.at[:, place, 0], field_ref.at[place], sems.at[place])
        for place in range(PLACES)
    ]
    for copy in copies:
        copy.start()
    for place in range(PLACES):
        copies[place].wait()
        value = field_ref[place]
        last_ref[place] = value[ROWS - COLS :]
        for part, piece in enumerate(split(value)):
            parts_ref[part * ROWS : (part + 1) * ROWS, place * 128 : (place + 1) * 128] = piece
    whole = parts_ref[: PARTS * ROWS]
    products = lax.dot_general(whole, whole, NT, preferred_element_type=F32)
    gram = part_products(products, ROWS, 0, ROWS)
    rows = [gram[block * COLS : (block + 1) * COLS, block * COLS :] for block in range(BLOCKS)]
    packed = jnp.concatenate([rows[0], rows[1], rows[3]], axis=1)
    halves = []
    for half in range(2):
        rest = rows[2][half * 8 : half * 8 + 8]
        rest = jnp.concatenate([rest[2 * i : 2 * i + 2] for i in range(4)], axis=1)
        halves.append((packed[half * 8 : half * 8 + 8], rest))
    own = lax.axis_index("core")
    first = jnp.full((8, 128), own) == 0
    for target, flip in ((keep_ref, False), (give_ref, True)):
        one, two = (halves[1], halves[0]) if flip else (halves[0], halves[1])
        target[0:8] = jnp.where(first, one[0], two[0])
        target[8:10] = jnp.where(first[:2], one[1], two[1])
        target[10:16] = jnp.zeros((6, 128), F32)


def basis_products(basis):
    return pl.pallas_call(
        basis_kernel,
        out_shape=(
            jax.ShapeDtypeStruct((PARTS * FULL, CELLS), BF16),
            jax.ShapeDtypeStruct((PLACES, COLS, 128), F32),
            jax.ShapeDtypeStruct((16, 128), F32),
            jax.ShapeDtypeStruct((16, 128), F32),
        ),
        in_specs=[HBM],
        out_specs=(VMEM, VMEM, VMEM, VMEM),
        scratch_shapes=[
            pltpu.VMEM((PLACES, ROWS, 128), F32),
            pltpu.SemaphoreType.DMA((PLACES,)),
        ],
        compiler_params=params(20),
        name="basis_products",
    )(in_hbm(basis))


def inner_kernel(sizes_ref, field_ref, late_ref, inner_ref):
    sizes = [sizes_ref[step] for step in range(STEPS)]
    first = (lax.axis_index("y") == 0) & (lax.axis_index("core") == 0)
    start = jnp.full((COLS, 128), first.astype(jnp.int32)) == 1
    weights = []
    for step in range(STEPS):
        if step == 0:
            before = late_ref[pl.ds(COLS * SIDE, LINES), :]
            before = jnp.where(start, sizes[0], jnp.concatenate([before, before], axis=0))
        else:
            before = sizes[step - 1]
        ratio = sizes[step] / before
        now = (1.0 + 2.0 * ratio) / (1.0 + ratio)
        one = 1.0 + ratio
        two = ratio * ratio / (1.0 + ratio)
        if step == 0:
            now = jnp.where(start, 1.0, now)
            one = jnp.where(start, 1.0, one)
            two = jnp.where(start, 0.0, two)
        weights.append((now, one, two, 0.5 * sizes[step]))
    lane = lax.broadcasted_iota(jnp.int32, (COLS, 128), 1)

    past = [late_ref[pl.ds(place, COLS, stride=SIDE), :] for place in range(SIDE)]

    def at(step, plane, line):
        if step < 0:
            return past[place_of(step + 2, plane, line)]
        return field_ref[place_of(step, plane, line)]

    for step in range(STEPS):
        now, one, two, kappa = weights[step]
        for plane in range(PLANES):
            for line in range(LINES):
                value = at(step, plane, line)
                beside = at(step, PLANES - 1 - plane, line)
                if line > 0:
                    beside += at(step, plane, line - 1)
                if line < LINES - 1:
                    beside += at(step, plane, line + 1)
                beside += jnp.where(lane < 127, pltpu.roll(value, 127, 1), 0.0)
                beside += jnp.where(lane > 0, pltpu.roll(value, 1, 1), 0.0)
                result = (
                    now * value
                    - one * at(step - 1, plane, line)
                    + two * at(step - 2, plane, line)
                    + kappa * (6.0 * value - beside)
                )
                inner_ref[place_of(step, plane, line)] = result


def inner(sizes, field, late):
    return pl.pallas_call(
        inner_kernel,
        out_shape=jax.ShapeDtypeStruct((PLACES, COLS, 128), F32),
        in_specs=[VMEM] * 3,
        out_specs=VMEM,
        compiler_params=params(8),
        name="inner",
    )(sizes, field, late)


def image_kernel(
    sizes_ref, inner_ref, first_ref, second_ref, keep_ref, got_ref, parts_in_ref, parts_ref, copies_ref
):
    base = PARTS * ROWS
    flip = (lax.axis_index("z") + lax.axis_index("core")) % 2
    flipped = jnp.full((COLS, 128), flip) == 1
    for step in range(STEPS):
        kappa = 0.5 * sizes_ref[step]
        for line in range(LINES):
            side = pl.ds(step * LINES + line, COLS, stride=STEPS * LINES)
            one = first_ref[side, :]
            two = second_ref[side, :]
            for plane, halo in ((0, jnp.where(flipped, one, two)), (1, jnp.where(flipped, two, one))):
                place = place_of(step, plane, line)
                for part, piece in enumerate(split(inner_ref[place] - kappa * halo)):
                    parts_ref[
                        base + part * COLS : base + (part + 1) * COLS, place * 128 : (place + 1) * 128
                    ] = piece
    own_parts = parts_ref[base:]
    products = lax.dot_general(own_parts, parts_ref[...], NT, preferred_element_type=F32)
    proj = part_products(products, COLS, 0, ROWS)
    gram = part_products(products, COLS, base, COLS)
    packed = jnp.concatenate([proj[:8], proj[8:]], axis=1)
    pieces = []
    for half in range(2):
        lines = [gram[half * 8 + row : half * 8 + row + 1] for row in range(8)]
        pieces.append(jnp.concatenate(lines, axis=1))
    chip = keep_ref[...] + got_ref[...]
    last = jnp.concatenate(pieces + [chip[8:10]], axis=0)
    for copy in range(SLABS):
        copies_ref[copy, 0] = packed[:4]
        copies_ref[copy, 1] = packed[4:]
        copies_ref[copy, 2] = chip[0:4]
        copies_ref[copy, 3] = chip[4:8]
        copies_ref[copy, 4] = last


def image_products(sizes, inside, one, two, keep, got, parts):
    return pl.pallas_call(
        image_kernel,
        out_shape=(
            jax.ShapeDtypeStruct((PARTS * FULL, CELLS), BF16),
            jax.ShapeDtypeStruct((SLABS, 5, 4, 128), F32),
        ),
        in_specs=[VMEM] * 7,
        out_specs=(VMEM, VMEM),
        input_output_aliases={6: 0},
        compiler_params=params(20),
        name="image_products",
    )(sizes, inside, one, two, keep, got, parts)


def regroup_kernel(sums_ref, copies_ref):
    total = sums_ref[0]
    for piece in range(1, SLABS):
        total = total + sums_ref[piece]
    for copy in range(GROUPS):
        copies_ref[copy] = total


def regroup(sums):
    return pl.pallas_call(
        regroup_kernel,
        out_shape=jax.ShapeDtypeStruct((GROUPS, 5, 4, 128), F32),
        in_specs=[VMEM],
        out_specs=VMEM,
        compiler_params=params(4),
        name="regroup",
    )(sums)


def finish_kernel(sums_ref, parts_ref, hess_ref, triangle_ref, next_ref):
    cores = []
    for core in range(2):
        total = sums_ref[core]
        for piece in range(core + 2, GROUPS, 2):
            total = total + sums_ref[piece]
        cores.append(total * (1.0 / TOTAL))
    sums = cores[0] + cores[1]
    proj = jnp.concatenate(
        [sums[0, :, :ROWS], sums[1, :, :ROWS], sums[0, :, ROWS:], sums[1, :, ROWS:]], axis=0
    )
    image_gram = jnp.concatenate(
        [
            sums[4, half : half + 1, line * COLS : (line + 1) * COLS]
            for half in range(2)
            for line in range(8)
        ],
        axis=0,
    )
    packed = jnp.concatenate([cores[0][2], cores[0][3], cores[1][2], cores[1][3]], axis=0)
    rest = jnp.concatenate(
        [cores[core][4, 2:4, 32 * i : 32 * i + 32] for core in range(2) for i in range(4)], axis=0
    )
    kept = [packed[:, :64], packed[:, 64:112], rest, packed[:, 112:]]
    upper = []
    for block in range(BLOCKS):
        pieces = [0.5 * kept[block][:, :COLS]]
        if block:
            pieces.insert(0, jnp.zeros((COLS, block * COLS), F32))
        if block < BLOCKS - 1:
            pieces.append(kept[block][:, COLS:])
        upper.append(jnp.concatenate(pieces, axis=1))
    half = jnp.concatenate(upper, axis=0)
    carried = lax.dot_general(proj, half, NN, precision=HIGHEST, preferred_element_type=F32) - proj
    cross = lax.dot_general(carried, proj, NT, precision=HIGHEST, preferred_element_type=F32)
    cross_t = lax.dot_general(proj, carried, NT, precision=HIGHEST, preferred_element_type=F32)
    gram = image_gram + (cross + cross_t)
    row = lax.broadcasted_iota(jnp.int32, (COLS, COLS), 0)
    col = lax.broadcasted_iota(jnp.int32, (COLS, COLS), 1)
    eye = jnp.where(row == col, 1.0, 0.0).astype(F32)
    work = jnp.concatenate(
        [gram, -proj, eye, jnp.zeros((COLS, 128 - FULL - COLS), F32)], axis=1
    )
    wide_row = lax.broadcasted_iota(jnp.int32, (COLS, 128), 0)
    columns = [jnp.broadcast_to(gram[:, k : k + 1], (COLS, 128)) for k in range(COLS)]
    scale = jnp.zeros((COLS, 128), F32)
    for step in range(COLS):
        pivot = jnp.broadcast_to(columns[step][step : step + 1], (COLS, 128))
        factor = jnp.where(wide_row > step, columns[step] * (1.0 / pivot), 0.0)
        for k in range(step + 1, COLS):
            columns[k] = columns[k] - factor * columns[k][step : step + 1]
        work = work - factor * work[step : step + 1]
        scale = jnp.where(wide_row == step, lax.rsqrt(pivot), scale)
    work = work * scale
    hess_ref[...] = proj.T
    triangle_ref[...] = jnp.where(row <= col, work[:, :COLS], 0.0)
    factors = split(work[:, COLS : COLS + FULL])
    stacked = []
    for part in range(PARTS):
        pieces = []
        for piece in (factors[part][:, :ROWS], factors[part][:, ROWS:]):
            for other in range(PARTS):
                pieces.append(piece if other < PARTS - part else jnp.zeros_like(piece))
        stacked.append(jnp.concatenate(pieces, axis=1))
    factor = jnp.concatenate(stacked, axis=0)
    for tile in range(PLACES // 8):
        lanes = slice(tile * 1024, (tile + 1) * 1024)
        product = lax.dot_general(factor, parts_ref[:, lanes], NN, preferred_element_type=F32)
        value = product[:COLS] + (product[COLS : 2 * COLS] + product[2 * COLS :])
        for line in range(8):
            next_ref[pl.ds(tile * 8 + line, COLS, stride=PLACES), :] = value[
                :, line * 128 : (line + 1) * 128
            ]


def finish(sums, parts):
    return pl.pallas_call(
        finish_kernel,
        out_shape=(
            jax.ShapeDtypeStruct((ROWS, COLS), F32),
            jax.ShapeDtypeStruct((COLS, COLS), F32),
            jax.ShapeDtypeStruct((COLS * PLACES, 128), F32),
        ),
        in_specs=[VMEM, VMEM],
        out_specs=(VMEM, VMEM, VMEM),
        compiler_params=params(20),
        name="finish",
    )(sums, parts)


def exchanged(copies, axes):
    return lax.all_to_all(copies, axes, 0, 0)


def per_device(basis, num, den):
    slabs = size_of(SPACE)
    groups = size_of(TM)
    pairs = [(i, i ^ 1) for i in range(slabs)]
    others = [(i, ((i + 1) ^ 1) - 1) for i in range(1, slabs - 1)]
    first = pairs + [(i + slabs, j + slabs) for i, j in others]
    second = others + [(i + slabs, j + slabs) for i, j in pairs]
    later = [(i, i + 1) for i in range(groups - 1)]
    flat = basis.reshape(ROWS, PLACES, 1, 128)
    near, far, late, sizes = edges(num, den, basis)
    near = lax.ppermute(near, ("core",) + SPACE, first).reshape(-1, 128)
    far = lax.ppermute(far, ("core",) + SPACE, second).reshape(-1, 128)
    late = lax.ppermute(late, TM, later).reshape(-1, 128)
    parts, field, keep, give = basis_products(flat)
    got = lax.ppermute(give, "core", [(0, 1), (1, 0)])
    inside = inner(sizes, field, late)
    parts, copies = image_products(sizes, inside, near, far, keep, got, parts)
    sums = exchanged(regroup(exchanged(copies, SPACE)), TM)
    hess, triangle, following = finish(sums, parts)
    return (
        hess.reshape(BLOCKS, COLS, COLS),
        triangle,
        following.reshape(COLS, STEPS, PLANES, LINES, 128),
    )


def solution(mesh):
    fine = Mesh(mesh.devices.reshape(8, 2, 4, 8), ("y", "core", "x", "z"))
    placed = (P(None, None, TM, SPACE, None, None), P(TM), P(TM))
    return jax.shard_map(
        per_device,
        mesh=fine,
        in_specs=placed,
        out_specs=(P(), P(), P(None, TM, SPACE, None, None)),
        check_vma=False,
    )
```

```python
import jax
import jax.numpy as jnp
from jax import lax
from jax.experimental import pallas as pl
from jax.experimental.pallas import tpu as pltpu
from jax.sharding import Mesh, PartitionSpec as P

TM = ("y", "core")
SPACE = ("x", "z")
GROUPS = 16
SLABS = 32
COLS = 16
BLOCKS = 4
ROWS = BLOCKS * COLS
FULL = ROWS + COLS
STEPS = 4
PLANES = 2
LINES = 8
PLACES = STEPS * PLANES * LINES
CELLS = PLACES * 128
SIDE = 2 * PLANES * LINES
SPARE = 2
TOTAL = 64 * 64 * 8 * 128
PARTS = 3
HIGHEST = lax.Precision.HIGHEST
F32 = jnp.float32
BF16 = jnp.bfloat16
NT = (((1,), (1,)), ((), ()))
NN = (((1,), (0,)), ((), ()))
VMEM = pl.BlockSpec(memory_space=pltpu.VMEM)
HBM = pl.BlockSpec(memory_space=pltpu.HBM)


def params(megabytes):
    return pltpu.CompilerParams(vmem_limit_bytes=megabytes * 1024 * 1024)


def in_hbm(array):
    return pltpu.with_memory_space_constraint(array, pltpu.HBM)


def size_of(axes):
    count = 1
    for axis in axes:
        count *= lax.axis_size(axis)
    return count


def place_of(step, plane, line):
    return (step * PLANES + plane) * LINES + line


def step_weights(size, before):
    ratio = size / before
    one = 1.0 + ratio
    return (1.0 + 2.0 * ratio) / one, one, ratio * ratio / one


def split(value):
    first = value.astype(BF16)
    rest = value - first.astype(F32)
    second = rest.astype(BF16)
    third = (rest - second.astype(F32)).astype(BF16)
    return first, second, third


def edges_kernel(
    num_hbm, den_hbm, basis_hbm, first_ref, second_ref, late_ref, sizes_ref, num_ref, den_ref, sems
):
    last = BLOCKS - 1
    own = pl.ds(0, COLS)
    flip = (lax.axis_index("z") + lax.axis_index("core")) % 2
    counts = [
        pltpu.make_async_copy(num_hbm, num_ref, sems.at[3]),
        pltpu.make_async_copy(den_hbm, den_ref, sems.at[4]),
    ]
    copies = [
        pltpu.make_async_copy(basis_hbm.at[last, :, :, 1 - flip], first_ref.at[own], sems.at[0]),
        pltpu.make_async_copy(basis_hbm.at[last, :, :, flip], second_ref.at[own], sems.at[1]),
        pltpu.make_async_copy(
            basis_hbm.at[last, :, pl.ds(STEPS - 2, 2)], late_ref.at[pl.ds(0, COLS)], sems.at[2]
        ),
    ]
    for copy in copies + counts:
        copy.start()
    for copy in counts:
        copy.wait()
    for step in range(STEPS):
        top = jnp.full((COLS, 128), num_ref[step]).astype(F32)
        bottom = jnp.full((COLS, 128), den_ref[step]).astype(F32)
        sizes_ref[step] = top / bottom
    for step in range(2):
        for plane in range(PLANES):
            late_ref[COLS, step, plane] = sizes_ref[STEPS - 1, :LINES]
    for copy in copies:
        copy.wait()


def edges(num, den, basis):
    face = jax.ShapeDtypeStruct((COLS + SPARE, STEPS, LINES, 128), F32)
    return pl.pallas_call(
        edges_kernel,
        out_shape=(
            face,
            face,
            jax.ShapeDtypeStruct((COLS + 1, 2, PLANES, LINES, 128), F32),
            jax.ShapeDtypeStruct((STEPS, COLS, 128), F32),
        ),
        in_specs=[HBM, HBM, HBM],
        out_specs=(VMEM, VMEM, VMEM, VMEM),
        scratch_shapes=[
            pltpu.SMEM((STEPS,), jnp.int32),
            pltpu.SMEM((STEPS,), jnp.int32),
            pltpu.SemaphoreType.DMA((5,)),
        ],
        compiler_params=params(4),
        name="edges",
    )(in_hbm(num), in_hbm(den), in_hbm(basis))


def part_products(products, count, offset, width):
    total = None
    for b in range(PARTS):
        group = None
        for a in range(PARTS - b):
            piece = products[a * count : (a + 1) * count, offset + b * width : offset + (b + 1) * width]
            group = piece if group is None else group + piece
        total = group if total is None else total + group
    return total


def basis_kernel(basis_hbm, parts_ref, last_ref, keep_ref, give_ref, field_ref, sems):
    copies = [
        pltpu.make_async_copy(basis_hbm.at[:, place, 0], field_ref.at[place], sems.at[place])
        for place in range(PLACES)
    ]
    for copy in copies:
        copy.start()
    for place in range(PLACES):
        copies[place].wait()
        value = field_ref[place]
        last_ref[place] = value[ROWS - COLS :]
        for part, piece in enumerate(split(value)):
            parts_ref[part * ROWS : (part + 1) * ROWS, place * 128 : (place + 1) * 128] = piece
    whole = parts_ref[: PARTS * ROWS]
    products = lax.dot_general(whole, whole, NT, preferred_element_type=F32)
    gram = part_products(products, ROWS, 0, ROWS)
    rows = [gram[block * COLS : (block + 1) * COLS, block * COLS :] for block in range(BLOCKS)]
    packed = jnp.concatenate([rows[0], rows[1], rows[3]], axis=1)
    halves = []
    for half in range(2):
        rest = rows[2][half * 8 : half * 8 + 8]
        rest = jnp.concatenate([rest[2 * i : 2 * i + 2] for i in range(4)], axis=1)
        halves.append((packed[half * 8 : half * 8 + 8], rest))
    own = lax.axis_index("core")
    first = jnp.full((8, 128), own) == 0
    for target, flip in ((keep_ref, False), (give_ref, True)):
        one, two = (halves[1], halves[0]) if flip else (halves[0], halves[1])
        target[0:8] = jnp.where(first, one[0], two[0])
        target[8:10] = jnp.where(first[:2], one[1], two[1])
        target[10:16] = jnp.zeros((6, 128), F32)


def basis_products(basis):
    return pl.pallas_call(
        basis_kernel,
        out_shape=(
            jax.ShapeDtypeStruct((PARTS * FULL, CELLS), BF16),
            jax.ShapeDtypeStruct((PLACES, COLS, 128), F32),
            jax.ShapeDtypeStruct((16, 128), F32),
            jax.ShapeDtypeStruct((16, 128), F32),
        ),
        in_specs=[HBM],
        out_specs=(VMEM, VMEM, VMEM, VMEM),
        scratch_shapes=[
            pltpu.VMEM((PLACES, ROWS, 128), F32),
            pltpu.SemaphoreType.DMA((PLACES,)),
        ],
        compiler_params=params(20),
        name="basis_products",
    )(in_hbm(basis))


def inner_kernel(sizes_ref, field_ref, first_ref, second_ref, inner_ref):
    sizes = [sizes_ref[step] for step in range(STEPS)]
    flip = (lax.axis_index("z") + lax.axis_index("core")) % 2
    flipped = jnp.full((COLS, 128), flip) == 1
    lane = lax.broadcasted_iota(jnp.int32, (COLS, 128), 1)

    def at(step, plane, line):
        return field_ref[place_of(step, plane, line)]

    for step in range(STEPS):
        kappa = 0.5 * sizes[step]
        if step > 0:
            now, one, two = step_weights(sizes[step], sizes[step - 1])
        for line in range(LINES):
            side = pl.ds(step * LINES + line, COLS, stride=STEPS * LINES)
            near = first_ref[side, :]
            far = second_ref[side, :]
            for plane, halo in ((0, jnp.where(flipped, near, far)), (1, jnp.where(flipped, far, near))):
                value = at(step, plane, line)
                beside = halo + at(step, PLANES - 1 - plane, line)
                if line > 0:
                    beside += at(step, plane, line - 1)
                if line < LINES - 1:
                    beside += at(step, plane, line + 1)
                beside += jnp.where(lane < 127, pltpu.roll(value, 127, 1), 0.0)
                beside += jnp.where(lane > 0, pltpu.roll(value, 1, 1), 0.0)
                result = kappa * (6.0 * value - beside)
                if step > 0:
                    result += now * value - one * at(step - 1, plane, line)
                if step > 1:
                    result += two * at(step - 2, plane, line)
                inner_ref[place_of(step, plane, line)] = result


def inner(sizes, field, near, far):
    return pl.pallas_call(
        inner_kernel,
        out_shape=jax.ShapeDtypeStruct((PLACES, COLS, 128), F32),
        in_specs=[VMEM] * 4,
        out_specs=VMEM,
        compiler_params=params(8),
        name="inner",
    )(sizes, field, near, far)


def image_kernel(
    sizes_ref, field_ref, inner_ref, late_ref, keep_ref, got_ref, parts_in_ref, parts_ref, copies_ref
):
    base = PARTS * ROWS
    first = (lax.axis_index("y") == 0) & (lax.axis_index("core") == 0)
    start = jnp.full((COLS, 128), first.astype(jnp.int32)) == 1
    before = late_ref[pl.ds(COLS * SIDE, LINES), :]
    before = jnp.where(start, sizes_ref[0], jnp.concatenate([before, before], axis=0))
    now, one, two = step_weights(sizes_ref[0], before)
    now = jnp.where(start, 1.0, now)
    one = jnp.where(start, 1.0, one)
    two = jnp.where(start, 0.0, two)
    next_two = step_weights(sizes_ref[1], sizes_ref[0])[2]

    def late(step, plane, line):
        return late_ref[pl.ds(place_of(step, plane, line), COLS, stride=SIDE), :]

    for step in range(STEPS):
        for plane in range(PLANES):
            for line in range(LINES):
                place = place_of(step, plane, line)
                result = inner_ref[place]
                if step == 0:
                    result += (
                        now * field_ref[place]
                        - one * late(1, plane, line)
                        + two * late(0, plane, line)
                    )
                if step == 1:
                    result += next_two * late(1, plane, line)
                for part, piece in enumerate(split(result)):
                    parts_ref[
                        base + part * COLS : base + (part + 1) * COLS, place * 128 : (place + 1) * 128
                    ] = piece
    own_parts = parts_ref[base:]
    products = lax.dot_general(own_parts, parts_ref[...], NT, preferred_element_type=F32)
    proj = part_products(products, COLS, 0, ROWS)
    gram = part_products(products, COLS, base, COLS)
    packed = jnp.concatenate([proj[:8], proj[8:]], axis=1)
    pieces = []
    for half in range(2):
        lines = [gram[half * 8 + row : half * 8 + row + 1] for row in range(8)]
        pieces.append(jnp.concatenate(lines, axis=1))
    chip = keep_ref[...] + got_ref[...]
    last = jnp.concatenate(pieces + [chip[8:10]], axis=0)
    for copy in range(SLABS):
        copies_ref[copy, 0] = packed[:4]
        copies_ref[copy, 1] = packed[4:]
        copies_ref[copy, 2] = chip[0:4]
        copies_ref[copy, 3] = chip[4:8]
        copies_ref[copy, 4] = last


def image_products(sizes, field, inside, late, keep, got, parts):
    return pl.pallas_call(
        image_kernel,
        out_shape=(
            jax.ShapeDtypeStruct((PARTS * FULL, CELLS), BF16),
            jax.ShapeDtypeStruct((SLABS, 5, 4, 128), F32),
        ),
        in_specs=[VMEM] * 7,
        out_specs=(VMEM, VMEM),
        input_output_aliases={6: 0},
        compiler_params=params(20),
        name="image_products",
    )(sizes, field, inside, late, keep, got, parts)


def regroup_kernel(sums_ref, copies_ref):
    total = sums_ref[0]
    for piece in range(1, SLABS):
        total = total + sums_ref[piece]
    for copy in range(GROUPS):
        copies_ref[copy] = total


def regroup(sums):
    return pl.pallas_call(
        regroup_kernel,
        out_shape=jax.ShapeDtypeStruct((GROUPS, 5, 4, 128), F32),
        in_specs=[VMEM],
        out_specs=VMEM,
        compiler_params=params(4),
        name="regroup",
    )(sums)


def finish_kernel(sums_ref, parts_ref, hess_ref, triangle_ref, next_ref):
    cores = []
    for core in range(2):
        total = sums_ref[core]
        for piece in range(core + 2, GROUPS, 2):
            total = total + sums_ref[piece]
        cores.append(total * (1.0 / TOTAL))
    sums = cores[0] + cores[1]
    proj = jnp.concatenate(
        [sums[0, :, :ROWS], sums[1, :, :ROWS], sums[0, :, ROWS:], sums[1, :, ROWS:]], axis=0
    )
    image_gram = jnp.concatenate(
        [
            sums[4, half : half + 1, line * COLS : (line + 1) * COLS]
            for half in range(2)
            for line in range(8)
        ],
        axis=0,
    )
    packed = jnp.concatenate([cores[0][2], cores[0][3], cores[1][2], cores[1][3]], axis=0)
    rest = jnp.concatenate(
        [cores[core][4, 2:4, 32 * i : 32 * i + 32] for core in range(2) for i in range(4)], axis=0
    )
    kept = [packed[:, :64], packed[:, 64:112], rest, packed[:, 112:]]
    upper = []
    for block in range(BLOCKS):
        pieces = [0.5 * kept[block][:, :COLS]]
        if block:
            pieces.insert(0, jnp.zeros((COLS, block * COLS), F32))
        if block < BLOCKS - 1:
            pieces.append(kept[block][:, COLS:])
        upper.append(jnp.concatenate(pieces, axis=1))
    half = jnp.concatenate(upper, axis=0)
    carried = lax.dot_general(proj, half, NN, precision=HIGHEST, preferred_element_type=F32) - proj
    cross = lax.dot_general(carried, proj, NT, precision=HIGHEST, preferred_element_type=F32)
    cross_t = lax.dot_general(proj, carried, NT, precision=HIGHEST, preferred_element_type=F32)
    gram = image_gram + (cross + cross_t)
    row = lax.broadcasted_iota(jnp.int32, (COLS, COLS), 0)
    col = lax.broadcasted_iota(jnp.int32, (COLS, COLS), 1)
    eye = jnp.where(row == col, 1.0, 0.0).astype(F32)
    work = jnp.concatenate(
        [gram, -proj, eye, jnp.zeros((COLS, 128 - FULL - COLS), F32)], axis=1
    )
    wide_row = lax.broadcasted_iota(jnp.int32, (COLS, 128), 0)
    columns = [jnp.broadcast_to(gram[:, k : k + 1], (COLS, 128)) for k in range(COLS)]
    scale = jnp.zeros((COLS, 128), F32)
    for step in range(COLS):
        pivot = jnp.broadcast_to(columns[step][step : step + 1], (COLS, 128))
        factor = jnp.where(wide_row > step, columns[step] * (1.0 / pivot), 0.0)
        for k in range(step + 1, COLS):
            columns[k] = columns[k] - factor * columns[k][step : step + 1]
        work = work - factor * work[step : step + 1]
        scale = jnp.where(wide_row == step, lax.rsqrt(pivot), scale)
    work = work * scale
    hess_ref[...] = proj.T
    triangle_ref[...] = jnp.where(row <= col, work[:, :COLS], 0.0)
    factors = split(work[:, COLS : COLS + FULL])
    stacked = []
    for part in range(PARTS):
        pieces = []
        for piece in (factors[part][:, :ROWS], factors[part][:, ROWS:]):
            for other in range(PARTS):
                pieces.append(piece if other < PARTS - part else jnp.zeros_like(piece))
        stacked.append(jnp.concatenate(pieces, axis=1))
    factor = jnp.concatenate(stacked, axis=0)
    for tile in range(PLACES // 8):
        lanes = slice(tile * 1024, (tile + 1) * 1024)
        product = lax.dot_general(factor, parts_ref[:, lanes], NN, preferred_element_type=F32)
        value = product[:COLS] + (product[COLS : 2 * COLS] + product[2 * COLS :])
        for line in range(8):
            next_ref[pl.ds(tile * 8 + line, COLS, stride=PLACES), :] = value[
                :, line * 128 : (line + 1) * 128
            ]


def finish(sums, parts):
    return pl.pallas_call(
        finish_kernel,
        out_shape=(
            jax.ShapeDtypeStruct((ROWS, COLS), F32),
            jax.ShapeDtypeStruct((COLS, COLS), F32),
            jax.ShapeDtypeStruct((COLS * PLACES, 128), F32),
        ),
        in_specs=[VMEM, VMEM],
        out_specs=(VMEM, VMEM, VMEM),
        compiler_params=params(20),
        name="finish",
    )(sums, parts)


def exchanged(copies, axes):
    return lax.all_to_all(copies, axes, 0, 0)


def per_device(basis, num, den):
    slabs = size_of(SPACE)
    groups = size_of(TM)
    pairs = [(i, i ^ 1) for i in range(slabs)]
    others = [(i, ((i + 1) ^ 1) - 1) for i in range(1, slabs - 1)]
    first = pairs + [(i + slabs, j + slabs) for i, j in others]
    second = others + [(i + slabs, j + slabs) for i, j in pairs]
    later = [(i, i + 1) for i in range(groups - 1)]
    flat = basis.reshape(ROWS, PLACES, 1, 128)
    near, far, late, sizes = edges(num, den, basis)
    near = lax.ppermute(near, ("core",) + SPACE, first).reshape(-1, 128)
    far = lax.ppermute(far, ("core",) + SPACE, second).reshape(-1, 128)
    late = lax.ppermute(late, TM, later).reshape(-1, 128)
    parts, field, keep, give = basis_products(flat)
    got = lax.ppermute(give, "core", [(0, 1), (1, 0)])
    inside = inner(sizes, field, near, far)
    parts, copies = image_products(sizes, field, inside, late, keep, got, parts)
    sums = exchanged(regroup(exchanged(copies, SPACE)), TM)
    hess, triangle, following = finish(sums, parts)
    return (
        hess.reshape(BLOCKS, COLS, COLS),
        triangle,
        following.reshape(COLS, STEPS, PLANES, LINES, 128),
    )


def solution(mesh):
    fine = Mesh(mesh.devices.reshape(8, 2, 4, 8), ("y", "core", "x", "z"))
    placed = (P(None, None, TM, SPACE, None, None), P(TM), P(TM))
    return jax.shard_map(
        per_device,
        mesh=fine,
        in_specs=placed,
        out_specs=(P(), P(), P(None, TM, SPACE, None, None)),
        check_vma=False,
    )
```

```python
import jax
import jax.numpy as jnp
from jax import lax
from jax.experimental import pallas as pl
from jax.experimental.pallas import tpu as pltpu
from jax.sharding import Mesh, PartitionSpec as P

TM = ("y", "core")
SPACE = ("x", "z")
GROUPS = 16
SLABS = 32
COLS = 16
BLOCKS = 4
ROWS = BLOCKS * COLS
FULL = ROWS + COLS
STEPS = 4
PLANES = 2
LINES = 8
PLACES = STEPS * PLANES * LINES
CELLS = PLACES * 128
SIDE = PLANES * LINES
TOTAL = 64 * 64 * 8 * 128
PARTS = 3
HIGHEST = lax.Precision.HIGHEST
F32 = jnp.float32
BF16 = jnp.bfloat16
NT = (((1,), (1,)), ((), ()))
NN = (((1,), (0,)), ((), ()))
VMEM = pl.BlockSpec(memory_space=pltpu.VMEM)
HBM = pl.BlockSpec(memory_space=pltpu.HBM)


def params(megabytes):
    return pltpu.CompilerParams(vmem_limit_bytes=megabytes * 1024 * 1024)


def in_hbm(array):
    return pltpu.with_memory_space_constraint(array, pltpu.HBM)


def size_of(axes):
    count = 1
    for axis in axes:
        count *= lax.axis_size(axis)
    return count


def place_of(step, plane, line):
    return (step * PLANES + plane) * LINES + line


def split(value):
    first = value.astype(BF16)
    rest = value - first.astype(F32)
    second = rest.astype(BF16)
    third = (rest - second.astype(F32)).astype(BF16)
    return first, second, third


def edges_kernel(
    num_hbm, den_hbm, basis_hbm, first_ref, second_ref, late_ref, sizes_ref, num_ref, den_ref, sems
):
    last = BLOCKS - 1
    flip = (lax.axis_index("z") + lax.axis_index("core")) % 2
    counts = [
        pltpu.make_async_copy(num_hbm, num_ref, sems.at[3]),
        pltpu.make_async_copy(den_hbm, den_ref, sems.at[4]),
    ]
    copies = [
        pltpu.make_async_copy(basis_hbm.at[last, :, :, 1 - flip], first_ref, sems.at[0]),
        pltpu.make_async_copy(basis_hbm.at[last, :, :, flip], second_ref, sems.at[1]),
        pltpu.make_async_copy(
            basis_hbm.at[last, :, STEPS - 1], late_ref.at[pl.ds(0, COLS)], sems.at[2]
        ),
    ]
    for copy in copies + counts:
        copy.start()
    for copy in counts:
        copy.wait()
    for step in range(STEPS):
        top = jnp.full((COLS, 128), num_ref[step]).astype(F32)
        bottom = jnp.full((COLS, 128), den_ref[step]).astype(F32)
        sizes_ref[step] = top / bottom
    for plane in range(PLANES):
        late_ref[COLS, plane] = sizes_ref[STEPS - 1, :LINES]
    for copy in copies:
        copy.wait()


def edges(num, den, basis):
    face = jax.ShapeDtypeStruct((COLS, STEPS, LINES, 128), F32)
    return pl.pallas_call(
        edges_kernel,
        out_shape=(
            face,
            face,
            jax.ShapeDtypeStruct((COLS + 1, PLANES, LINES, 128), F32),
            jax.ShapeDtypeStruct((STEPS, COLS, 128), F32),
        ),
        in_specs=[HBM, HBM, HBM],
        out_specs=(VMEM, VMEM, VMEM, VMEM),
        scratch_shapes=[
            pltpu.SMEM((STEPS,), jnp.int32),
            pltpu.SMEM((STEPS,), jnp.int32),
            pltpu.SemaphoreType.DMA((5,)),
        ],
        compiler_params=params(4),
        name="edges",
    )(in_hbm(num), in_hbm(den), in_hbm(basis))


def part_products(products, count, offset, width):
    total = None
    for b in range(PARTS):
        group = None
        for a in range(PARTS - b):
            piece = products[a * count : (a + 1) * count, offset + b * width : offset + (b + 1) * width]
            group = piece if group is None else group + piece
        total = group if total is None else total + group
    return total


def basis_kernel(basis_hbm, parts_ref, last_ref, keep_ref, give_ref, field_ref, sems):
    copies = [
        pltpu.make_async_copy(basis_hbm.at[:, place, 0], field_ref.at[place], sems.at[place])
        for place in range(PLACES)
    ]
    for copy in copies:
        copy.start()
    for place in range(PLACES):
        copies[place].wait()
        value = field_ref[place]
        last_ref[place] = value[ROWS - COLS :]
        if place_of(STEPS - 2, 0, 0) <= place < place_of(STEPS - 1, 0, 0):
            give_ref[place - place_of(STEPS - 2, 0, 0)] = value[ROWS - COLS :]
        for part, piece in enumerate(split(value)):
            parts_ref[part * ROWS : (part + 1) * ROWS, place * 128 : (place + 1) * 128] = piece
    whole = parts_ref[: PARTS * ROWS]
    products = lax.dot_general(whole, whole, NT, preferred_element_type=F32)
    gram = part_products(products, ROWS, 0, ROWS)
    rows = [gram[block * COLS : (block + 1) * COLS, block * COLS :] for block in range(BLOCKS)]
    packed = jnp.concatenate([rows[0], rows[1], rows[3]], axis=1)
    halves = []
    for half in range(2):
        rest = rows[2][half * 8 : half * 8 + 8]
        rest = jnp.concatenate([rest[2 * i : 2 * i + 2] for i in range(4)], axis=1)
        halves.append((packed[half * 8 : half * 8 + 8], rest))
    own = lax.axis_index("core")
    first = jnp.full((8, 128), own) == 0
    for target, flip in ((keep_ref, False), (give_ref.at[SIDE], True)):
        one, two = (halves[1], halves[0]) if flip else (halves[0], halves[1])
        target[0:8] = jnp.where(first, one[0], two[0])
        target[8:10] = jnp.where(first[:2], one[1], two[1])
        target[10:COLS] = jnp.zeros((COLS - 10, 128), F32)


def basis_products(basis):
    return pl.pallas_call(
        basis_kernel,
        out_shape=(
            jax.ShapeDtypeStruct((PARTS * FULL, CELLS), BF16),
            jax.ShapeDtypeStruct((PLACES, COLS, 128), F32),
            jax.ShapeDtypeStruct((COLS, 128), F32),
            jax.ShapeDtypeStruct((SIDE + 1, COLS, 128), F32),
        ),
        in_specs=[HBM],
        out_specs=(VMEM, VMEM, VMEM, VMEM),
        scratch_shapes=[
            pltpu.VMEM((PLACES, ROWS, 128), F32),
            pltpu.SemaphoreType.DMA((PLACES,)),
        ],
        compiler_params=params(20),
        name="basis_products",
    )(in_hbm(basis))


def inner_kernel(sizes_ref, field_ref, late_ref, first_ref, second_ref, inner_ref, weight_ref):
    sizes = [sizes_ref[step] for step in range(STEPS)]
    flip = (lax.axis_index("z") + lax.axis_index("core")) % 2
    flipped = jnp.full((COLS, 128), flip) == 1
    first = (lax.axis_index("y") == 0) & (lax.axis_index("core") == 0)
    start = jnp.full((COLS, 128), first.astype(jnp.int32)) == 1
    lane = lax.broadcasted_iota(jnp.int32, (COLS, 128), 1)

    def at(step, plane, line):
        if step < 0:
            return late_ref[pl.ds(plane * LINES + line, COLS, stride=SIDE), :]
        return field_ref[place_of(step, plane, line)]

    for step in range(STEPS):
        kappa = 0.5 * sizes[step]
        if step == 0:
            before = late_ref[pl.ds(COLS * SIDE, LINES), :]
            before = jnp.where(start, sizes[0], jnp.concatenate([before, before], axis=0))
        else:
            before = sizes[step - 1]
        ratio = sizes[step] / before
        now = (1.0 + 2.0 * ratio) / (1.0 + ratio)
        one = 1.0 + ratio
        two = ratio * ratio / (1.0 + ratio)
        if step == 0:
            now = jnp.where(start, 1.0, now)
            one = jnp.where(start, 1.0, one)
            weight_ref[...] = jnp.where(start, 0.0, two)
        for line in range(LINES):
            side = pl.ds(step * LINES + line, COLS, stride=STEPS * LINES)
            near = first_ref[side, :]
            far = second_ref[side, :]
            for plane, halo in ((0, jnp.where(flipped, near, far)), (1, jnp.where(flipped, far, near))):
                value = at(step, plane, line)
                beside = halo + at(step, PLANES - 1 - plane, line)
                if line > 0:
                    beside += at(step, plane, line - 1)
                if line < LINES - 1:
                    beside += at(step, plane, line + 1)
                beside += jnp.where(lane < 127, pltpu.roll(value, 127, 1), 0.0)
                beside += jnp.where(lane > 0, pltpu.roll(value, 1, 1), 0.0)
                result = now * value - one * at(step - 1, plane, line)
                if step > 0:
                    result += two * at(step - 2, plane, line)
                result += kappa * (6.0 * value - beside)
                inner_ref[place_of(step, plane, line)] = result


def inner(sizes, field, late, near, far):
    return pl.pallas_call(
        inner_kernel,
        out_shape=(
            jax.ShapeDtypeStruct((PLACES, COLS, 128), F32),
            jax.ShapeDtypeStruct((COLS, 128), F32),
        ),
        in_specs=[VMEM] * 5,
        out_specs=(VMEM, VMEM),
        compiler_params=params(8),
        name="inner",
    )(sizes, field, late, near, far)


def image_kernel(
    weight_ref, inner_ref, keep_ref, got_ref, parts_in_ref, parts_ref, copies_ref
):
    base = PARTS * ROWS
    weight = weight_ref[...]
    for place in range(PLACES):
        result = inner_ref[place]
        if place < SIDE:
            result += weight * got_ref[place]
        for part, piece in enumerate(split(result)):
            parts_ref[
                base + part * COLS : base + (part + 1) * COLS, place * 128 : (place + 1) * 128
            ] = piece
    own_parts = parts_ref[base:]
    products = lax.dot_general(own_parts, parts_ref[...], NT, preferred_element_type=F32)
    proj = part_products(products, COLS, 0, ROWS)
    gram = part_products(products, COLS, base, COLS)
    packed = jnp.concatenate([proj[:8], proj[8:]], axis=1)
    pieces = []
    for half in range(2):
        lines = [gram[half * 8 + row : half * 8 + row + 1] for row in range(8)]
        pieces.append(jnp.concatenate(lines, axis=1))
    chip = keep_ref[...] + got_ref[SIDE]
    last = jnp.concatenate(pieces + [chip[8:10]], axis=0)
    for copy in range(SLABS):
        copies_ref[copy, 0] = packed[:4]
        copies_ref[copy, 1] = packed[4:]
        copies_ref[copy, 2] = chip[0:4]
        copies_ref[copy, 3] = chip[4:8]
        copies_ref[copy, 4] = last


def image_products(weight, inside, keep, got, parts):
    return pl.pallas_call(
        image_kernel,
        out_shape=(
            jax.ShapeDtypeStruct((PARTS * FULL, CELLS), BF16),
            jax.ShapeDtypeStruct((SLABS, 5, 4, 128), F32),
        ),
        in_specs=[VMEM] * 5,
        out_specs=(VMEM, VMEM),
        input_output_aliases={4: 0},
        compiler_params=params(20),
        name="image_products",
    )(weight, inside, keep, got, parts)


def regroup_kernel(sums_ref, copies_ref):
    total = sums_ref[0]
    for piece in range(1, SLABS):
        total = total + sums_ref[piece]
    for copy in range(GROUPS):
        copies_ref[copy] = total


def regroup(sums):
    return pl.pallas_call(
        regroup_kernel,
        out_shape=jax.ShapeDtypeStruct((GROUPS, 5, 4, 128), F32),
        in_specs=[VMEM],
        out_specs=VMEM,
        compiler_params=params(4),
        name="regroup",
    )(sums)


def finish_kernel(sums_ref, parts_ref, hess_ref, triangle_ref, next_ref):
    cores = []
    for core in range(2):
        total = sums_ref[core]
        for piece in range(core + 2, GROUPS, 2):
            total = total + sums_ref[piece]
        cores.append(total * (1.0 / TOTAL))
    sums = cores[0] + cores[1]
    proj = jnp.concatenate(
        [sums[0, :, :ROWS], sums[1, :, :ROWS], sums[0, :, ROWS:], sums[1, :, ROWS:]], axis=0
    )
    image_gram = jnp.concatenate(
        [
            sums[4, half : half + 1, line * COLS : (line + 1) * COLS]
            for half in range(2)
            for line in range(8)
        ],
        axis=0,
    )
    packed = jnp.concatenate([cores[0][2], cores[0][3], cores[1][2], cores[1][3]], axis=0)
    rest = jnp.concatenate(
        [cores[core][4, 2:4, 32 * i : 32 * i + 32] for core in range(2) for i in range(4)], axis=0
    )
    kept = [packed[:, :64], packed[:, 64:112], rest, packed[:, 112:]]
    upper = []
    for block in range(BLOCKS):
        pieces = [0.5 * kept[block][:, :COLS]]
        if block:
            pieces.insert(0, jnp.zeros((COLS, block * COLS), F32))
        if block < BLOCKS - 1:
            pieces.append(kept[block][:, COLS:])
        upper.append(jnp.concatenate(pieces, axis=1))
    half = jnp.concatenate(upper, axis=0)
    carried = lax.dot_general(proj, half, NN, precision=HIGHEST, preferred_element_type=F32) - proj
    cross = lax.dot_general(carried, proj, NT, precision=HIGHEST, preferred_element_type=F32)
    cross_t = lax.dot_general(proj, carried, NT, precision=HIGHEST, preferred_element_type=F32)
    gram = image_gram + (cross + cross_t)
    row = lax.broadcasted_iota(jnp.int32, (COLS, COLS), 0)
    col = lax.broadcasted_iota(jnp.int32, (COLS, COLS), 1)
    eye = jnp.where(row == col, 1.0, 0.0).astype(F32)
    work = jnp.concatenate(
        [gram, -proj, eye, jnp.zeros((COLS, 128 - FULL - COLS), F32)], axis=1
    )
    wide_row = lax.broadcasted_iota(jnp.int32, (COLS, 128), 0)
    columns = [jnp.broadcast_to(gram[:, k : k + 1], (COLS, 128)) for k in range(COLS)]
    scale = jnp.zeros((COLS, 128), F32)
    for step in range(COLS):
        pivot = jnp.broadcast_to(columns[step][step : step + 1], (COLS, 128))
        factor = jnp.where(wide_row > step, columns[step] * (1.0 / pivot), 0.0)
        for k in range(step + 1, COLS):
            columns[k] = columns[k] - factor * columns[k][step : step + 1]
        work = work - factor * work[step : step + 1]
        scale = jnp.where(wide_row == step, lax.rsqrt(pivot), scale)
    work = work * scale
    hess_ref[...] = proj.T
    triangle_ref[...] = jnp.where(row <= col, work[:, :COLS], 0.0)
    factors = split(work[:, COLS : COLS + FULL])
    stacked = []
    for part in range(PARTS):
        pieces = []
        for piece in (factors[part][:, :ROWS], factors[part][:, ROWS:]):
            for other in range(PARTS):
                pieces.append(piece if other < PARTS - part else jnp.zeros_like(piece))
        stacked.append(jnp.concatenate(pieces, axis=1))
    factor = jnp.concatenate(stacked, axis=0)
    for tile in range(PLACES // 8):
        lanes = slice(tile * 1024, (tile + 1) * 1024)
        product = lax.dot_general(factor, parts_ref[:, lanes], NN, preferred_element_type=F32)
        value = product[:COLS] + (product[COLS : 2 * COLS] + product[2 * COLS :])
        for line in range(8):
            next_ref[pl.ds(tile * 8 + line, COLS, stride=PLACES), :] = value[
                :, line * 128 : (line + 1) * 128
            ]


def finish(sums, parts):
    return pl.pallas_call(
        finish_kernel,
        out_shape=(
            jax.ShapeDtypeStruct((ROWS, COLS), F32),
            jax.ShapeDtypeStruct((COLS, COLS), F32),
            jax.ShapeDtypeStruct((COLS * PLACES, 128), F32),
        ),
        in_specs=[VMEM, VMEM],
        out_specs=(VMEM, VMEM, VMEM),
        compiler_params=params(20),
        name="finish",
    )(sums, parts)


def exchanged(copies, axes):
    return lax.all_to_all(copies, axes, 0, 0)


def per_device(basis, num, den):
    slabs = size_of(SPACE)
    groups = size_of(TM)
    pairs = [(i, i ^ 1) for i in range(slabs)]
    others = [(i, ((i + 1) ^ 1) - 1) for i in range(1, slabs - 1)]
    first = pairs + [(i + slabs, j + slabs) for i, j in others]
    second = others + [(i + slabs, j + slabs) for i, j in pairs]
    later = [(i, i + 1) for i in range(groups - 1)]
    flat = basis.reshape(ROWS, PLACES, 1, 128)
    near, far, late, sizes = edges(num, den, basis)
    near = lax.ppermute(near, ("core",) + SPACE, first).reshape(-1, 128)
    far = lax.ppermute(far, ("core",) + SPACE, second).reshape(-1, 128)
    late = lax.ppermute(late, TM, later).reshape(-1, 128)
    parts, field, keep, give = basis_products(flat)
    got = lax.ppermute(give, TM, later + [(groups - 1, 0)])
    inside, weight = inner(sizes, field, late, near, far)
    parts, copies = image_products(weight, inside, keep, got, parts)
    sums = exchanged(regroup(exchanged(copies, SPACE)), TM)
    hess, triangle, following = finish(sums, parts)
    return (
        hess.reshape(BLOCKS, COLS, COLS),
        triangle,
        following.reshape(COLS, STEPS, PLANES, LINES, 128),
    )


def solution(mesh):
    fine = Mesh(mesh.devices.reshape(8, 2, 4, 8), ("y", "core", "x", "z"))
    placed = (P(None, None, TM, SPACE, None, None), P(TM), P(TM))
    return jax.shard_map(
        per_device,
        mesh=fine,
        in_specs=placed,
        out_specs=(P(), P(), P(None, TM, SPACE, None, None)),
        check_vma=False,
    )
```

```python
import jax
import jax.numpy as jnp
from jax import lax
from jax.experimental import pallas as pl
from jax.experimental.pallas import tpu as pltpu
from jax.sharding import Mesh, PartitionSpec as P

TM = ("y", "core")
SPACE = ("x", "z")
GROUPS = 16
SLABS = 32
COLS = 16
BLOCKS = 4
ROWS = BLOCKS * COLS
FULL = ROWS + COLS
STEPS = 4
PLANES = 2
LINES = 8
PLACES = STEPS * PLANES * LINES
CELLS = PLACES * 128
SIDE = 2 * PLANES * LINES
SPARE = 2
TOTAL = 64 * 64 * 8 * 128
PARTS = 3
HIGHEST = lax.Precision.HIGHEST
F32 = jnp.float32
BF16 = jnp.bfloat16
NT = (((1,), (1,)), ((), ()))
NN = (((1,), (0,)), ((), ()))
VMEM = pl.BlockSpec(memory_space=pltpu.VMEM)
HBM = pl.BlockSpec(memory_space=pltpu.HBM)


def params(megabytes):
    return pltpu.CompilerParams(vmem_limit_bytes=megabytes * 1024 * 1024)


def in_hbm(array):
    return pltpu.with_memory_space_constraint(array, pltpu.HBM)


def size_of(axes):
    count = 1
    for axis in axes:
        count *= lax.axis_size(axis)
    return count


def place_of(step, plane, line):
    return (step * PLANES + plane) * LINES + line


def step_weights(size, before):
    ratio = size / before
    one = 1.0 + ratio
    return (1.0 + 2.0 * ratio) / one, one, ratio * ratio / one


def split(value):
    first = value.astype(BF16)
    rest = value - first.astype(F32)
    second = rest.astype(BF16)
    third = (rest - second.astype(F32)).astype(BF16)
    return first, second, third


def prepare_kernel(
    num_hbm, den_hbm, basis_hbm, parts_ref, last_ref, sizes_ref, first_ref, second_ref, late_ref,
    field_ref, num_ref, den_ref, sems, count_sems,
):
    counts = [
        pltpu.make_async_copy(num_hbm, num_ref, count_sems.at[0]),
        pltpu.make_async_copy(den_hbm, den_ref, count_sems.at[1]),
    ]
    copies = [
        pltpu.make_async_copy(basis_hbm.at[:, place, 0], field_ref.at[place], sems.at[place])
        for place in range(PLACES)
    ]
    for copy in counts + copies:
        copy.start()
    for copy in counts:
        copy.wait()
    for step in range(STEPS):
        top = jnp.full((COLS, 128), num_ref[step]).astype(F32)
        bottom = jnp.full((COLS, 128), den_ref[step]).astype(F32)
        sizes_ref[step] = top / bottom
    late_ref[SIDE] = sizes_ref[STEPS - 1]
    flip = (lax.axis_index("z") + lax.axis_index("core")) % 2
    flipped = jnp.full((COLS, 128), flip) == 1
    for place in range(PLACES):
        copies[place].wait()
        value = field_ref[place]
        own = value[ROWS - COLS :]
        last_ref[place] = own
        if place >= PLACES - SIDE:
            late_ref[place - (PLACES - SIDE)] = own
        step, plane, line = place // (PLANES * LINES), place // LINES % PLANES, place % LINES
        if plane == PLANES - 1:
            other = last_ref[place_of(step, 0, line)]
            first_ref[step * LINES + line] = jnp.where(flipped, other, own)
            second_ref[step * LINES + line] = jnp.where(flipped, own, other)
        for part, piece in enumerate(split(value)):
            parts_ref[part * ROWS : (part + 1) * ROWS, place * 128 : (place + 1) * 128] = piece


def prepare(num, den, basis):
    face = jax.ShapeDtypeStruct((STEPS * LINES + SPARE, COLS, 128), F32)
    return pl.pallas_call(
        prepare_kernel,
        out_shape=(
            jax.ShapeDtypeStruct((PARTS * FULL, CELLS), BF16),
            jax.ShapeDtypeStruct((PLACES, COLS, 128), F32),
            jax.ShapeDtypeStruct((STEPS, COLS, 128), F32),
            face,
            face,
            jax.ShapeDtypeStruct((SIDE + 1, COLS, 128), F32),
        ),
        in_specs=[HBM, HBM, HBM],
        out_specs=(VMEM,) * 6,
        scratch_shapes=[
            pltpu.VMEM((PLACES, ROWS, 128), F32),
            pltpu.SMEM((STEPS,), jnp.int32),
            pltpu.SMEM((STEPS,), jnp.int32),
            pltpu.SemaphoreType.DMA((PLACES,)),
            pltpu.SemaphoreType.DMA((2,)),
        ],
        compiler_params=params(20),
        name="prepare",
    )(in_hbm(num), in_hbm(den), in_hbm(basis))


def part_products(products, count, offset, width):
    total = None
    for b in range(PARTS):
        group = None
        for a in range(PARTS - b):
            piece = products[a * count : (a + 1) * count, offset + b * width : offset + (b + 1) * width]
            group = piece if group is None else group + piece
        total = group if total is None else total + group
    return total


def basis_kernel(parts_ref, keep_ref, give_ref):
    whole = parts_ref[: PARTS * ROWS]
    products = lax.dot_general(whole, whole, NT, preferred_element_type=F32)
    gram = part_products(products, ROWS, 0, ROWS)
    rows = [gram[block * COLS : (block + 1) * COLS, block * COLS :] for block in range(BLOCKS)]
    packed = jnp.concatenate([rows[0], rows[1], rows[3]], axis=1)
    halves = []
    for half in range(2):
        rest = rows[2][half * 8 : half * 8 + 8]
        rest = jnp.concatenate([rest[2 * i : 2 * i + 2] for i in range(4)], axis=1)
        halves.append((packed[half * 8 : half * 8 + 8], rest))
    own = lax.axis_index("core")
    first = jnp.full((8, 128), own) == 0
    for target, flip in ((keep_ref, False), (give_ref, True)):
        one, two = (halves[1], halves[0]) if flip else (halves[0], halves[1])
        target[0:8] = jnp.where(first, one[0], two[0])
        target[8:10] = jnp.where(first[:2], one[1], two[1])
        target[10:16] = jnp.zeros((6, 128), F32)


def basis_products(parts):
    half = jax.ShapeDtypeStruct((COLS, 128), F32)
    return pl.pallas_call(
        basis_kernel,
        out_shape=(half, half),
        in_specs=[VMEM],
        out_specs=(VMEM, VMEM),
        compiler_params=params(20),
        name="basis_products",
    )(parts)


def inner_kernel(sizes_ref, field_ref, first_ref, second_ref, inner_ref):
    sizes = [sizes_ref[step] for step in range(STEPS)]
    flip = (lax.axis_index("z") + lax.axis_index("core")) % 2
    flipped = jnp.full((COLS, 128), flip) == 1
    lane = lax.broadcasted_iota(jnp.int32, (COLS, 128), 1)

    def at(step, plane, line):
        return field_ref[place_of(step, plane, line)]

    for step in range(STEPS):
        kappa = 0.5 * sizes[step]
        if step > 0:
            now, one, two = step_weights(sizes[step], sizes[step - 1])
        for line in range(LINES):
            near = first_ref[step * LINES + line]
            far = second_ref[step * LINES + line]
            for plane, halo in ((0, jnp.where(flipped, near, far)), (1, jnp.where(flipped, far, near))):
                value = at(step, plane, line)
                beside = halo + at(step, PLANES - 1 - plane, line)
                if line > 0:
                    beside += at(step, plane, line - 1)
                if line < LINES - 1:
                    beside += at(step, plane, line + 1)
                beside += jnp.where(lane < 127, pltpu.roll(value, 127, 1), 0.0)
                beside += jnp.where(lane > 0, pltpu.roll(value, 1, 1), 0.0)
                result = kappa * (6.0 * value - beside)
                if step > 0:
                    result += now * value - one * at(step - 1, plane, line)
                if step > 1:
                    result += two * at(step - 2, plane, line)
                inner_ref[place_of(step, plane, line)] = result


def inner(sizes, field, near, far):
    return pl.pallas_call(
        inner_kernel,
        out_shape=jax.ShapeDtypeStruct((PLACES, COLS, 128), F32),
        in_specs=[VMEM] * 4,
        out_specs=VMEM,
        compiler_params=params(8),
        name="inner",
    )(sizes, field, near, far)


def image_kernel(
    sizes_ref, field_ref, inner_ref, late_ref, keep_ref, got_ref, parts_in_ref, parts_ref, copies_ref
):
    base = PARTS * ROWS
    first = (lax.axis_index("y") == 0) & (lax.axis_index("core") == 0)
    start = jnp.full((COLS, 128), first.astype(jnp.int32)) == 1
    before = jnp.where(start, sizes_ref[0], late_ref[SIDE])
    now, one, two = step_weights(sizes_ref[0], before)
    now = jnp.where(start, 1.0, now)
    one = jnp.where(start, 1.0, one)
    two = jnp.where(start, 0.0, two)
    next_two = step_weights(sizes_ref[1], sizes_ref[0])[2]

    def late(step, plane, line):
        return late_ref[place_of(step, plane, line)]

    for step in range(STEPS):
        for plane in range(PLANES):
            for line in range(LINES):
                place = place_of(step, plane, line)
                result = inner_ref[place]
                if step == 0:
                    result += (
                        now * field_ref[place]
                        - one * late(1, plane, line)
                        + two * late(0, plane, line)
                    )
                if step == 1:
                    result += next_two * late(1, plane, line)
                for part, piece in enumerate(split(result)):
                    parts_ref[
                        base + part * COLS : base + (part + 1) * COLS, place * 128 : (place + 1) * 128
                    ] = piece
    own_parts = parts_ref[base:]
    products = lax.dot_general(own_parts, parts_ref[...], NT, preferred_element_type=F32)
    proj = part_products(products, COLS, 0, ROWS)
    gram = part_products(products, COLS, base, COLS)
    packed = jnp.concatenate([proj[:8], proj[8:]], axis=1)
    pieces = []
    for half in range(2):
        lines = [gram[half * 8 + row : half * 8 + row + 1] for row in range(8)]
        pieces.append(jnp.concatenate(lines, axis=1))
    chip = keep_ref[...] + got_ref[...]
    last = jnp.concatenate(pieces + [chip[8:10]], axis=0)
    for copy in range(SLABS):
        copies_ref[copy, 0] = packed[:4]
        copies_ref[copy, 1] = packed[4:]
        copies_ref[copy, 2] = chip[0:4]
        copies_ref[copy, 3] = chip[4:8]
        copies_ref[copy, 4] = last


def image_products(sizes, field, inside, late, keep, got, parts):
    return pl.pallas_call(
        image_kernel,
        out_shape=(
            jax.ShapeDtypeStruct((PARTS * FULL, CELLS), BF16),
            jax.ShapeDtypeStruct((SLABS, 5, 4, 128), F32),
        ),
        in_specs=[VMEM] * 7,
        out_specs=(VMEM, VMEM),
        input_output_aliases={6: 0},
        compiler_params=params(20),
        name="image_products",
    )(sizes, field, inside, late, keep, got, parts)


def regroup_kernel(sums_ref, copies_ref):
    total = sums_ref[0]
    for piece in range(1, SLABS):
        total = total + sums_ref[piece]
    for copy in range(GROUPS):
        copies_ref[copy] = total


def regroup(sums):
    return pl.pallas_call(
        regroup_kernel,
        out_shape=jax.ShapeDtypeStruct((GROUPS, 5, 4, 128), F32),
        in_specs=[VMEM],
        out_specs=VMEM,
        compiler_params=params(4),
        name="regroup",
    )(sums)


def finish_kernel(sums_ref, parts_ref, hess_ref, triangle_ref, next_ref):
    cores = []
    for core in range(2):
        total = sums_ref[core]
        for piece in range(core + 2, GROUPS, 2):
            total = total + sums_ref[piece]
        cores.append(total * (1.0 / TOTAL))
    sums = cores[0] + cores[1]
    proj = jnp.concatenate(
        [sums[0, :, :ROWS], sums[1, :, :ROWS], sums[0, :, ROWS:], sums[1, :, ROWS:]], axis=0
    )
    image_gram = jnp.concatenate(
        [
            sums[4, half : half + 1, line * COLS : (line + 1) * COLS]
            for half in range(2)
            for line in range(8)
        ],
        axis=0,
    )
    packed = jnp.concatenate([cores[0][2], cores[0][3], cores[1][2], cores[1][3]], axis=0)
    rest = jnp.concatenate(
        [cores[core][4, 2:4, 32 * i : 32 * i + 32] for core in range(2) for i in range(4)], axis=0
    )
    kept = [packed[:, :64], packed[:, 64:112], rest, packed[:, 112:]]
    upper = []
    for block in range(BLOCKS):
        pieces = [0.5 * kept[block][:, :COLS]]
        if block:
            pieces.insert(0, jnp.zeros((COLS, block * COLS), F32))
        if block < BLOCKS - 1:
            pieces.append(kept[block][:, COLS:])
        upper.append(jnp.concatenate(pieces, axis=1))
    half = jnp.concatenate(upper, axis=0)
    carried = lax.dot_general(proj, half, NN, precision=HIGHEST, preferred_element_type=F32) - proj
    cross = lax.dot_general(carried, proj, NT, precision=HIGHEST, preferred_element_type=F32)
    cross_t = lax.dot_general(proj, carried, NT, precision=HIGHEST, preferred_element_type=F32)
    gram = image_gram + (cross + cross_t)
    row = lax.broadcasted_iota(jnp.int32, (COLS, COLS), 0)
    col = lax.broadcasted_iota(jnp.int32, (COLS, COLS), 1)
    eye = jnp.where(row == col, 1.0, 0.0).astype(F32)
    work = jnp.concatenate(
        [gram, -proj, eye, jnp.zeros((COLS, 128 - FULL - COLS), F32)], axis=1
    )
    wide_row = lax.broadcasted_iota(jnp.int32, (COLS, 128), 0)
    columns = [jnp.broadcast_to(gram[:, k : k + 1], (COLS, 128)) for k in range(COLS)]
    scale = jnp.zeros((COLS, 128), F32)
    for step in range(COLS):
        pivot = jnp.broadcast_to(columns[step][step : step + 1], (COLS, 128))
        factor = jnp.where(wide_row > step, columns[step] * (1.0 / pivot), 0.0)
        for k in range(step + 1, COLS):
            columns[k] = columns[k] - factor * columns[k][step : step + 1]
        work = work - factor * work[step : step + 1]
        scale = jnp.where(wide_row == step, lax.rsqrt(pivot), scale)
    work = work * scale
    hess_ref[...] = proj.T
    triangle_ref[...] = jnp.where(row <= col, work[:, :COLS], 0.0)
    factors = split(work[:, COLS : COLS + FULL])
    stacked = []
    for part in range(PARTS):
        pieces = []
        for piece in (factors[part][:, :ROWS], factors[part][:, ROWS:]):
            for other in range(PARTS):
                pieces.append(piece if other < PARTS - part else jnp.zeros_like(piece))
        stacked.append(jnp.concatenate(pieces, axis=1))
    factor = jnp.concatenate(stacked, axis=0)
    for tile in range(PLACES // 8):
        lanes = slice(tile * 1024, (tile + 1) * 1024)
        product = lax.dot_general(factor, parts_ref[:, lanes], NN, preferred_element_type=F32)
        value = product[:COLS] + (product[COLS : 2 * COLS] + product[2 * COLS :])
        for line in range(8):
            next_ref[pl.ds(tile * 8 + line, COLS, stride=PLACES), :] = value[
                :, line * 128 : (line + 1) * 128
            ]


def finish(sums, parts):
    return pl.pallas_call(
        finish_kernel,
        out_shape=(
            jax.ShapeDtypeStruct((ROWS, COLS), F32),
            jax.ShapeDtypeStruct((COLS, COLS), F32),
            jax.ShapeDtypeStruct((COLS * PLACES, 128), F32),
        ),
        in_specs=[VMEM, VMEM],
        out_specs=(VMEM, VMEM, VMEM),
        compiler_params=params(20),
        name="finish",
    )(sums, parts)


def exchanged(copies, axes):
    return lax.all_to_all(copies, axes, 0, 0)


def per_device(basis, num, den):
    slabs = size_of(SPACE)
    groups = size_of(TM)
    pairs = [(i, i ^ 1) for i in range(slabs)]
    others = [(i, ((i + 1) ^ 1) - 1) for i in range(1, slabs - 1)]
    first = pairs + [(i + slabs, j + slabs) for i, j in others]
    second = others + [(i + slabs, j + slabs) for i, j in pairs]
    later = [(i, i + 1) for i in range(groups - 1)]
    flat = basis.reshape(ROWS, PLACES, 1, 128)
    parts, field, sizes, near, far, late = prepare(num, den, flat)
    near = lax.ppermute(near, ("core",) + SPACE, first)
    far = lax.ppermute(far, ("core",) + SPACE, second)
    late = lax.ppermute(late, TM, later)
    keep, give = basis_products(parts)
    got = lax.ppermute(give, "core", [(0, 1), (1, 0)])
    inside = inner(sizes, field, near, far)
    parts, copies = image_products(sizes, field, inside, late, keep, got, parts)
    sums = exchanged(regroup(exchanged(copies, SPACE)), TM)
    hess, triangle, following = finish(sums, parts)
    return (
        hess.reshape(BLOCKS, COLS, COLS),
        triangle,
        following.reshape(COLS, STEPS, PLANES, LINES, 128),
    )


def solution(mesh):
    fine = Mesh(mesh.devices.reshape(8, 2, 4, 8), ("y", "core", "x", "z"))
    placed = (P(None, None, TM, SPACE, None, None), P(TM), P(TM))
    return jax.shard_map(
        per_device,
        mesh=fine,
        in_specs=placed,
        out_specs=(P(), P(), P(None, TM, SPACE, None, None)),
        check_vma=False,
    )
```

```python
import jax
import jax.numpy as jnp
from jax import lax
from jax.experimental import pallas as pl
from jax.experimental.pallas import tpu as pltpu
from jax.sharding import Mesh, PartitionSpec as P

TM = ("y", "core")
SPACE = ("x", "z")
GROUPS = 16
SLABS = 32
COLS = 16
BLOCKS = 4
ROWS = BLOCKS * COLS
FULL = ROWS + COLS
STEPS = 4
PLANES = 2
LINES = 8
PLACES = STEPS * PLANES * LINES
CELLS = PLACES * 128
SIDE = 2 * PLANES * LINES
TOTAL = 64 * 64 * 8 * 128
PARTS = 3
HIGHEST = lax.Precision.HIGHEST
F32 = jnp.float32
BF16 = jnp.bfloat16
NT = (((1,), (1,)), ((), ()))
NN = (((1,), (0,)), ((), ()))
VMEM = pl.BlockSpec(memory_space=pltpu.VMEM)
HBM = pl.BlockSpec(memory_space=pltpu.HBM)


def params(megabytes):
    return pltpu.CompilerParams(vmem_limit_bytes=megabytes * 1024 * 1024)


def in_hbm(array):
    return pltpu.with_memory_space_constraint(array, pltpu.HBM)


def size_of(axes):
    count = 1
    for axis in axes:
        count *= lax.axis_size(axis)
    return count


def place_of(step, plane, line):
    return (step * PLANES + plane) * LINES + line


def split(value):
    first = value.astype(BF16)
    rest = value - first.astype(F32)
    second = rest.astype(BF16)
    third = (rest - second.astype(F32)).astype(BF16)
    return first, second, third


def edges_kernel(
    num_hbm, den_hbm, basis_hbm, first_ref, second_ref, late_ref, sizes_ref, num_ref, den_ref, sems
):
    last = BLOCKS - 1
    flip = (lax.axis_index("z") + lax.axis_index("core") + 1) % 2
    counts = [
        pltpu.make_async_copy(num_hbm, num_ref, sems.at[3]),
        pltpu.make_async_copy(den_hbm, den_ref, sems.at[4]),
    ]
    copies = [
        pltpu.make_async_copy(basis_hbm.at[last, :, :, 1 - flip], first_ref, sems.at[0]),
        pltpu.make_async_copy(basis_hbm.at[last, :, :, flip], second_ref, sems.at[1]),
        pltpu.make_async_copy(
            basis_hbm.at[last, :, pl.ds(STEPS - 2, 2)], late_ref.at[pl.ds(0, COLS)], sems.at[2]
        ),
    ]
    for copy in copies + counts:
        copy.start()
    for copy in counts:
        copy.wait()
    for step in range(STEPS):
        top = jnp.full((COLS, 128), num_ref[step]).astype(F32)
        bottom = jnp.full((COLS, 128), den_ref[step]).astype(F32)
        sizes_ref[step] = top / bottom
    for step in range(2):
        for plane in range(PLANES):
            late_ref[COLS, step, plane] = sizes_ref[STEPS - 1, :LINES]
    for copy in copies:
        copy.wait()


def edges(num, den, basis):
    face = jax.ShapeDtypeStruct((COLS, STEPS, LINES, 128), F32)
    return pl.pallas_call(
        edges_kernel,
        out_shape=(
            face,
            face,
            jax.ShapeDtypeStruct((COLS + 1, 2, PLANES, LINES, 128), F32),
            jax.ShapeDtypeStruct((STEPS, COLS, 128), F32),
        ),
        in_specs=[HBM, HBM, HBM],
        out_specs=(VMEM, VMEM, VMEM, VMEM),
        scratch_shapes=[
            pltpu.SMEM((STEPS,), jnp.int32),
            pltpu.SMEM((STEPS,), jnp.int32),
            pltpu.SemaphoreType.DMA((5,)),
        ],
        compiler_params=params(4),
        name="edges",
    )(in_hbm(num), in_hbm(den), in_hbm(basis))


def part_products(products, count, offset, width):
    total = None
    for b in range(PARTS):
        group = None
        for a in range(PARTS - b):
            piece = products[a * count : (a + 1) * count, offset + b * width : offset + (b + 1) * width]
            group = piece if group is None else group + piece
        total = group if total is None else total + group
    return total


def basis_kernel(basis_hbm, parts_ref, last_ref, keep_ref, give_ref, field_ref, sems):
    copies = [
        pltpu.make_async_copy(basis_hbm.at[:, place, 0], field_ref.at[place], sems.at[place])
        for place in range(PLACES)
    ]
    for copy in copies:
        copy.start()
    for place in range(PLACES):
        copies[place].wait()
        value = field_ref[place]
        last_ref[place] = value[ROWS - COLS :]
        for part, piece in enumerate(split(value)):
            parts_ref[part * ROWS : (part + 1) * ROWS, place * 128 : (place + 1) * 128] = piece
    whole = parts_ref[: PARTS * ROWS]
    products = lax.dot_general(whole, whole, NT, preferred_element_type=F32)
    gram = part_products(products, ROWS, 0, ROWS)
    row = lax.broadcasted_iota(jnp.int32, (COLS, COLS), 0)
    col = lax.broadcasted_iota(jnp.int32, (COLS, COLS), 1)
    tiles = [
        gram[block * COLS : (block + 1) * COLS, block * COLS : (block + 1) * COLS]
        for block in range(BLOCKS)
    ]
    packed = jnp.concatenate(
        [
            gram[:COLS, COLS:],
            gram[COLS : 2 * COLS, 2 * COLS :],
            gram[2 * COLS : 3 * COLS, 3 * COLS :],
            jnp.where(row <= col, tiles[0], tiles[1]),
            jnp.where(row <= col, tiles[2], tiles[3]),
        ],
        axis=1,
    )
    halves = []
    for half in range(2):
        diagonal = jnp.sum(jnp.where(row == col, tiles[2 * half + 1], 0.0), axis=0, keepdims=True)
        diagonal = jnp.concatenate([diagonal, jnp.zeros((1, 128 - COLS), F32)], axis=1)
        halves.append((packed[half * 8 : half * 8 + 8], diagonal))
    own = lax.axis_index("core")
    first = jnp.full((8, 128), own) == 0
    for target, flip in ((keep_ref, False), (give_ref, True)):
        one, two = (halves[1], halves[0]) if flip else (halves[0], halves[1])
        target[0:8] = jnp.where(first, one[0], two[0])
        target[8:9] = jnp.where(first[:1], one[1], two[1])
        target[9:16] = jnp.zeros((7, 128), F32)


def basis_products(basis):
    return pl.pallas_call(
        basis_kernel,
        out_shape=(
            jax.ShapeDtypeStruct((PARTS * FULL, CELLS), BF16),
            jax.ShapeDtypeStruct((PLACES, COLS, 128), F32),
            jax.ShapeDtypeStruct((16, 128), F32),
            jax.ShapeDtypeStruct((16, 128), F32),
        ),
        in_specs=[HBM],
        out_specs=(VMEM, VMEM, VMEM, VMEM),
        scratch_shapes=[
            pltpu.VMEM((PLACES, ROWS, 128), F32),
            pltpu.SemaphoreType.DMA((PLACES,)),
        ],
        compiler_params=params(20),
        name="basis_products",
    )(in_hbm(basis))


def inner_kernel(sizes_ref, field_ref, late_ref, inner_ref):
    sizes = [sizes_ref[step] for step in range(STEPS)]
    first = (lax.axis_index("y") == 0) & (lax.axis_index("core") == 0)
    start = jnp.full((COLS, 128), first.astype(jnp.int32)) == 1
    weights = []
    for step in range(STEPS):
        if step == 0:
            before = late_ref[pl.ds(COLS * SIDE, LINES), :]
            before = jnp.where(start, sizes[0], jnp.concatenate([before, before], axis=0))
        else:
            before = sizes[step - 1]
        ratio = sizes[step] / before
        now = (1.0 + 2.0 * ratio) / (1.0 + ratio)
        one = 1.0 + ratio
        two = ratio * ratio / (1.0 + ratio)
        if step == 0:
            now = jnp.where(start, 1.0, now)
            one = jnp.where(start, 1.0, one)
            two = jnp.where(start, 0.0, two)
        weights.append((now, one, two, 0.5 * sizes[step]))
    lane = lax.broadcasted_iota(jnp.int32, (COLS, 128), 1)

    past = [late_ref[pl.ds(place, COLS, stride=SIDE), :] for place in range(SIDE)]

    def at(step, plane, line):
        if step < 0:
            return past[place_of(step + 2, plane, line)]
        return field_ref[place_of(step, plane, line)]

    for step in range(STEPS):
        now, one, two, kappa = weights[step]
        for plane in range(PLANES):
            for line in range(LINES):
                value = at(step, plane, line)
                beside = at(step, PLANES - 1 - plane, line)
                if line > 0:
                    beside += at(step, plane, line - 1)
                if line < LINES - 1:
                    beside += at(step, plane, line + 1)
                beside += jnp.where(lane < 127, pltpu.roll(value, 127, 1), 0.0)
                beside += jnp.where(lane > 0, pltpu.roll(value, 1, 1), 0.0)
                result = (
                    now * value
                    - one * at(step - 1, plane, line)
                    + two * at(step - 2, plane, line)
                    + kappa * (6.0 * value - beside)
                )
                inner_ref[place_of(step, plane, line)] = result


def inner(sizes, field, late):
    return pl.pallas_call(
        inner_kernel,
        out_shape=jax.ShapeDtypeStruct((PLACES, COLS, 128), F32),
        in_specs=[VMEM] * 3,
        out_specs=VMEM,
        compiler_params=params(8),
        name="inner",
    )(sizes, field, late)


def image_kernel(
    sizes_ref, inner_ref, first_ref, second_ref, keep_ref, got_ref, parts_in_ref, parts_ref, copies_ref
):
    base = PARTS * ROWS
    flip = (lax.axis_index("z") + lax.axis_index("core") + 1) % 2
    flipped = jnp.full((COLS, 128), flip) == 1
    for step in range(STEPS):
        kappa = 0.5 * sizes_ref[step]
        for line in range(LINES):
            side = pl.ds(step * LINES + line, COLS, stride=STEPS * LINES)
            one = first_ref[side, :]
            two = second_ref[side, :]
            for plane, halo in ((0, jnp.where(flipped, one, two)), (1, jnp.where(flipped, two, one))):
                place = place_of(step, plane, line)
                for part, piece in enumerate(split(inner_ref[place] - kappa * halo)):
                    parts_ref[
                        base + part * COLS : base + (part + 1) * COLS, place * 128 : (place + 1) * 128
                    ] = piece
    own_parts = parts_ref[base:]
    products = lax.dot_general(own_parts, parts_ref[...], NT, preferred_element_type=F32)
    proj = part_products(products, COLS, 0, ROWS)
    gram = part_products(products, COLS, base, COLS)
    packed = jnp.concatenate([proj[:8], proj[8:]], axis=1)
    chip = keep_ref[...] + got_ref[...]
    row = lax.broadcasted_iota(jnp.int32, (COLS, COLS), 0)
    col = lax.broadcasted_iota(jnp.int32, (COLS, COLS), 1)
    diagonal = chip[8:9, :COLS]
    turned = jnp.concatenate([diagonal[:, COLS - 1 :], diagonal[:, : COLS - 1]], axis=1)
    mixed = jnp.where(row <= col, gram, jnp.where(row == COLS - 1, diagonal, turned))
    pieces = []
    for half in range(2):
        lines = [mixed[half * 8 + line : half * 8 + line + 1] for line in range(8)]
        pieces.append(jnp.concatenate(lines, axis=1))
    parcels = [packed[2 * i : 2 * i + 2] for i in range(4)]
    parcels += [chip[2 * i : 2 * i + 2] for i in range(4)]
    parcels.append(jnp.concatenate(pieces, axis=0))
    for copy in range(SLABS):
        for index, parcel in enumerate(parcels):
            copies_ref[copy, index] = parcel


def image_products(sizes, inside, one, two, keep, got, parts):
    return pl.pallas_call(
        image_kernel,
        out_shape=(
            jax.ShapeDtypeStruct((PARTS * FULL, CELLS), BF16),
            jax.ShapeDtypeStruct((SLABS, 9, 2, 128), F32),
        ),
        in_specs=[VMEM] * 7,
        out_specs=(VMEM, VMEM),
        input_output_aliases={6: 0},
        compiler_params=params(20),
        name="image_products",
    )(sizes, inside, one, two, keep, got, parts)


def regroup_kernel(sums_ref, copies_ref):
    total = sums_ref[0]
    for piece in range(1, SLABS):
        total = total + sums_ref[piece]
    for copy in range(GROUPS):
        copies_ref[copy] = total


def regroup(sums):
    return pl.pallas_call(
        regroup_kernel,
        out_shape=jax.ShapeDtypeStruct((GROUPS, 9, 2, 128), F32),
        in_specs=[VMEM],
        out_specs=VMEM,
        compiler_params=params(4),
        name="regroup",
    )(sums)


def finish_kernel(sums_ref, parts_ref, hess_ref, triangle_ref, next_ref):
    cores = []
    for core in range(2):
        total = sums_ref[core]
        for piece in range(core + 2, GROUPS, 2):
            total = total + sums_ref[piece]
        cores.append(total * (1.0 / TOTAL))
    sums = cores[0] + cores[1]
    high = jnp.concatenate([sums[i] for i in range(4)], axis=0)
    proj = jnp.concatenate([high[:, :ROWS], high[:, ROWS:]], axis=0)
    mixed = jnp.concatenate(
        [
            sums[8, half : half + 1, line * COLS : (line + 1) * COLS]
            for half in range(2)
            for line in range(8)
        ],
        axis=0,
    )
    packed = jnp.concatenate([cores[core][4 + i] for core in range(2) for i in range(4)], axis=0)
    row = lax.broadcasted_iota(jnp.int32, (COLS, COLS), 0)
    col = lax.broadcasted_iota(jnp.int32, (COLS, COLS), 1)

    def upper_half(block, diagonal):
        return jnp.where(row < col, block, 0.0) + jnp.where(row == col, 0.5 * diagonal, 0.0)

    def lower_half(block, diagonal):
        return jnp.where(row > col, block, 0.0) + jnp.where(row == col, 0.5 * diagonal, 0.0)

    diagonals = [
        jnp.concatenate(
            [cores[core][8, 1:2, 7 * COLS : 8 * COLS - 1], cores[core][8, 1:2, 6 * COLS : 6 * COLS + 1]],
            axis=1,
        )
        for core in range(2)
    ]
    pairs = [packed[:, 6 * COLS : 7 * COLS], packed[:, 7 * COLS :]]
    zero = jnp.zeros((COLS, COLS), F32)
    half = jnp.concatenate(
        [
            jnp.concatenate([upper_half(pairs[0], pairs[0]), packed[:, : 3 * COLS]], axis=1),
            jnp.concatenate(
                [zero, lower_half(pairs[0], diagonals[0]), packed[:, 3 * COLS : 5 * COLS]], axis=1
            ),
            jnp.concatenate(
                [zero, zero, upper_half(pairs[1], pairs[1]), packed[:, 5 * COLS : 6 * COLS]], axis=1
            ),
            jnp.concatenate([zero, zero, zero, lower_half(pairs[1], diagonals[1])], axis=1),
        ],
        axis=0,
    )
    carried = lax.dot_general(proj, half, NN, precision=HIGHEST, preferred_element_type=F32) - proj
    cross = lax.dot_general(carried, proj, NT, precision=HIGHEST, preferred_element_type=F32)
    share = cross + upper_half(mixed, mixed)
    gram = share + share.T
    eye = jnp.where(row == col, 1.0, 0.0).astype(F32)
    work = jnp.concatenate(
        [gram, -proj, eye, jnp.zeros((COLS, 128 - FULL - COLS), F32)], axis=1
    )
    wide_row = lax.broadcasted_iota(jnp.int32, (COLS, 128), 0)
    columns = [jnp.broadcast_to(gram[:, k : k + 1], (COLS, 128)) for k in range(COLS)]
    scale = jnp.zeros((COLS, 128), F32)
    for step in range(COLS):
        pivot = jnp.broadcast_to(columns[step][step : step + 1], (COLS, 128))
        factor = jnp.where(wide_row > step, columns[step] * (1.0 / pivot), 0.0)
        for k in range(step + 1, COLS):
            columns[k] = columns[k] - factor * columns[k][step : step + 1]
        work = work - factor * work[step : step + 1]
        scale = jnp.where(wide_row == step, lax.rsqrt(pivot), scale)
    work = work * scale
    hess_ref[...] = proj.T
    triangle_ref[...] = jnp.where(row <= col, work[:, :COLS], 0.0)
    factors = split(work[:, COLS : COLS + FULL])
    stacked = []
    for part in range(PARTS):
        pieces = []
        for piece in (factors[part][:, :ROWS], factors[part][:, ROWS:]):
            for other in range(PARTS):
                pieces.append(piece if other < PARTS - part else jnp.zeros_like(piece))
        stacked.append(jnp.concatenate(pieces, axis=1))
    factor = jnp.concatenate(stacked, axis=0)
    for tile in range(PLACES // 8):
        lanes = slice(tile * 1024, (tile + 1) * 1024)
        product = lax.dot_general(factor, parts_ref[:, lanes], NN, preferred_element_type=F32)
        value = product[:COLS] + (product[COLS : 2 * COLS] + product[2 * COLS :])
        for line in range(8):
            next_ref[pl.ds(tile * 8 + line, COLS, stride=PLACES), :] = value[
                :, line * 128 : (line + 1) * 128
            ]


def finish(sums, parts):
    return pl.pallas_call(
        finish_kernel,
        out_shape=(
            jax.ShapeDtypeStruct((ROWS, COLS), F32),
            jax.ShapeDtypeStruct((COLS, COLS), F32),
            jax.ShapeDtypeStruct((COLS * PLACES, 128), F32),
        ),
        in_specs=[VMEM, VMEM],
        out_specs=(VMEM, VMEM, VMEM),
        compiler_params=params(20),
        name="finish",
    )(sums, parts)


def exchanged(copies, axes):
    return lax.all_to_all(copies, axes, 0, 0)


def per_device(basis, num, den):
    slabs = size_of(SPACE)
    groups = size_of(TM)
    pairs = [(i, i ^ 1) for i in range(slabs)]
    others = [(i, ((i + 1) ^ 1) - 1) for i in range(1, slabs - 1)]
    first = others + [(i + slabs, j + slabs) for i, j in pairs]
    second = pairs + [(i + slabs, j + slabs) for i, j in others]
    later = [(i, i + 1) for i in range(groups - 1)]
    flat = basis.reshape(ROWS, PLACES, 1, 128)
    near, far, late, sizes = edges(num, den, basis)
    near = lax.ppermute(near, ("core",) + SPACE, first).reshape(-1, 128)
    far = lax.ppermute(far, ("core",) + SPACE, second).reshape(-1, 128)
    late = lax.ppermute(late, TM, later).reshape(-1, 128)
    parts, field, keep, give = basis_products(flat)
    got = lax.ppermute(give, "core", [(0, 1), (1, 0)])
    inside = inner(sizes, field, late)
    parts, copies = image_products(sizes, inside, near, far, keep, got, parts)
    sums = exchanged(regroup(exchanged(copies, SPACE)), TM)
    hess, triangle, following = finish(sums, parts)
    return (
        hess.reshape(BLOCKS, COLS, COLS),
        triangle,
        following.reshape(COLS, STEPS, PLANES, LINES, 128),
    )


def solution(mesh):
    fine = Mesh(mesh.devices.reshape(8, 2, 4, 8), ("y", "core", "x", "z"))
    placed = (P(None, None, TM, SPACE, None, None), P(TM), P(TM))
    return jax.shard_map(
        per_device,
        mesh=fine,
        in_specs=placed,
        out_specs=(P(), P(), P(None, TM, SPACE, None, None)),
        check_vma=False,
    )
```

```python
import jax
import jax.numpy as jnp
from jax import lax
from jax.experimental import pallas as pl
from jax.experimental.pallas import tpu as pltpu
from jax.sharding import Mesh, PartitionSpec as P

TM = ("y", "core")
SPACE = ("x", "z")
GROUPS = 16
SLABS = 32
COLS = 16
BLOCKS = 4
ROWS = BLOCKS * COLS
FULL = ROWS + COLS
STEPS = 4
PLANES = 2
LINES = 8
PLACES = STEPS * PLANES * LINES
CELLS = PLACES * 128
SIDE = 2 * PLANES * LINES
TOTAL = 64 * 64 * 8 * 128
PARTS = 3
HIGHEST = lax.Precision.HIGHEST
F32 = jnp.float32
BF16 = jnp.bfloat16
NT = (((1,), (1,)), ((), ()))
NN = (((1,), (0,)), ((), ()))
VMEM = pl.BlockSpec(memory_space=pltpu.VMEM)
HBM = pl.BlockSpec(memory_space=pltpu.HBM)


def params(megabytes):
    return pltpu.CompilerParams(vmem_limit_bytes=megabytes * 1024 * 1024)


def in_hbm(array):
    return pltpu.with_memory_space_constraint(array, pltpu.HBM)


def size_of(axes):
    count = 1
    for axis in axes:
        count *= lax.axis_size(axis)
    return count


def place_of(step, plane, line):
    return (step * PLANES + plane) * LINES + line


def split(value):
    first = value.astype(BF16)
    rest = value - first.astype(F32)
    second = rest.astype(BF16)
    third = (rest - second.astype(F32)).astype(BF16)
    return first, second, third


def edges_kernel(
    num_hbm, den_hbm, basis_hbm, first_ref, second_ref, late_ref, sizes_ref, num_ref, den_ref, sems
):
    last = BLOCKS - 1
    flip = (lax.axis_index("z") + lax.axis_index("core") + 1) % 2
    counts = [
        pltpu.make_async_copy(num_hbm, num_ref, sems.at[3]),
        pltpu.make_async_copy(den_hbm, den_ref, sems.at[4]),
    ]
    copies = [
        pltpu.make_async_copy(basis_hbm.at[last, :, :, 1 - flip], first_ref, sems.at[0]),
        pltpu.make_async_copy(basis_hbm.at[last, :, :, flip], second_ref, sems.at[1]),
        pltpu.make_async_copy(
            basis_hbm.at[last, :, pl.ds(STEPS - 2, 2)], late_ref.at[pl.ds(0, COLS)], sems.at[2]
        ),
    ]
    for copy in copies + counts:
        copy.start()
    for copy in counts:
        copy.wait()
    for step in range(STEPS):
        top = jnp.full((COLS, 128), num_ref[step]).astype(F32)
        bottom = jnp.full((COLS, 128), den_ref[step]).astype(F32)
        sizes_ref[step] = top / bottom
    for step in range(2):
        for plane in range(PLANES):
            late_ref[COLS, step, plane] = sizes_ref[STEPS - 1, :LINES]
    for copy in copies:
        copy.wait()


def edges(num, den, basis):
    face = jax.ShapeDtypeStruct((COLS, STEPS, LINES, 128), F32)
    return pl.pallas_call(
        edges_kernel,
        out_shape=(
            face,
            face,
            jax.ShapeDtypeStruct((COLS + 1, 2, PLANES, LINES, 128), F32),
            jax.ShapeDtypeStruct((STEPS, COLS, 128), F32),
        ),
        in_specs=[HBM, HBM, HBM],
        out_specs=(VMEM, VMEM, VMEM, VMEM),
        scratch_shapes=[
            pltpu.SMEM((STEPS,), jnp.int32),
            pltpu.SMEM((STEPS,), jnp.int32),
            pltpu.SemaphoreType.DMA((5,)),
        ],
        compiler_params=params(4),
        name="edges",
    )(in_hbm(num), in_hbm(den), in_hbm(basis))


def part_products(products, count, offset, width):
    total = None
    for b in range(PARTS):
        group = None
        for a in range(PARTS - b):
            piece = products[a * count : (a + 1) * count, offset + b * width : offset + (b + 1) * width]
            group = piece if group is None else group + piece
        total = group if total is None else total + group
    return total


def basis_kernel(basis_hbm, parts_ref, last_ref, keep_ref, give_ref, field_ref, sems):
    copies = [
        pltpu.make_async_copy(basis_hbm.at[:, place, 0], field_ref.at[place], sems.at[place])
        for place in range(PLACES)
    ]
    for copy in copies:
        copy.start()
    for place in range(PLACES):
        copies[place].wait()
        value = field_ref[place]
        last_ref[place] = value[ROWS - COLS :]
        for part, piece in enumerate(split(value)):
            parts_ref[part * ROWS : (part + 1) * ROWS, place * 128 : (place + 1) * 128] = piece
    whole = parts_ref[: PARTS * ROWS]
    products = lax.dot_general(whole, whole, NT, preferred_element_type=F32)
    gram = part_products(products, ROWS, 0, ROWS)
    row = lax.broadcasted_iota(jnp.int32, (COLS, COLS), 0)
    col = lax.broadcasted_iota(jnp.int32, (COLS, COLS), 1)
    tiles = [
        gram[block * COLS : (block + 1) * COLS, block * COLS : (block + 1) * COLS]
        for block in range(BLOCKS)
    ]
    packed = jnp.concatenate(
        [
            gram[:COLS, COLS:],
            gram[COLS : 2 * COLS, 2 * COLS :],
            gram[2 * COLS : 3 * COLS, 3 * COLS :],
            jnp.where(row <= col, tiles[0], tiles[1]),
            jnp.where(row <= col, tiles[2], tiles[3]),
        ],
        axis=1,
    )
    halves = []
    for half in range(2):
        diagonal = jnp.sum(jnp.where(row == col, tiles[2 * half + 1], 0.0), axis=0, keepdims=True)
        diagonal = jnp.concatenate([diagonal, jnp.zeros((1, 128 - COLS), F32)], axis=1)
        halves.append((packed[half * 8 : half * 8 + 8], diagonal))
    own = lax.axis_index("core")
    first = jnp.full((8, 128), own) == 0
    for target, flip in ((keep_ref, False), (give_ref, True)):
        one, two = (halves[1], halves[0]) if flip else (halves[0], halves[1])
        target[0:8] = jnp.where(first, one[0], two[0])
        target[8:9] = jnp.where(first[:1], one[1], two[1])
        target[9:16] = jnp.zeros((7, 128), F32)


def basis_products(basis):
    return pl.pallas_call(
        basis_kernel,
        out_shape=(
            jax.ShapeDtypeStruct((PARTS * FULL, CELLS), BF16),
            jax.ShapeDtypeStruct((PLACES, COLS, 128), F32),
            jax.ShapeDtypeStruct((16, 128), F32),
            jax.ShapeDtypeStruct((16, 128), F32),
        ),
        in_specs=[HBM],
        out_specs=(VMEM, VMEM, VMEM, VMEM),
        scratch_shapes=[
            pltpu.VMEM((PLACES, ROWS, 128), F32),
            pltpu.SemaphoreType.DMA((PLACES,)),
        ],
        compiler_params=params(20),
        name="basis_products",
    )(in_hbm(basis))


def inner_kernel(sizes_ref, field_ref, late_ref, inner_ref):
    sizes = [sizes_ref[step] for step in range(STEPS)]
    first = (lax.axis_index("y") == 0) & (lax.axis_index("core") == 0)
    start = jnp.full((COLS, 128), first.astype(jnp.int32)) == 1
    weights = []
    for step in range(STEPS):
        if step == 0:
            before = late_ref[pl.ds(COLS * SIDE, LINES), :]
            before = jnp.where(start, sizes[0], jnp.concatenate([before, before], axis=0))
        else:
            before = sizes[step - 1]
        ratio = sizes[step] / before
        now = (1.0 + 2.0 * ratio) / (1.0 + ratio)
        one = 1.0 + ratio
        two = ratio * ratio / (1.0 + ratio)
        if step == 0:
            now = jnp.where(start, 1.0, now)
            one = jnp.where(start, 1.0, one)
            two = jnp.where(start, 0.0, two)
        weights.append((now, one, two, 0.5 * sizes[step]))
    lane = lax.broadcasted_iota(jnp.int32, (COLS, 128), 1)

    past = [late_ref[pl.ds(place, COLS, stride=SIDE), :] for place in range(SIDE)]

    def at(step, plane, line):
        if step < 0:
            return past[place_of(step + 2, plane, line)]
        return field_ref[place_of(step, plane, line)]

    for step in range(STEPS):
        now, one, two, kappa = weights[step]
        for plane in range(PLANES):
            for line in range(LINES):
                value = at(step, plane, line)
                beside = at(step, PLANES - 1 - plane, line)
                if line > 0:
                    beside += at(step, plane, line - 1)
                if line < LINES - 1:
                    beside += at(step, plane, line + 1)
                beside += jnp.where(lane < 127, pltpu.roll(value, 127, 1), 0.0)
                beside += jnp.where(lane > 0, pltpu.roll(value, 1, 1), 0.0)
                result = (
                    now * value
                    - one * at(step - 1, plane, line)
                    + two * at(step - 2, plane, line)
                    + kappa * (6.0 * value - beside)
                )
                inner_ref[place_of(step, plane, line)] = result


def inner(sizes, field, late):
    return pl.pallas_call(
        inner_kernel,
        out_shape=jax.ShapeDtypeStruct((PLACES, COLS, 128), F32),
        in_specs=[VMEM] * 3,
        out_specs=VMEM,
        compiler_params=params(8),
        name="inner",
    )(sizes, field, late)


def image_kernel(
    sizes_ref, inner_ref, first_ref, second_ref, keep_ref, got_ref, parts_in_ref, parts_ref, copies_ref
):
    base = PARTS * ROWS
    flip = (lax.axis_index("z") + lax.axis_index("core") + 1) % 2
    flipped = jnp.full((COLS, 128), flip) == 1
    for step in range(STEPS):
        kappa = 0.5 * sizes_ref[step]
        for line in range(LINES):
            side = pl.ds(step * LINES + line, COLS, stride=STEPS * LINES)
            one = first_ref[side, :]
            two = second_ref[side, :]
            for plane, halo in ((0, jnp.where(flipped, one, two)), (1, jnp.where(flipped, two, one))):
                place = place_of(step, plane, line)
                for part, piece in enumerate(split(inner_ref[place] - kappa * halo)):
                    parts_ref[
                        base + part * COLS : base + (part + 1) * COLS, place * 128 : (place + 1) * 128
                    ] = piece
    own_parts = parts_ref[base:]
    products = lax.dot_general(parts_ref[...], own_parts, NT, preferred_element_type=F32)

    def pairs_of(offset, width):
        total = None
        for b in range(PARTS):
            group = None
            for a in range(PARTS - b):
                piece = products[
                    offset + b * width : offset + (b + 1) * width, a * COLS : (a + 1) * COLS
                ]
                group = piece if group is None else group + piece
            total = group if total is None else total + group
        return total

    proj = pairs_of(0, ROWS)
    gram = pairs_of(base, COLS)
    packed = jnp.concatenate([proj[8 * i : 8 * i + 8] for i in range(8)], axis=1)
    chip = keep_ref[...] + got_ref[...]
    row = lax.broadcasted_iota(jnp.int32, (COLS, COLS), 0)
    col = lax.broadcasted_iota(jnp.int32, (COLS, COLS), 1)
    diagonal = chip[8:9, :COLS]
    turned = jnp.concatenate([diagonal[:, COLS - 1 :], diagonal[:, : COLS - 1]], axis=1)
    mixed = jnp.where(row <= col, gram, jnp.where(row == COLS - 1, diagonal, turned))
    pieces = []
    for half in range(2):
        lines = [mixed[half * 8 + line : half * 8 + line + 1] for line in range(8)]
        pieces.append(jnp.concatenate(lines, axis=1))
    parcels = [packed[2 * i : 2 * i + 2] for i in range(4)]
    parcels += [chip[2 * i : 2 * i + 2] for i in range(4)]
    parcels.append(jnp.concatenate(pieces, axis=0))
    for copy in range(SLABS):
        for index, parcel in enumerate(parcels):
            copies_ref[copy, index] = parcel


def image_products(sizes, inside, one, two, keep, got, parts):
    return pl.pallas_call(
        image_kernel,
        out_shape=(
            jax.ShapeDtypeStruct((PARTS * FULL, CELLS), BF16),
            jax.ShapeDtypeStruct((SLABS, 9, 2, 128), F32),
        ),
        in_specs=[VMEM] * 7,
        out_specs=(VMEM, VMEM),
        input_output_aliases={6: 0},
        compiler_params=params(20),
        name="image_products",
    )(sizes, inside, one, two, keep, got, parts)


def regroup_kernel(sums_ref, copies_ref):
    total = sums_ref[0]
    for piece in range(1, SLABS):
        total = total + sums_ref[piece]
    for copy in range(GROUPS):
        copies_ref[copy] = total


def regroup(sums):
    return pl.pallas_call(
        regroup_kernel,
        out_shape=jax.ShapeDtypeStruct((GROUPS, 9, 2, 128), F32),
        in_specs=[VMEM],
        out_specs=VMEM,
        compiler_params=params(4),
        name="regroup",
    )(sums)


def finish_kernel(sums_ref, parts_ref, hess_ref, triangle_ref, next_ref):
    cores = []
    for core in range(2):
        total = sums_ref[core]
        for piece in range(core + 2, GROUPS, 2):
            total = total + sums_ref[piece]
        cores.append(total * (1.0 / TOTAL))
    sums = cores[0] + cores[1]
    high = jnp.concatenate([sums[i] for i in range(4)], axis=0)
    hess = jnp.concatenate([high[:, COLS * i : COLS * i + COLS] for i in range(8)], axis=0)
    proj = hess.T
    mixed = jnp.concatenate(
        [
            sums[8, half : half + 1, line * COLS : (line + 1) * COLS]
            for half in range(2)
            for line in range(8)
        ],
        axis=0,
    )
    packed = jnp.concatenate([cores[core][4 + i] for core in range(2) for i in range(4)], axis=0)
    row = lax.broadcasted_iota(jnp.int32, (COLS, COLS), 0)
    col = lax.broadcasted_iota(jnp.int32, (COLS, COLS), 1)

    def upper_half(block, diagonal):
        return jnp.where(row < col, block, 0.0) + jnp.where(row == col, 0.5 * diagonal, 0.0)

    def lower_half(block, diagonal):
        return jnp.where(row > col, block, 0.0) + jnp.where(row == col, 0.5 * diagonal, 0.0)

    diagonals = [
        jnp.concatenate(
            [cores[core][8, 1:2, 7 * COLS : 8 * COLS - 1], cores[core][8, 1:2, 6 * COLS : 6 * COLS + 1]],
            axis=1,
        )
        for core in range(2)
    ]
    pairs = [packed[:, 6 * COLS : 7 * COLS], packed[:, 7 * COLS :]]
    zero = jnp.zeros((COLS, COLS), F32)
    half = jnp.concatenate(
        [
            jnp.concatenate([upper_half(pairs[0], pairs[0]), packed[:, : 3 * COLS]], axis=1),
            jnp.concatenate(
                [zero, lower_half(pairs[0], diagonals[0]), packed[:, 3 * COLS : 5 * COLS]], axis=1
            ),
            jnp.concatenate(
                [zero, zero, upper_half(pairs[1], pairs[1]), packed[:, 5 * COLS : 6 * COLS]], axis=1
            ),
            jnp.concatenate([zero, zero, zero, lower_half(pairs[1], diagonals[1])], axis=1),
        ],
        axis=0,
    )
    carried = lax.dot_general(proj, half, NN, precision=HIGHEST, preferred_element_type=F32) - proj
    cross = lax.dot_general(carried, proj, NT, precision=HIGHEST, preferred_element_type=F32)
    share = cross + upper_half(mixed, mixed)
    gram = share + share.T
    eye = jnp.where(row == col, 1.0, 0.0).astype(F32)
    work = jnp.concatenate(
        [gram, -proj, eye, jnp.zeros((COLS, 128 - FULL - COLS), F32)], axis=1
    )
    wide_row = lax.broadcasted_iota(jnp.int32, (COLS, 128), 0)
    columns = [jnp.broadcast_to(gram[:, k : k + 1], (COLS, 128)) for k in range(COLS)]
    scale = jnp.zeros((COLS, 128), F32)
    for step in range(COLS):
        pivot = jnp.broadcast_to(columns[step][step : step + 1], (COLS, 128))
        factor = jnp.where(wide_row > step, columns[step] * (1.0 / pivot), 0.0)
        for k in range(step + 1, COLS):
            columns[k] = columns[k] - factor * columns[k][step : step + 1]
        work = work - factor * work[step : step + 1]
        scale = jnp.where(wide_row == step, lax.rsqrt(pivot), scale)
    work = work * scale
    hess_ref[...] = hess
    triangle_ref[...] = jnp.where(row <= col, work[:, :COLS], 0.0)
    factors = split(work[:, COLS : COLS + FULL])
    stacked = []
    for part in range(PARTS):
        pieces = []
        for piece in (factors[part][:, :ROWS], factors[part][:, ROWS:]):
            for other in range(PARTS):
                pieces.append(piece if other < PARTS - part else jnp.zeros_like(piece))
        stacked.append(jnp.concatenate(pieces, axis=1))
    factor = jnp.concatenate(stacked, axis=0)
    for tile in range(PLACES // 8):
        lanes = slice(tile * 1024, (tile + 1) * 1024)
        product = lax.dot_general(factor, parts_ref[:, lanes], NN, preferred_element_type=F32)
        value = product[:COLS] + (product[COLS : 2 * COLS] + product[2 * COLS :])
        for line in range(8):
            next_ref[pl.ds(tile * 8 + line, COLS, stride=PLACES), :] = value[
                :, line * 128 : (line + 1) * 128
            ]


def finish(sums, parts):
    return pl.pallas_call(
        finish_kernel,
        out_shape=(
            jax.ShapeDtypeStruct((ROWS, COLS), F32),
            jax.ShapeDtypeStruct((COLS, COLS), F32),
            jax.ShapeDtypeStruct((COLS * PLACES, 128), F32),
        ),
        in_specs=[VMEM, VMEM],
        out_specs=(VMEM, VMEM, VMEM),
        compiler_params=params(20),
        name="finish",
    )(sums, parts)


def exchanged(copies, axes):
    return lax.all_to_all(copies, axes, 0, 0)


def per_device(basis, num, den):
    slabs = size_of(SPACE)
    groups = size_of(TM)
    pairs = [(i, i ^ 1) for i in range(slabs)]
    others = [(i, ((i + 1) ^ 1) - 1) for i in range(1, slabs - 1)]
    first = others + [(i + slabs, j + slabs) for i, j in pairs]
    second = pairs + [(i + slabs, j + slabs) for i, j in others]
    later = [(i, i + 1) for i in range(groups - 1)]
    flat = basis.reshape(ROWS, PLACES, 1, 128)
    near, far, late, sizes = edges(num, den, basis)
    near = lax.ppermute(near, ("core",) + SPACE, first).reshape(-1, 128)
    far = lax.ppermute(far, ("core",) + SPACE, second).reshape(-1, 128)
    late = lax.ppermute(late, TM, later).reshape(-1, 128)
    parts, field, keep, give = basis_products(flat)
    got = lax.ppermute(give, "core", [(0, 1), (1, 0)])
    inside = inner(sizes, field, late)
    parts, copies = image_products(sizes, inside, near, far, keep, got, parts)
    sums = exchanged(regroup(exchanged(copies, SPACE)), TM)
    hess, triangle, following = finish(sums, parts)
    return (
        hess.reshape(BLOCKS, COLS, COLS),
        triangle,
        following.reshape(COLS, STEPS, PLANES, LINES, 128),
    )


def solution(mesh):
    fine = Mesh(mesh.devices.reshape(8, 2, 4, 8), ("y", "core", "x", "z"))
    placed = (P(None, None, TM, SPACE, None, None), P(TM), P(TM))
    return jax.shard_map(
        per_device,
        mesh=fine,
        in_specs=placed,
        out_specs=(P(), P(), P(None, TM, SPACE, None, None)),
        check_vma=False,
    )
```
